128 devices in a mesh: row: 16 (over y_lo, z, core), col: 8 (over x, y_hi).
Axes of the slice: x: 4, y: 4 (y_hi: 2, y_lo: 2; y = y_hi * 2 + y_lo), z: 4, core: 2. Of those that a mesh axis runs over, the one named last changes fastest.
Arguments:
- out_grad: bfloat16 [65536, 256], P(('row', 'col')), may hold values from -6 to 6
- out_bits: int32 [65536, 16], P(('row', 'col')), may hold values from 0 to 65535
- agg_saved: bfloat16 [65536, 256], P(('row', 'col')), may hold values from -6 to 6
- weight: bfloat16 [256, 256], replicated, may hold values from -0.375 to 0.375
- tiles: bfloat16 [16, 8, 512, 128, 128], P('row', 'col'), may hold values from -0.0625 to 0.0625
- tile_coords: int32 [16, 8, 512, 2], P('row', 'col'), may hold values from 0 to 63, as said below
- tile_count: int32 [16, 8], P('row', 'col'), may hold values from 64 to 512, as said below
- in_bits: int32 [65536, 16], P(('row', 'col')), may hold values from 0 to 65535
Outputs:
- weight_grad: float32 [256, 256], replicated
- prev_grad: bfloat16 [65536, 256], P(('row', 'col'))
The draws below stay inside these ranges and needn't reach their ends.
Inputs may be any that keep to these rules, and one draw needn't show every extreme that they name: `tile_coords`: within one block, all 512 slots name distinct tile positions; tile rows are below 32 and tile columns below 64. `tile_count`: slots at or beyond a block's count are ignored; some block uses all 512 slots.
All inputs are finite; a program needn't handle non-finite values.
Results may differ from the reference program's by a relative error of at most 0.0049.
Values may be sent and summed in bfloat16 or wider, within the bound.
No kernel may reach another device: no remote copies, remote signals or barrier semaphores. Data moves between devices by JAX's collectives and lax.ppermute only.
A program may use at most 128 MiB of HBM per device.

```python
import jax
import jax.numpy as jnp
from jax import lax

H = 256
TILE = 128
CH = 512
MAXT = 512
NODES = 65536
N_ROW = 16
N_COL = 8


def draw_tile_coords(key, part):
    tile_rows = N_COL * CH // TILE
    tile_cols = N_ROW * CH // TILE
    device_keys = jax.random.split(key, N_ROW * N_COL)

    def one_device(device_key):
        order = jax.random.permutation(device_key, tile_rows * tile_cols)[:MAXT]
        return jnp.stack([order // tile_cols, order % tile_cols], axis=-1)
    return jax.vmap(one_device)(device_keys).reshape(N_ROW, N_COL, MAXT, 2).astype(jnp.int32)


def draw_tile_count(key, part):
    lowest = MAXT // 8
    spread = MAXT - lowest + 1
    first_draw = jax.random.randint(jax.random.fold_in(key, 11), (N_ROW * N_COL,), 0, spread)
    second_draw = jax.random.randint(jax.random.fold_in(key, 12), (N_ROW * N_COL,), 0, spread)
    counts = lowest + first_draw * second_draw // max(spread - 1, 1)
    chosen = jax.random.randint(jax.random.fold_in(key, 13), (), 0, N_ROW * N_COL)
    positions = jnp.arange(N_ROW * N_COL, dtype=jnp.int32)
    counts = jnp.where(positions == chosen, MAXT, counts)
    return counts.reshape(N_ROW, N_COL).astype(jnp.int32)


def with_ends(array, key, least, high):
    dims = array.shape
    place = [jax.random.randint(jax.random.fold_in(key, axis), (), 0, dims[axis]) for axis in range(len(dims))]
    array = array.at[tuple(place)].set(least)
    longest = dims.index(max(dims))
    place[longest] = (place[longest] + 1) % dims[longest]
    return array.at[tuple(place)].set(high)


def shard_levels(own_key, dims, shards, least, largest):
    gain, own = 1.0, jax.random.fold_in(own_key, 6)
    for dim, shards_of in shards:
        steps = jnp.exp(jax.random.uniform(jax.random.fold_in(own, dim), (shards_of,), jnp.float32, least / len(shards), largest / len(shards)))
        gain = gain * jnp.repeat(steps, dims[dim] // shards_of).reshape([-1 if axis == dim else 1 for axis in range(len(dims))])
    return gain


def centred(key, extent, deviation, bound, shards=(), kind=jnp.bfloat16):
    gain = shard_levels(key, extent, shards, -0.22, 0.18) if shards else 1.0
    entries = jax.random.normal(key, extent, jnp.float32) * deviation * gain
    return jnp.minimum(jnp.maximum(entries, -bound), bound).astype(kind)


def setup_inputs(seed: int = 0) -> dict:
    key_list = jax.random.split(jax.random.key(seed), 9)
    out_grad = centred(key_list[0], (NODES, H), 1.0, 6.0, ((0, 128),))
    out_bits = with_ends(jax.random.randint(key_list[1], (NODES, H // 16), 0, 65536), jax.random.fold_in(key_list[1], 1), 0, 65535).astype(jnp.int32)
    agg_saved = centred(key_list[2], (NODES, H), 1.0, 6.0, ((0, 128),))
    weight = centred(key_list[3], (H, H), H ** -0.5, 0.375)
    tiles = centred(key_list[4], (N_ROW, N_COL, MAXT, TILE, TILE), (MAXT * TILE * TILE // (2 * CH)) ** -0.5, 0.0625, ((0, 16), (1, 8)))
    tile_coords = draw_tile_coords(jax.random.fold_in(key_list[8], 71), 0)
    tile_count = draw_tile_count(jax.random.fold_in(key_list[8], 71), 0)
    in_bits = with_ends(jax.random.randint(key_list[7], (NODES, H // 16), 0, 65536), jax.random.fold_in(key_list[7], 1), 0, 65535).astype(jnp.int32)
    return {"out_grad": out_grad, "out_bits": out_bits, "agg_saved": agg_saved, "weight": weight, "tiles": tiles, "tile_coords": tile_coords, "tile_count": tile_count, "in_bits": in_bits}


def unpack(packed):
    shift_list = jnp.arange(16, dtype=jnp.int32)
    bit_values = jnp.right_shift(packed[:, :, None], shift_list[None, None, :]) & 1
    return bit_values.reshape(packed.shape[0], packed.shape[1] * 16)


def block_product(block_tiles, block_coords, tile_total, row_values):
    tile_rows = row_values.reshape(-1, TILE, H)
    picked = tile_rows[block_coords[:, 0]].astype(jnp.float32)
    products = jnp.einsum('kij,kih->kjh', block_tiles.astype(jnp.float32), picked)
    alive_mask = jnp.arange(MAXT, dtype=jnp.int32) < tile_total
    products = jnp.where(alive_mask[:, None, None], products, jnp.zeros_like(products))
    col_tiles = N_ROW * CH // TILE
    sums = jnp.zeros((col_tiles, TILE, H), jnp.float32).at[block_coords[:, 1]].add(products)
    return sums.reshape(col_tiles * TILE, H)


def reference(out_grad, out_bits, agg_saved, weight, tiles, tile_coords, tile_count, in_bits):
    masked_grad = jnp.where(unpack(out_bits) == 1, out_grad, jnp.zeros_like(out_grad))
    weight_grad = lax.dot_general(agg_saved, masked_grad, (((0,), (0,)), ((), ())),
                                  preferred_element_type=jnp.float32) * (NODES ** -0.5)
    hidden_grad = lax.dot_general(masked_grad, weight, (((1,), (1,)), ((), ())),
                                  preferred_element_type=jnp.float32).astype(jnp.bfloat16)
    row_blocks = hidden_grad.reshape(N_ROW, N_COL * CH, H)

    def accumulate(running, row_index):
        def one_block(col_index):
            return block_product(tiles[row_index, col_index], tile_coords[row_index, col_index],
                                 tile_count[row_index, col_index], row_blocks[row_index])
        block_sums = lax.map(one_block, jnp.arange(N_COL, dtype=jnp.int32))
        block_sums = block_sums.reshape(N_COL, N_ROW, CH, H).transpose(1, 0, 2, 3)
        return running + block_sums, None

    running, unused = lax.scan(accumulate, jnp.zeros((N_ROW, N_COL, CH, H), jnp.float32),
                               jnp.arange(N_ROW, dtype=jnp.int32))
    node_grad = running.reshape(NODES, H)
    prev_grad = jnp.where(unpack(in_bits) == 1, node_grad, jnp.zeros_like(node_grad)).astype(jnp.bfloat16)
    return weight_grad, prev_grad
```

```python
import functools

import jax
import jax.numpy as jnp
from jax import lax
from jax.experimental import pallas as pl
from jax.experimental.pallas import tpu as pltpu
from jax.sharding import PartitionSpec as P

T = 128
N_STEP = 384
UNROLL = 16
LIMIT = 40
AHEAD = 3
ZERO_ROW = 32
bf16 = jnp.bfloat16
f32 = jnp.float32
tie = lambda *values: lax.optimization_barrier(values)
VMEM = pl.BlockSpec(memory_space=pltpu.VMEM)
SMEM = pl.BlockSpec(memory_space=pltpu.SMEM)


def call(body, outs, ins, name, limit=8, scratch=(), flops=0, touched=0):
    return pl.pallas_call(
        body,
        in_specs=ins,
        out_specs=[VMEM] * len(outs),
        out_shape=[jax.ShapeDtypeStruct(s, d) for s, d in outs],
        scratch_shapes=list(scratch),
        compiler_params=pltpu.CompilerParams(vmem_limit_bytes=limit * 2**20),
        cost_estimate=pl.CostEstimate(flops=flops, bytes_accessed=touched, transcendentals=0),
        name=name,
    )


def contract(a, b, da, db):
    return lax.dot_general(a, b, (((da,), (db,)), ((), ())), preferred_element_type=f32)


def mask_of(words):
    low = (words & 255).astype(f32)
    high = ((words >> 8) & 255).astype(f32)
    pieces = jnp.concatenate([low, high], 0).astype(bf16)
    w = lax.broadcasted_iota(jnp.int32, (32, 256), 0)
    f = lax.broadcasted_iota(jnp.int32, (32, 256), 1)
    spread = ((f >> 4) + 16 * ((f >> 3) & 1) == w).astype(f32).astype(bf16)
    byte = contract(pieces, spread, 0, 0).astype(jnp.int32)
    lane = lax.broadcasted_iota(jnp.int32, byte.shape, 1)
    return ((byte >> (lane & 7)) & 1) == 1


def prep(grad_ref, words_ref, agg_ref, weight_ref, ha_ref, hb_ref, wp_ref):
    masked = jnp.where(mask_of(words_ref[...]), grad_ref[...], jnp.zeros((), bf16))
    hidden = contract(weight_ref[...], masked, 1, 1).astype(bf16)
    for t in range(4):
        ref = ha_ref if t < 2 else hb_ref
        ref[t & 1] = hidden[:, t * T : (t + 1) * T]
    wp_ref[...] = contract(agg_ref[...], masked, 0, 0) * (1.0 / 256.0)


def in_mask(words_ref, out_ref):
    out_ref[...] = mask_of(words_ref[...]).astype(f32).astype(bf16)


def order_slots(count_ref, coords_ref, sib_ref, own_ref):
    device_row, device_col = lax.axis_index("row"), lax.axis_index("col")
    x, y_hi = device_col >> 1, device_col & 1
    y_lo, z, core = device_row >> 3, (device_row >> 1) & 3, device_row & 1
    slots = coords_ref.shape[1]
    slot = lax.broadcasted_iota(jnp.int32, (1, slots), 1)
    i, j = coords_ref[0:1, :], coords_ref[1:2, :]
    t, src = i & 3, i >> 2
    dx, dyh = ((src >> 1) - x) & 3, (src & 1) ^ y_hi
    row = jnp.where(t < 2, dx * 4 + dyh * 2 + t, 16 + dyh * 8 + dx * 2 + (t & 1))
    u, q = j & 3, j >> 2
    dc, dz, dy = (q & 1) ^ core ^ 1, ((q >> 1) - z) & 3, (q >> 3) ^ y_lo
    key = dc * 32 + jnp.where(u < 2, (dy * 4 + dz) * 2 + u, 16 + (dz * 2 + dy) * 2 + (u & 1))
    key = jnp.where(slot < count_ref[0], key, 64)
    word = slot | (row << 9)
    both = jnp.concatenate([key, word, jnp.zeros((6, slots), jnp.int32)], 0).T
    key_c, word_c = both[:, 0:1], both[:, 1:2]
    s_id = lax.broadcasted_iota(jnp.int32, (slots, slots), 0)
    t_id = lax.broadcasted_iota(jnp.int32, (slots, slots), 1)
    rank = jnp.sum(jnp.where((key == key_c) & (t_id < s_id), 1, 0), 1, keepdims=True)
    k_id = lax.broadcasted_iota(jnp.int32, (slots, T), 1)
    held = jnp.sum(jnp.where(key_c == k_id, 1, 0), 0, keepdims=True)
    pairs = jnp.where(k_id[0:1] < 64, (held + 1) >> 1, 0)
    ahead = (k_id < key_c) & ((k_id >> 5) == (key_c >> 5))
    step = jnp.sum(jnp.where(ahead, pairs, 0), 1, keepdims=True) + (rank >> 1)
    kind = jnp.where(key_c < 64, (key_c >> 5) * 2 + (rank & 1), 4)
    p_id = lax.broadcasted_iota(jnp.int32, (slots, N_STEP), 1)
    here = step == p_id
    none = ZERO_ROW << 9
    for half, ref in ((0, sib_ref), (1, own_ref)):
        first = here & (kind == half * 2)
        second = here & (kind == half * 2 + 1)
        total = jnp.sum(jnp.where((k_id[0:1] >> 5) == half, pairs, 0), 1, keepdims=True)
        ref[0:1, :] = jnp.sum(jnp.where(first, (key_c & 31) - 32, 0), 0, keepdims=True) + 32
        ref[1:2, :] = jnp.sum(jnp.where(first, word_c - none, 0), 0, keepdims=True) + none
        ref[2:3, :] = jnp.sum(jnp.where(second, word_c - none, 0), 0, keepdims=True) + none
        ref[3:4, :] = jnp.broadcast_to(total, (1, N_STEP))
        ref[4:8, :] = jnp.zeros((4, N_STEP), jnp.int32)


def products(steps_ref, h_ref, tiles_ref, acc_ref, buf, sems):
    groups = (steps_ref[3, 0] + UNROLL - 1) // UNROLL

    def fetch(g):
        slot = lax.rem(g, AHEAD + 1)
        for u in range(UNROLL):
            for side in range(2):
                word = steps_ref[1 + side, g * UNROLL + u]
                pltpu.make_async_copy(
                    tiles_ref.at[word & 511], buf.at[slot * 2 * UNROLL + 2 * u + side], sems.at[slot]
                ).start()

    for g in range(AHEAD):
        pl.when(g < groups)(lambda g=g: fetch(g))

    def clear(k, carry):
        acc_ref[k] = jnp.zeros((256, T), f32)
        return carry

    lax.fori_loop(0, 33, clear, 0)

    def some(g, carry):
        slot = lax.rem(g, AHEAD + 1)
        part = pl.ds(pl.multiple_of(slot * 2 * UNROLL, 2 * UNROLL), 2 * UNROLL)
        pl.when(g + AHEAD < groups)(lambda: fetch(g + AHEAD))
        pltpu.make_async_copy(tiles_ref.at[pl.ds(0, 2 * UNROLL)], buf.at[part], sems.at[slot]).wait()
        results = []
        for u in range(UNROLL):
            s = g * UNROLL + u
            left = jnp.concatenate([h_ref[steps_ref[1 + side, s] >> 9] for side in range(2)], 1)
            right = jnp.concatenate([buf[slot * 2 * UNROLL + 2 * u + side] for side in range(2)], 0)
            results.append((steps_ref[0, s], jnp.dot(left, right, preferred_element_type=f32)))
        for k, result in results:
            acc_ref[k] += result
        return carry

    lax.fori_loop(0, groups, some, 0)


def for_partner(steps_ref, a0, a3, a1, a2, b0, b1, tiles_ref, out_ref, h_ref, acc_ref, buf, sems):
    h_ref[0:4], h_ref[4:8], h_ref[8:12], h_ref[12:16] = a0[...], a1[...], a2[...], a3[...]
    h_ref[16:24], h_ref[24:32] = b0[...], b1[...]
    h_ref[ZERO_ROW] = jnp.zeros((256, T), bf16)
    products(steps_ref, h_ref, tiles_ref, acc_ref, buf, sems)

    def narrow(k, carry):
        out_ref[k] = acc_ref[k].astype(bf16)
        return carry

    lax.fori_loop(0, 32, narrow, 0)


def for_self(steps_ref, h_ref, tiles_ref, acc_ref, buf, sems):
    products(steps_ref, h_ref, tiles_ref, acc_ref, buf, sems)


def join_cores(acc_ref, got_ref, a_keep, a_y, b_keep, b_z1, b_z2, b_z3):
    def add(k):
        return acc_ref[k] + got_ref[k].astype(f32)

    for k in range(8):
        a_keep[k] = add(k)
        a_y[k] = add(8 + k).astype(bf16)
    for k in range(4):
        b_keep[k] = add(16 + k)
        b_z1[k] = add(20 + k).astype(bf16)
        b_z2[k] = add(24 + k).astype(bf16)
        b_z3[k] = add(28 + k).astype(bf16)


def join_a(keep_ref, got_ref, a_keep, a_z1, a_z2, a_z3):
    for t in range(2):
        a_keep[t] = keep_ref[t] + got_ref[t].astype(f32)
        for dz, ref in ((1, a_z1), (2, a_z2), (3, a_z3)):
            ref[t] = (keep_ref[2 * dz + t] + got_ref[2 * dz + t].astype(f32)).astype(bf16)


def join_b(keep_ref, g1, g2, g3, b_keep, b_y):
    for k in range(4):
        total = keep_ref[k] + g1[k].astype(f32) + g2[k].astype(f32) + g3[k].astype(f32)
        if k < 2:
            b_keep[k] = total
        else:
            b_y[k - 2] = total.astype(bf16)


def finish(a_keep, g1, g2, g3, b_keep, gy, mask_ref, out_ref):
    for t in range(4):
        if t < 2:
            total = a_keep[t] + g1[t].astype(f32) + g2[t].astype(f32) + g3[t].astype(f32)
        else:
            total = b_keep[t - 2] + gy[t - 2].astype(f32)
        rows = slice(t * T, (t + 1) * T)
        out_ref[rows] = jnp.where(mask_ref[rows] == 1, total.T, 0.0).astype(bf16)


def shards(out_grad, out_bits, agg_saved, weight, tiles, tile_coords, tile_count, in_bits):
    def over_x(v, s):
        return lax.ppermute(v, "col", [(c, (((c >> 1) + s) & 3) * 2 + (c & 1)) for c in range(8)])

    def over_y_hi(v):
        return lax.ppermute(v, "col", [(c, c ^ 1) for c in range(8)])

    def over_z(v, s):
        return lax.ppermute(v, "row", [(r, (r & 9) | ((((r >> 1) + s) & 3) << 1)) for r in range(16)])

    def over_y_lo(v):
        return lax.ppermute(v, "row", [(r, r ^ 8) for r in range(16)])

    def over_core(v):
        return lax.ppermute(v, "row", [(r, r ^ 1) for r in range(16)])

    half = (2, 256, T)
    ha, hb, part = call(
        prep, [(half, bf16), (half, bf16), ((256, 256), f32)], [VMEM] * 4, "prep", flops=2 * 10**8
    )(out_grad, out_bits.T, agg_saved, weight)

    ha_y = over_y_hi(ha)
    hb_1, hb_2, hb_3 = over_x(hb, -1), over_x(hb, 2), over_x(hb, 1)
    pieces = lax.all_to_all(part.reshape(16, 16, 256), "row", 0, 0)

    count, coords, words, own_tiles, ha = tie(
        tile_count.reshape(1), tile_coords[0, 0].T, in_bits.T, tiles[0, 0], ha
    )
    sib_steps, own_steps = call(
        order_slots,
        [((8, N_STEP), jnp.int32)] * 2,
        [SMEM, VMEM],
        "order_slots",
        flops=10**7,
    )(count, coords)
    (mask,) = call(in_mask, [((512, 256), bf16)], [VMEM], "in_mask", flops=10**7)(words)

    ha, ha_y, hb, hb_1, hb_2, hb_3, sib_steps, own_steps, mask = tie(
        ha, ha_y, hb, hb_1, hb_2, hb_3, sib_steps, own_steps, mask
    )
    a0 = jnp.concatenate([ha, ha_y], 0)
    b0 = jnp.concatenate([hb, hb_1, hb_2, hb_3], 0)
    a3, a1, a2 = over_x(a0, 1), over_x(a0, -1), over_x(a0, 2)
    b1 = over_y_hi(b0)

    piece = jnp.sum(pieces, 0)
    pieces = lax.all_to_all(jnp.broadcast_to(piece[None], (8, 16, 256)), "col", 0, 0)
    piece = jnp.sum(pieces, 0)
    a0, a1, a2, a3, b0, b1, piece = tie(a0, a1, a2, a3, b0, b1, piece)
    fetching = [pltpu.VMEM(((AHEAD + 1) * 2 * UNROLL, T, T), bf16), pltpu.SemaphoreType.DMA((AHEAD + 1,))]
    to_partner, hidden = call(
        for_partner,
        [((32, 256, T), bf16), ((33, 256, T), bf16)],
        [SMEM] + [VMEM] * 6 + [pl.BlockSpec(memory_space=pl.ANY)],
        "for_partner",
        limit=LIMIT,
        scratch=[pltpu.VMEM((33, 256, T), f32)] + fetching,
        flops=4 * 10**9,
        touched=2**23,
    )(sib_steps, a0, a3, a1, a2, b0, b1, own_tiles)
    from_partner = over_core(to_partner)
    (acc,) = call(
        for_self,
        [((33, 256, T), f32)],
        [SMEM, VMEM, pl.BlockSpec(memory_space=pl.ANY)],
        "for_self",
        limit=LIMIT,
        scratch=fetching,
        flops=4 * 10**9,
        touched=2**23,
    )(own_steps, hidden, own_tiles)
    quad = (4, 256, T)
    a_keep, a_y, b_keep, b_z1, b_z2, b_z3 = call(
        join_cores,
        [((8, 256, T), f32), ((8, 256, T), bf16), (quad, f32)] + [(quad, bf16)] * 3,
        [VMEM] * 2,
        "join_cores",
        flops=10**6,
    )(acc, from_partner)

    a_keep, a_y, b_keep, b_z1, b_z2, b_z3, piece = tie(a_keep, a_y, b_keep, b_z1, b_z2, b_z3, piece)
    a_got = over_y_lo(a_y)
    b_got = [over_z(b_z1, 1), over_z(b_z2, 2), over_z(b_z3, -1)]
    a_keep, a_z1, a_z2, a_z3 = call(
        join_a, [(half, f32)] + [(half, bf16)] * 3, [VMEM] * 2, "join_a", flops=10**6
    )(a_keep, a_got)
    a_got = [over_z(a_z1, 1), over_z(a_z2, 2), over_z(a_z3, -1)]
    b_keep, b_y = call(join_b, [(half, f32), (half, bf16)], [VMEM] * 4, "join_b", flops=10**6)(b_keep, *b_got)
    b_got = over_y_lo(b_y)
    pieces = lax.all_to_all(jnp.broadcast_to(piece[None], (16, 16, 256)), "row", 0, 0)
    weight_grad = pieces.reshape(256, 256)
    a_keep, b_keep, weight_grad = tie(a_keep, b_keep, weight_grad)
    (prev_grad,) = call(finish, [((512, 256), bf16)], [VMEM] * 7, "finish", flops=10**6)(
        a_keep, *a_got, b_keep, b_got, mask
    )
    return weight_grad, prev_grad


def solution(mesh):
    nodes = P(("row", "col"), None)
    return jax.shard_map(
        shards,
        mesh=mesh,
        in_specs=(nodes, nodes, nodes, P(), P("row", "col"), P("row", "col"), P("row", "col"), nodes),
        out_specs=(P(), nodes),
        check_vma=False,
    )
```

```python
import functools

import jax
import jax.numpy as jnp
from jax import lax
from jax.experimental import pallas as pl
from jax.experimental.pallas import tpu as pltpu
from jax.sharding import PartitionSpec as P

T = 128
N_STEP = 384
UNROLL = 16
LIMIT = 28
PREP_LIMIT = 61
STAGE_LIMIT = 24
ZERO_ROW = 32
bf16 = jnp.bfloat16
f32 = jnp.float32
tie = lambda *values: lax.optimization_barrier(values)
VMEM = pl.BlockSpec(memory_space=pltpu.VMEM)
ANY = pl.BlockSpec(memory_space=pl.ANY)
SMEM = pl.BlockSpec(memory_space=pltpu.SMEM)


def call(body, outs, ins, name, limit=8, scratch=(), flops=0, touched=0):
    return pl.pallas_call(
        body,
        in_specs=ins,
        out_specs=[VMEM] * len(outs),
        out_shape=[jax.ShapeDtypeStruct(s, d) for s, d in outs],
        scratch_shapes=list(scratch),
        compiler_params=pltpu.CompilerParams(vmem_limit_bytes=limit * 2**20),
        cost_estimate=pl.CostEstimate(flops=flops, bytes_accessed=touched, transcendentals=0),
        name=name,
    )


def contract(a, b, da, db):
    return lax.dot_general(a, b, (((da,), (db,)), ((), ())), preferred_element_type=f32)


def mask_of(words):
    low = (words & 255).astype(f32)
    high = ((words >> 8) & 255).astype(f32)
    pieces = jnp.concatenate([low, high], 0).astype(bf16)
    w = lax.broadcasted_iota(jnp.int32, (32, 256), 0)
    f = lax.broadcasted_iota(jnp.int32, (32, 256), 1)
    spread = ((f >> 4) + 16 * ((f >> 3) & 1) == w).astype(f32).astype(bf16)
    byte = contract(pieces, spread, 0, 0).astype(jnp.int32)
    lane = lax.broadcasted_iota(jnp.int32, byte.shape, 1)
    return ((byte >> (lane & 7)) & 1) == 1


def prep(grad_hbm, words_hbm, agg_hbm, weight_hbm, ha_ref, hb_ref, keep_ref, send_ref, grad, words, agg, weight, part, sems):
    copies = [
        pltpu.make_async_copy(src, dst, sems.at[i])
        for i, (src, dst) in enumerate(((words_hbm, words), (grad_hbm, grad), (weight_hbm, weight), (agg_hbm, agg)))
    ]
    for copy in copies:
        copy.start()
    copies[0].wait()
    mask = mask_of(words[...])
    copies[1].wait()
    masked = jnp.where(mask, grad[...], jnp.zeros((), bf16))
    copies[2].wait()
    hidden = contract(weight[...], masked, 1, 1).astype(bf16)
    for t in range(4):
        ref = ha_ref if t < 2 else hb_ref
        ref[t & 1] = hidden[:, t * T : (t + 1) * T]
    copies[3].wait()
    part[...] = contract(agg[...], masked, 0, 0) * (1.0 / 256.0)
    core = lax.axis_index("row") & 1
    keep_ref[...] = part[pl.ds(pl.multiple_of(core * T, T), T)]
    send_ref[...] = part[pl.ds(pl.multiple_of((1 - core) * T, T), T)]


def add_two(a, b, out):
    out[...] = a[...] + b[...]


def add_ring(own, left, across, right, out):
    out[...] = (own[...] + across[...]) + (left[...] + right[...])


def in_mask(words_ref, out_ref):
    out_ref[...] = mask_of(words_ref[...]).astype(f32).astype(bf16)


def order_slots(count_ref, coords_ref, sib_ref, own_ref):
    device_row, device_col = lax.axis_index("row"), lax.axis_index("col")
    x, y_hi = device_col >> 1, device_col & 1
    y_lo, z, core = device_row >> 3, (device_row >> 1) & 3, device_row & 1
    slots = coords_ref.shape[1]
    slot = lax.broadcasted_iota(jnp.int32, (1, slots), 1)
    i, j = coords_ref[0:1, :], coords_ref[1:2, :]
    t, src = i & 3, i >> 2
    dx, dyh = ((src >> 1) - x) & 3, (src & 1) ^ y_hi
    row = jnp.where(t < 2, dx * 4 + dyh * 2 + t, 16 + dyh * 8 + dx * 2 + (t & 1))
    u, q = j & 3, j >> 2
    dc, dz, dy = (q & 1) ^ core ^ 1, ((q >> 1) - z) & 3, (q >> 3) ^ y_lo
    key = dc * 32 + jnp.where(u < 2, (dy * 4 + dz) * 2 + u, 16 + (dz * 2 + dy) * 2 + (u & 1))
    key = jnp.where(slot < count_ref[0], key, 64)
    word = slot | (row << 9)
    both = jnp.concatenate([key, word, jnp.zeros((6, slots), jnp.int32)], 0).T
    key_c, word_c = both[:, 0:1], both[:, 1:2]
    s_id = lax.broadcasted_iota(jnp.int32, (slots, slots), 0)
    t_id = lax.broadcasted_iota(jnp.int32, (slots, slots), 1)
    rank = jnp.sum(jnp.where((key == key_c) & (t_id < s_id), 1, 0), 1, keepdims=True)
    k_id = lax.broadcasted_iota(jnp.int32, (slots, T), 1)
    held = jnp.sum(jnp.where(key_c == k_id, 1, 0), 0, keepdims=True)
    pairs = jnp.where(k_id[0:1] < 64, (held + 1) >> 1, 0)
    ahead = (k_id < key_c) & ((k_id >> 5) == (key_c >> 5))
    step = jnp.sum(jnp.where(ahead, pairs, 0), 1, keepdims=True) + (rank >> 1)
    kind = jnp.where(key_c < 64, (key_c >> 5) * 2 + (rank & 1), 4)
    p_id = lax.broadcasted_iota(jnp.int32, (slots, N_STEP), 1)
    here = step == p_id
    none = ZERO_ROW << 9
    for half, ref in ((0, sib_ref), (1, own_ref)):
        first = here & (kind == half * 2)
        second = here & (kind == half * 2 + 1)
        total = jnp.sum(jnp.where((k_id[0:1] >> 5) == half, pairs, 0), 1, keepdims=True)
        ref[0:1, :] = jnp.sum(jnp.where(first, (key_c & 31) - 32, 0), 0, keepdims=True) + 32
        ref[1:2, :] = jnp.sum(jnp.where(first, word_c - none, 0), 0, keepdims=True) + none
        ref[2:3, :] = jnp.sum(jnp.where(second, word_c - none, 0), 0, keepdims=True) + none
        ref[3:4, :] = jnp.broadcast_to(total, (1, N_STEP))
        ref[4:8, :] = jnp.zeros((4, N_STEP), jnp.int32)


def stage(count_ref, tiles_ref, out_ref, sems):
    chunk = tiles_ref.shape[0] // 8

    def copy(i):
        part = pl.ds(i * chunk, chunk)
        return pltpu.make_async_copy(tiles_ref.at[part], out_ref.at[part], sems.at[i])

    used = (count_ref[0] + chunk - 1) // chunk
    for i in range(8):
        pl.when(i < used)(lambda i=i: copy(i).start())
    for i in range(8):
        pl.when(i < used)(lambda i=i: copy(i).wait())


def products(steps_ref, h_ref, tiles_ref, acc_ref):
    def clear(k, carry):
        acc_ref[k] = jnp.zeros((256, T), f32)
        return carry

    lax.fori_loop(0, 33, clear, 0)

    def some(g, carry):
        results = []
        for u in range(UNROLL):
            s = g * UNROLL + u
            a, b = steps_ref[1, s], steps_ref[2, s]
            left = jnp.concatenate([h_ref[a >> 9], h_ref[b >> 9]], 1)
            right = jnp.concatenate([tiles_ref[a & 511], tiles_ref[b & 511]], 0)
            results.append((steps_ref[0, s], jnp.dot(left, right, preferred_element_type=f32)))
        for k, result in results:
            acc_ref[k] += result
        return carry

    lax.fori_loop(0, (steps_ref[3, 0] + UNROLL - 1) // UNROLL, some, 0)


def for_partner(steps_ref, a0, a3, a1, a2, b0, b1, tiles_ref, out_ref, h_ref, acc_ref):
    h_ref[0:4], h_ref[4:8], h_ref[8:12], h_ref[12:16] = a0[...], a1[...], a2[...], a3[...]
    h_ref[16:24], h_ref[24:32] = b0[...], b1[...]
    h_ref[ZERO_ROW] = jnp.zeros((256, T), bf16)
    products(steps_ref, h_ref, tiles_ref, acc_ref)

    def narrow(k, carry):
        out_ref[k] = acc_ref[k].astype(bf16)
        return carry

    lax.fori_loop(0, 32, narrow, 0)


def for_self(steps_ref, h_ref, tiles_ref, acc_ref):
    products(steps_ref, h_ref, tiles_ref, acc_ref)


def join_cores(acc_ref, got_ref, w, wl, wx, wr, a_keep, a_y, b_keep, b_z1, b_z2, b_z3, w_out):
    def add(k):
        return acc_ref[k] + got_ref[k].astype(f32)

    for k in range(8):
        a_keep[k] = add(k)
        a_y[k] = add(8 + k).astype(bf16)
    for k in range(4):
        b_keep[k] = add(16 + k)
        b_z1[k] = add(20 + k).astype(bf16)
        b_z2[k] = add(24 + k).astype(bf16)
        b_z3[k] = add(28 + k).astype(bf16)
    add_ring(w, wl, wx, wr, w_out)


def join_a(keep_ref, got_ref, w, w_got, a_keep, a_z1, a_z2, a_z3, w_out):
    for t in range(2):
        a_keep[t] = keep_ref[t] + got_ref[t].astype(f32)
        for dz, ref in ((1, a_z1), (2, a_z2), (3, a_z3)):
            ref[t] = (keep_ref[2 * dz + t] + got_ref[2 * dz + t].astype(f32)).astype(bf16)
    add_two(w, w_got, w_out)


def join_b(keep_ref, g1, g2, g3, b_keep, b_y):
    for k in range(4):
        total = keep_ref[k] + g1[k].astype(f32) + g2[k].astype(f32) + g3[k].astype(f32)
        if k < 2:
            b_keep[k] = total
        else:
            b_y[k - 2] = total.astype(bf16)


def finish(a_keep, g1, g2, g3, b_keep, gy, mask_ref, w, w_got, out_ref, weight_ref):
    core = lax.axis_index("row") & 1
    weight_ref[pl.ds(pl.multiple_of(core * T, T), T)] = w[...]
    weight_ref[pl.ds(pl.multiple_of((1 - core) * T, T), T)] = w_got[...]
    for t in range(4):
        if t < 2:
            total = a_keep[t] + g1[t].astype(f32) + g2[t].astype(f32) + g3[t].astype(f32)
        else:
            total = b_keep[t - 2] + gy[t - 2].astype(f32)
        rows = slice(t * T, (t + 1) * T)
        out_ref[rows] = jnp.where(mask_ref[rows] == 1, total.T, 0.0).astype(bf16)


def shards(out_grad, out_bits, agg_saved, weight, tiles, tile_coords, tile_count, in_bits):
    def over_x(v, s):
        return lax.ppermute(v, "col", [(c, (((c >> 1) + s) & 3) * 2 + (c & 1)) for c in range(8)])

    def over_y_hi(v):
        return lax.ppermute(v, "col", [(c, c ^ 1) for c in range(8)])

    def over_z(v, s):
        return lax.ppermute(v, "row", [(r, (r & 9) | ((((r >> 1) + s) & 3) << 1)) for r in range(16)])

    def over_y_lo(v):
        return lax.ppermute(v, "row", [(r, r ^ 8) for r in range(16)])

    def over_core(v):
        return lax.ppermute(v, "row", [(r, r ^ 1) for r in range(16)])

    half, quad, part = (2, 256, T), (4, 256, T), (T, 256)
    ha, hb, w, w_send = call(
        prep,
        [(half, bf16), (half, bf16), (part, f32), (part, f32)],
        [ANY] * 4,
        "prep",
        limit=PREP_LIMIT,
        scratch=[
            pltpu.VMEM((512, 256), bf16),
            pltpu.VMEM((16, 512), jnp.int32),
            pltpu.VMEM((512, 256), bf16),
            pltpu.VMEM((256, 256), bf16),
            pltpu.VMEM((256, 256), f32),
            pltpu.SemaphoreType.DMA((4,)),
        ],
        flops=2 * 10**8,
    )(out_grad, out_bits.T, agg_saved, weight)

    ha_y = over_y_hi(ha)
    hb_1, hb_2, hb_3 = over_x(hb, -1), over_x(hb, 2), over_x(hb, 1)
    w_got = over_core(w_send)
    count, coords, words, own_tiles, ha = tie(
        tile_count.reshape(1), tile_coords[0, 0].T, in_bits.T, tiles[0, 0], ha
    )
    sib_steps, own_steps = call(
        order_slots, [((8, N_STEP), jnp.int32)] * 2, [SMEM, VMEM], "order_slots", flops=10**7
    )(count, coords)
    (mask,) = call(in_mask, [((512, 256), bf16)], [VMEM], "in_mask", flops=10**7)(words)
    ha, ha_y, hb, hb_1, hb_2, hb_3, sib_steps, own_steps, mask, w_got = tie(
        ha, ha_y, hb, hb_1, hb_2, hb_3, sib_steps, own_steps, mask, w_got
    )

    a0 = jnp.concatenate([ha, ha_y], 0)
    b0 = jnp.concatenate([hb, hb_1, hb_2, hb_3], 0)
    a3, a1, a2 = over_x(a0, 1), over_x(a0, -1), over_x(a0, 2)
    b1 = over_y_hi(b0)
    add = functools.partial(call, outs=[(part, f32)], limit=2)
    (w,) = add(add_two, ins=[VMEM] * 2, name="w_core")(w, w_got)
    w_got = over_y_hi(w)
    count, own_tiles, w = tie(count, own_tiles, w)
    (own_tiles,) = call(
        stage,
        [(own_tiles.shape, bf16)],
        [SMEM, ANY],
        "stage",
        limit=STAGE_LIMIT,
        scratch=[pltpu.SemaphoreType.DMA((8,))],
        flops=10**9,
    )(count, own_tiles)
    (w,) = add(add_two, ins=[VMEM] * 2, name="w_y")(w, w_got)
    a0, a1, a2, a3, b0, b1, own_tiles, w = tie(a0, a1, a2, a3, b0, b1, own_tiles, w)

    w_3, w_1, w_2 = over_x(w, 1), over_x(w, -1), over_x(w, 2)
    to_partner, hidden = call(
        for_partner,
        [((32, 256, T), bf16), ((33, 256, T), bf16)],
        [SMEM] + [VMEM] * 7,
        "for_partner",
        limit=LIMIT,
        scratch=[pltpu.VMEM((33, 256, T), f32)],
        flops=4 * 10**9,
        touched=2**23,
    )(sib_steps, a0, a3, a1, a2, b0, b1, own_tiles)
    to_partner, hidden, w, w_1, w_2, w_3 = tie(to_partner, hidden, w, w_1, w_2, w_3)
    from_partner = over_core(to_partner)
    (w,) = add(add_ring, ins=[VMEM] * 4, name="w_x")(w, w_1, w_2, w_3)
    hidden, w = tie(hidden, w)
    w_3, w_1, w_2 = over_z(w, 1), over_z(w, -1), over_z(w, 2)
    (acc,) = call(
        for_self,
        [((33, 256, T), f32)],
        [SMEM, VMEM, VMEM],
        "for_self",
        limit=LIMIT,
        flops=4 * 10**9,
        touched=2**23,
    )(own_steps, hidden, own_tiles)
    a_keep, a_y, b_keep, b_z1, b_z2, b_z3, w = call(
        join_cores,
        [((8, 256, T), f32), ((8, 256, T), bf16), (quad, f32)] + [(quad, bf16)] * 3 + [(part, f32)],
        [VMEM] * 6,
        "join_cores",
        flops=10**6,
    )(acc, from_partner, w, w_1, w_2, w_3)

    a_got = over_y_lo(a_y)
    b_got = [over_z(b_z1, 1), over_z(b_z2, 2), over_z(b_z3, -1)]
    w_got = over_y_lo(w)
    a_got, w_got, b_got[0], b_got[1], b_got[2] = tie(a_got, w_got, *b_got)
    a_keep, a_z1, a_z2, a_z3, w = call(
        join_a, [(half, f32)] + [(half, bf16)] * 3 + [(part, f32)], [VMEM] * 4, "join_a", flops=10**6
    )(a_keep, a_got, w, w_got)
    a_got = [over_z(a_z1, 1), over_z(a_z2, 2), over_z(a_z3, -1)]
    b_keep, b_y = call(join_b, [(half, f32), (half, bf16)], [VMEM] * 4, "join_b", flops=10**6)(b_keep, *b_got)
    b_got = over_y_lo(b_y)
    w_got = over_core(w)
    prev_grad, weight_grad = call(
        finish, [((512, 256), bf16), ((256, 256), f32)], [VMEM] * 9, "finish", flops=10**6
    )(a_keep, *a_got, b_keep, b_got, mask, w, w_got)
    return weight_grad, prev_grad


def solution(mesh):
    nodes = P(("row", "col"), None)
    return jax.shard_map(
        shards,
        mesh=mesh,
        in_specs=(nodes, nodes, nodes, P(), P("row", "col"), P("row", "col"), P("row", "col"), nodes),
        out_specs=(P(), nodes),
        check_vma=False,
    )
```

```python
import functools

import jax
import jax.numpy as jnp
from jax import lax
from jax.experimental import pallas as pl
from jax.experimental.pallas import tpu as pltpu
from jax.sharding import PartitionSpec as P

T = 128
N_STEP = 512
UNROLL = 16
LIMIT = 16
PREP_LIMIT = 61
STAGE_LIMIT = 24
ZERO_ROW = 32
bf16 = jnp.bfloat16
f32 = jnp.float32
tie = lambda *values: lax.optimization_barrier(values)
VMEM = pl.BlockSpec(memory_space=pltpu.VMEM)
ANY = pl.BlockSpec(memory_space=pl.ANY)
SMEM = pl.BlockSpec(memory_space=pltpu.SMEM)


def call(body, outs, ins, name, limit=8, scratch=(), flops=0, touched=0):
    return pl.pallas_call(
        body,
        in_specs=ins,
        out_specs=[VMEM] * len(outs),
        out_shape=[jax.ShapeDtypeStruct(s, d) for s, d in outs],
        scratch_shapes=list(scratch),
        compiler_params=pltpu.CompilerParams(vmem_limit_bytes=limit * 2**20),
        cost_estimate=pl.CostEstimate(flops=flops, bytes_accessed=touched, transcendentals=0),
        name=name,
    )


def contract(a, b, da, db):
    return lax.dot_general(a, b, (((da,), (db,)), ((), ())), preferred_element_type=f32)


def mask_of(words):
    low = (words & 255).astype(f32)
    high = ((words >> 8) & 255).astype(f32)
    pieces = jnp.concatenate([low, high], 0).astype(bf16)
    w = lax.broadcasted_iota(jnp.int32, (32, 256), 0)
    f = lax.broadcasted_iota(jnp.int32, (32, 256), 1)
    spread = ((f >> 4) + 16 * ((f >> 3) & 1) == w).astype(f32).astype(bf16)
    byte = contract(pieces, spread, 0, 0).astype(jnp.int32)
    lane = lax.broadcasted_iota(jnp.int32, byte.shape, 1)
    return ((byte >> (lane & 7)) & 1) == 1


def prep(grad_hbm, words_hbm, agg_hbm, weight_hbm, ha_ref, hb_ref, keep_ref, send_ref, grad, words, agg, weight, part, sems):
    copies = [
        pltpu.make_async_copy(src, dst, sems.at[i])
        for i, (src, dst) in enumerate(((words_hbm, words), (grad_hbm, grad), (weight_hbm, weight), (agg_hbm, agg)))
    ]
    for copy in copies:
        copy.start()
    copies[0].wait()
    mask = mask_of(words[...])
    copies[1].wait()
    masked = jnp.where(mask, grad[...], jnp.zeros((), bf16))
    copies[2].wait()
    hidden = contract(weight[...], masked, 1, 1).astype(bf16)
    for t in range(4):
        ref = ha_ref if t < 2 else hb_ref
        ref[t & 1] = hidden[:, t * T : (t + 1) * T]
    copies[3].wait()
    part[...] = contract(agg[...], masked, 0, 0) * (1.0 / 256.0)
    core = lax.axis_index("row") & 1
    keep_ref[...] = part[pl.ds(pl.multiple_of(core * T, T), T)]
    send_ref[...] = part[pl.ds(pl.multiple_of((1 - core) * T, T), T)]


def add_two(a, b, out):
    out[...] = a[...] + b[...]


def in_mask(words_ref, out_ref):
    out_ref[...] = mask_of(words_ref[...]).astype(f32).astype(bf16)


def order_slots(count_ref, coords_ref, out_ref):
    device_row, device_col = lax.axis_index("row"), lax.axis_index("col")
    x, y_hi = device_col >> 1, device_col & 1
    y_lo, z, core = device_row >> 3, (device_row >> 1) & 3, device_row & 1
    slots = coords_ref.shape[1]
    slot = lax.broadcasted_iota(jnp.int32, (1, slots), 1)
    i, j = coords_ref[0:1, :], coords_ref[1:2, :]
    t, src = i & 3, i >> 2
    dx, dyh = ((src >> 1) - x) & 3, (src & 1) ^ y_hi
    row = jnp.where(t < 2, dx * 4 + dyh * 2 + t, 16 + dyh * 8 + dx * 2 + (t & 1))
    late = jnp.where(jnp.where(t < 2, dx, dyh) == 0, 0, 64)
    u, q = j & 3, j >> 2
    dc, dz, dy = (q & 1) ^ core ^ 1, ((q >> 1) - z) & 3, (q >> 3) ^ y_lo
    column = (u >> 1) * 32 + dc * 16 + dz * 4 + dy * 2 + (u & 1)
    key = jnp.where(slot < count_ref[0], column + late, T)
    both = jnp.concatenate([key, slot | (row << 9), column << 15, jnp.zeros((5, slots), jnp.int32)], 0).T
    key_c, word_c, high_c = both[:, 0:1], both[:, 1:2], both[:, 2:3]
    s_id = lax.broadcasted_iota(jnp.int32, (slots, slots), 0)
    t_id = lax.broadcasted_iota(jnp.int32, (slots, slots), 1)
    rank = jnp.sum(jnp.where((key == key_c) & (t_id < s_id), 1, 0), 1, keepdims=True)
    k_id = lax.broadcasted_iota(jnp.int32, (slots, T), 1)
    lane = k_id[0:1]
    held = jnp.sum(jnp.where(key_c == k_id, 1, 0), 0, keepdims=True)
    pairs = (held + 1) >> 1

    def list_of(k):
        return jnp.where(k < 64, 0, (k >> 4) - 3)

    start = jnp.zeros((1, 1), jnp.int32)
    starts, counts, base = (jnp.zeros((1, T), jnp.int32) for _ in range(3))
    for number in range(5):
        total = jnp.sum(jnp.where(list_of(lane) == number, pairs, 0), 1, keepdims=True)
        groups = (total + UNROLL - 1) // UNROLL
        starts = jnp.where(lane == number, start, starts)
        counts = jnp.where(lane == number, groups, counts)
        base = jnp.where(list_of(lane) == number, start * UNROLL, base)
        start = start + groups
    ahead = (k_id < key_c) & (list_of(k_id) == list_of(key_c))
    step = jnp.sum(jnp.where(ahead, pairs, 0) + jnp.where(k_id == key_c, base, 0), 1, keepdims=True) + (rank >> 1)
    step = jnp.where(key_c < T, step, -1)
    first = jnp.where((rank & 1) == 0, step, -1)
    second = jnp.where((rank & 1) == 1, step, -1)
    p_id = lax.broadcasted_iota(jnp.int32, (slots, N_STEP), 1)
    none = ZERO_ROW << 9
    none_high = 64 << 15
    out_ref[0:1, :] = (
        jnp.sum(jnp.where(first == p_id, word_c + high_c - none - none_high, 0), 0, keepdims=True) + none + none_high
    )
    out_ref[1:2, :] = jnp.sum(jnp.where(second == p_id, word_c - none, 0), 0, keepdims=True) + none
    out_ref[2:8, :] = jnp.zeros((6, N_STEP), jnp.int32)
    out_ref[2:3, 0:T] = starts
    out_ref[3:4, 0:T] = counts


def stage(count_ref, tiles_ref, out_ref, sems):
    chunk = tiles_ref.shape[0] // 8

    def copy(i):
        part = pl.ds(i * chunk, chunk)
        return pltpu.make_async_copy(tiles_ref.at[part], out_ref.at[part], sems.at[i])

    used = (count_ref[0] + chunk - 1) // chunk
    for i in range(8):
        pl.when(i < used)(lambda i=i: copy(i).start())
    for i in range(8):
        pl.when(i < used)(lambda i=i: copy(i).wait())


def products(number, steps_ref, h_ref, tiles_ref, acc_ref):
    lowest = 0 if number == 0 else (number - 1) * 16
    spare = acc_ref.shape[0] - 1

    def some(g, carry):
        results = []
        for u in range(UNROLL):
            s = g * UNROLL + u
            a, b = steps_ref[0, s], steps_ref[1, s]
            left = jnp.concatenate([h_ref[(a >> 9) & 63], h_ref[b >> 9]], 1)
            right = jnp.concatenate([tiles_ref[a & 511], tiles_ref[b & 511]], 0)
            column = jnp.minimum((a >> 15) - lowest, spare)
            results.append((column, jnp.dot(left, right, preferred_element_type=f32)))
        for column, result in results:
            acc_ref[column] += result
        return carry

    first = steps_ref[2, number]
    lax.fori_loop(first, first + steps_ref[3, number], some, 0)


def early(steps_ref, a0, b0, tiles_ref, acc_ref, h_ref):
    h_ref[0:4], h_ref[16:24] = a0[...], b0[...]
    h_ref[ZERO_ROW] = jnp.zeros((256, T), bf16)

    def clear(k, carry):
        acc_ref[k] = jnp.zeros((256, T), f32)
        return carry

    lax.fori_loop(0, 65, clear, 0)
    products(0, steps_ref, h_ref, tiles_ref, acc_ref)


def late(number, steps_ref, h_ref, tiles_ref, so_far_ref, out_ref, acc_ref):
    base = (number - 1) * 16

    def take(k, carry):
        acc_ref[k] = so_far_ref[base + k]
        return carry

    lax.fori_loop(0, 16, take, 0)
    acc_ref[16] = jnp.zeros((256, T), f32)
    products(number, steps_ref, h_ref, tiles_ref, acc_ref)

    def give(k, carry):
        out_ref[k] = acc_ref[k].astype(out_ref.dtype)
        return carry

    lax.fori_loop(0, 16, give, 0)


def late_first(steps_ref, a0, a3, a1, a2, b0, b1, tiles_ref, so_far_ref, p_ref, q_ref, h_ref, acc_ref):
    h_ref[0:4], h_ref[4:8], h_ref[8:12], h_ref[12:16] = a0[...], a1[...], a2[...], a3[...]
    h_ref[16:24], h_ref[24:32] = b0[...], b1[...]
    h_ref[ZERO_ROW] = jnp.zeros((256, T), bf16)
    late(1, steps_ref, h_ref, tiles_ref, so_far_ref, p_ref, acc_ref)
    late(3, steps_ref, h_ref, tiles_ref, so_far_ref, q_ref, acc_ref)


def join_cores(acc_ref, got_ref, keep, z1, z2, z3):
    for k in range(4):
        keep[k] = acc_ref[k] + got_ref[k].astype(f32)
        for dz, ref in ((1, z1), (2, z2), (3, z3)):
            ref[k] = (acc_ref[4 * dz + k] + got_ref[4 * dz + k].astype(f32)).astype(bf16)


def join_z(keep_ref, g1, g2, g3, keep, y):
    for k in range(4):
        total = keep_ref[k] + g1[k].astype(f32) + g2[k].astype(f32) + g3[k].astype(f32)
        if k < 2:
            keep[k] = total
        else:
            y[k - 2] = total.astype(bf16)


def finish(p_keep, p_got, q_keep, q_got, mask_ref, w, w_got, out_ref, weight_ref):
    core = lax.axis_index("row") & 1
    weight_ref[pl.ds(pl.multiple_of(core * T, T), T)] = w[...]
    weight_ref[pl.ds(pl.multiple_of((1 - core) * T, T), T)] = w_got[...]
    for t in range(4):
        keep, got = (p_keep, p_got) if t < 2 else (q_keep, q_got)
        total = keep[t & 1] + got[t & 1].astype(f32)
        rows = slice(t * T, (t + 1) * T)
        out_ref[rows] = jnp.where(mask_ref[rows] == 1, total.T, 0.0).astype(bf16)


def shards(out_grad, out_bits, agg_saved, weight, tiles, tile_coords, tile_count, in_bits):
    def over_x(v, s):
        return lax.ppermute(v, "col", [(c, (((c >> 1) + s) & 3) * 2 + (c & 1)) for c in range(8)])

    def over_y_hi(v):
        return lax.ppermute(v, "col", [(c, c ^ 1) for c in range(8)])

    def over_z(v, s):
        return lax.ppermute(v, "row", [(r, (r & 9) | ((((r >> 1) + s) & 3) << 1)) for r in range(16)])

    def swap_x(v, bit):
        return lax.ppermute(v, "col", [(c, c ^ (2 << bit)) for c in range(8)])

    def swap_z(v, bit):
        return lax.ppermute(v, "row", [(r, r ^ (2 << bit)) for r in range(16)])

    def over_y_lo(v):
        return lax.ppermute(v, "row", [(r, r ^ 8) for r in range(16)])

    def over_core(v):
        return lax.ppermute(v, "row", [(r, r ^ 1) for r in range(16)])

    half, quad, part = (2, 256, T), (4, 256, T), (T, 256)
    ha, hb, w, w_send = call(
        prep,
        [(half, bf16), (half, bf16), (part, f32), (part, f32)],
        [ANY] * 4,
        "prep",
        limit=PREP_LIMIT,
        scratch=[
            pltpu.VMEM((512, 256), bf16),
            pltpu.VMEM((16, 512), jnp.int32),
            pltpu.VMEM((512, 256), bf16),
            pltpu.VMEM((256, 256), bf16),
            pltpu.VMEM((256, 256), f32),
            pltpu.SemaphoreType.DMA((4,)),
        ],
        flops=2 * 10**8,
    )(out_grad, out_bits.T, agg_saved, weight)

    w_got = over_core(w_send)
    ha_y = over_y_hi(ha)
    hb_1, hb_2, hb_3 = over_x(hb, -1), over_x(hb, 2), over_x(hb, 1)
    count, own_tiles, ha = tie(tile_count.reshape(1), tiles[0, 0], ha)
    (own_tiles,) = call(
        stage,
        [(own_tiles.shape, bf16)],
        [SMEM, ANY],
        "stage",
        limit=STAGE_LIMIT,
        scratch=[pltpu.SemaphoreType.DMA((8,))],
        flops=10**9,
    )(count, own_tiles)
    ha, ha_y, hb, hb_1, hb_2, hb_3, own_tiles, w_got, coords, count = tie(
        ha, ha_y, hb, hb_1, hb_2, hb_3, own_tiles, w_got, tile_coords[0, 0].T, count
    )

    a0 = jnp.concatenate([ha, ha_y], 0)
    b0 = jnp.concatenate([hb, hb_1, hb_2, hb_3], 0)
    a3, a1, a2 = over_x(a0, 1), over_x(a0, -1), over_x(a0, 2)
    b1 = over_y_hi(b0)
    add_w = call(add_two, [(part, f32)], [VMEM] * 2, "add_w", limit=2)
    (steps,) = call(order_slots, [((8, N_STEP), jnp.int32)], [SMEM, VMEM], "order_slots", flops=10**7)(count, coords)
    (w,) = add_w(w, w_got)
    w_got = swap_z(w, 0)
    (acc,) = call(
        early,
        [((65, 256, T), f32)],
        [SMEM] + [VMEM] * 3,
        "early",
        limit=LIMIT,
        scratch=[pltpu.VMEM((33, 256, T), bf16)],
        flops=4 * 10**9,
    )(steps, a0, b0, own_tiles)
    acc, w, w_got = tie(acc, w, w_got)
    (w,) = add_w(w, w_got)
    a0, a1, a2, a3, b0, b1, acc, w = tie(a0, a1, a2, a3, b0, b1, acc, w)
    w_got = swap_z(w, 1)

    cost = dict(flops=2 * 10**9)
    group = [pltpu.VMEM((17, 256, T), f32)]
    sixteen = (16, 256, T)

    def later(number, kind):
        body = functools.partial(late, number)
        name = "late_" + str(number)
        outs = [(sixteen, kind)]
        return call(body, outs, [SMEM] + [VMEM] * 3, name, limit=LIMIT, scratch=group, **cost)

    def split(own, got, name):
        outs = [(quad, f32)] + [(quad, bf16)] * 3
        return call(join_cores, outs, [VMEM] * 2, name, flops=10**6)(own, got)

    def around_z(z1, z2, z3):
        return over_z(z1, 1), over_z(z2, 2), over_z(z3, -1)

    def gather_z(keep, got, name):
        return call(join_z, [(half, f32), (half, bf16)], [VMEM] * 4, name, flops=10**6)(keep, *got)

    p_partner, q_partner, hidden = call(
        late_first,
        [(sixteen, bf16), (sixteen, bf16), ((33, 256, T), bf16)],
        [SMEM] + [VMEM] * 8,
        "late_first",
        limit=LIMIT,
        scratch=group,
        **cost,
    )(steps, a0, a3, a1, a2, b0, b1, own_tiles, acc)
    p_partner, q_partner, hidden, w, w_got = tie(p_partner, q_partner, hidden, w, w_got)
    p_partner, q_partner = over_core(p_partner), over_core(q_partner)
    (w,) = add_w(w, w_got)
    hidden, w = tie(hidden, w)
    w_got = over_y_lo(w)
    (own,) = later(2, f32)(steps, hidden, own_tiles, acc)
    p_keep, *p_z = split(own, p_partner, "split_p")
    p_z = around_z(*p_z)
    p_keep, hidden, w, w_got, q_partner = tie(p_keep, hidden, w, w_got, q_partner)
    (w,) = add_w(w, w_got)
    hidden, w = tie(hidden, w)
    w_got = over_y_hi(w)
    (own,) = later(4, f32)(steps, hidden, own_tiles, acc)
    q_keep, *q_z = split(own, q_partner, "split_q")
    q_z = around_z(*q_z)
    q_keep, w, w_got, words = tie(q_keep, w, w_got, in_bits.T)
    (w,) = add_w(w, w_got)
    w_got = swap_x(w, 0)
    (mask,) = call(in_mask, [((512, 256), bf16)], [VMEM], "in_mask", flops=10**7)(words)
    p_keep, p_y = gather_z(p_keep, p_z, "gather_p")
    p_got = over_y_lo(p_y)
    p_keep, w, w_got, mask = tie(p_keep, w, w_got, mask)
    (w,) = add_w(w, w_got)
    w_got = swap_x(w, 1)
    (w,) = add_w(w, w_got)
    w_got = over_core(w)
    q_keep, p_got = tie(q_keep, p_got)
    q_keep, q_y = gather_z(q_keep, q_z, "gather_q")
    q_got = over_y_lo(q_y)
    prev_grad, weight_grad = call(
        finish, [((512, 256), bf16), ((256, 256), f32)], [VMEM] * 7, "finish", flops=10**6
    )(p_keep, p_got, q_keep, q_got, mask, w, w_got)
    return weight_grad, prev_grad


def solution(mesh):
    nodes = P(("row", "col"), None)
    return jax.shard_map(
        shards,
        mesh=mesh,
        in_specs=(nodes, nodes, nodes, P(), P("row", "col"), P("row", "col"), P("row", "col"), nodes),
        out_specs=(P(), nodes),
        check_vma=False,
    )
```

```python
import functools

import jax
import jax.numpy as jnp
from jax import lax
from jax.experimental import pallas as pl
from jax.experimental.pallas import tpu as pltpu
from jax.sharding import PartitionSpec as P

T = 128
N_STEP = 512
UNROLL = 16
LIMIT = 16
PREP_LIMIT = 61
STAGE_LIMIT = 24
ZERO_ROW = 32
LOWEST = (0, 0, 32, 48)
bf16 = jnp.bfloat16
f32 = jnp.float32
tie = lambda *values: lax.optimization_barrier(values)
VMEM = pl.BlockSpec(memory_space=pltpu.VMEM)
ANY = pl.BlockSpec(memory_space=pl.ANY)
SMEM = pl.BlockSpec(memory_space=pltpu.SMEM)


def call(body, outs, ins, name, limit=8, scratch=(), flops=0, touched=0):
    return pl.pallas_call(
        body,
        in_specs=ins,
        out_specs=[VMEM] * len(outs),
        out_shape=[jax.ShapeDtypeStruct(s, d) for s, d in outs],
        scratch_shapes=list(scratch),
        compiler_params=pltpu.CompilerParams(vmem_limit_bytes=limit * 2**20),
        cost_estimate=pl.CostEstimate(flops=flops, bytes_accessed=touched, transcendentals=0),
        name=name,
    )


def contract(a, b, da, db):
    return lax.dot_general(a, b, (((da,), (db,)), ((), ())), preferred_element_type=f32)


def mask_of(words):
    low = (words & 255).astype(f32)
    high = ((words >> 8) & 255).astype(f32)
    pieces = jnp.concatenate([low, high], 0).astype(bf16)
    w = lax.broadcasted_iota(jnp.int32, (32, 256), 0)
    f = lax.broadcasted_iota(jnp.int32, (32, 256), 1)
    spread = ((f >> 4) + 16 * ((f >> 3) & 1) == w).astype(f32).astype(bf16)
    byte = contract(pieces, spread, 0, 0).astype(jnp.int32)
    lane = lax.broadcasted_iota(jnp.int32, byte.shape, 1)
    return ((byte >> (lane & 7)) & 1) == 1


def both_parts(value):
    high = value.astype(bf16)
    return jnp.concatenate([high, (value - high.astype(f32)).astype(bf16)], 0)


def whole(parts):
    return parts[0:T].astype(f32) + parts[T : 2 * T].astype(f32)


def prep(grad_hbm, words_hbm, agg_hbm, weight_hbm, ha, hb, m1, m2, m3, keep, grad, words, agg, weight, part, sems):
    copies = [
        pltpu.make_async_copy(src, dst, sems.at[i])
        for i, (src, dst) in enumerate(((words_hbm, words), (grad_hbm, grad), (weight_hbm, weight), (agg_hbm, agg)))
    ]
    for copy in copies:
        copy.start()
    copies[0].wait()
    mask = mask_of(words[...])
    copies[1].wait()
    masked = jnp.where(mask, grad[...], jnp.zeros((), bf16))
    copies[2].wait()
    hidden = contract(weight[...], masked, 1, 1).astype(bf16)
    for t in range(2):
        ha[t] = hidden[:, t * T : (t + 1) * T]
        for ref in (hb, m1, m2, m3):
            ref[t] = hidden[:, (t + 2) * T : (t + 3) * T]
    copies[3].wait()
    part[...] = contract(agg[...], masked, 0, 0) * (1.0 / 256.0)
    x = lax.axis_index("col") >> 1

    def quarter(q):
        rows = part[pl.ds(pl.multiple_of(q * 64, 64), 64)]
        return jnp.concatenate([rows[:, 0:T], rows[:, T : 2 * T]], 0)

    keep[...] = quarter(x)
    for s, ref in ((1, m1), (2, m2), (3, m3)):
        ref[2] = both_parts(quarter((x + s) & 3))


def pack(ha, ha_y, hb, m1, m2, m3, keep, a0, b0):
    a0[0:2], a0[2:4] = ha[...], ha_y[...]
    b0[0:2], b0[2:4], b0[4:6], b0[6:8] = hb[...], m1[0:2], m2[0:2], m3[0:2]
    b0[8] = both_parts((keep[...] + whole(m2[2])) + (whole(m1[2]) + whole(m3[2])))


def sum_parts(own, got, out):
    out[...] = whole(own[2]) + whole(got[2])


def pair_up(own, got, out):
    odd = (lax.axis_index("col") >> 1) & 1
    out[odd] = own[...]
    out[1 - odd] = got[...]


def in_mask(words_ref, out_ref):
    out_ref[...] = mask_of(words_ref[...]).astype(f32).astype(bf16)


def order_slots(count_ref, coords_ref, out_ref):
    device_row, device_col = lax.axis_index("row"), lax.axis_index("col")
    x, y_hi = device_col >> 1, device_col & 1
    y_lo, z, core = device_row >> 3, (device_row >> 1) & 3, device_row & 1
    slots = coords_ref.shape[1]
    slot = lax.broadcasted_iota(jnp.int32, (1, slots), 1)
    i, j = coords_ref[0:1, :], coords_ref[1:2, :]
    t, src = i & 3, i >> 2
    dx, dyh = ((src >> 1) - x) & 3, (src & 1) ^ y_hi
    row = jnp.where(t < 2, dx * 4 + dyh * 2 + t, 16 + dyh * 8 + dx * 2 + (t & 1))
    late = jnp.where(jnp.where(t < 2, dx, dyh) == 0, 0, 64)
    u, q = j & 3, j >> 2
    dc, dz, dy = (q & 1) ^ core ^ 1, ((q >> 1) - z) & 3, (q >> 3) ^ y_lo
    column = dc * 32 + (u >> 1) * 16 + dz * 4 + dy * 2 + (u & 1)
    key = jnp.where(slot < count_ref[0], column + late, T)
    both = jnp.concatenate([key, slot | (row << 9), column << 15, jnp.zeros((5, slots), jnp.int32)], 0).T
    key_c, word_c, high_c = both[:, 0:1], both[:, 1:2], both[:, 2:3]
    s_id = lax.broadcasted_iota(jnp.int32, (slots, slots), 0)
    t_id = lax.broadcasted_iota(jnp.int32, (slots, slots), 1)
    rank = jnp.sum(jnp.where((key == key_c) & (t_id < s_id), 1, 0), 1, keepdims=True)
    k_id = lax.broadcasted_iota(jnp.int32, (slots, T), 1)
    lane = k_id[0:1]
    held = jnp.sum(jnp.where(key_c == k_id, 1, 0), 0, keepdims=True)
    pairs = (held + 1) >> 1

    def list_of(k):
        return jnp.where(k < 64, 0, jnp.maximum((k >> 4) - 4, 1))

    start = jnp.zeros((1, 1), jnp.int32)
    starts, counts, base = (jnp.zeros((1, T), jnp.int32) for _ in range(3))
    for number in range(4):
        total = jnp.sum(jnp.where(list_of(lane) == number, pairs, 0), 1, keepdims=True)
        groups = (total + UNROLL - 1) // UNROLL
        starts = jnp.where(lane == number, start, starts)
        counts = jnp.where(lane == number, groups, counts)
        base = jnp.where(list_of(lane) == number, start * UNROLL, base)
        start = start + groups
    ahead = (k_id < key_c) & (list_of(k_id) == list_of(key_c))
    step = jnp.sum(jnp.where(ahead, pairs, 0) + jnp.where(k_id == key_c, base, 0), 1, keepdims=True) + (rank >> 1)
    step = jnp.where(key_c < T, step, -1)
    first = jnp.where((rank & 1) == 0, step, -1)
    second = jnp.where((rank & 1) == 1, step, -1)
    p_id = lax.broadcasted_iota(jnp.int32, (slots, N_STEP), 1)
    none = ZERO_ROW << 9
    none_high = 64 << 15
    out_ref[0:1, :] = (
        jnp.sum(jnp.where(first == p_id, word_c + high_c - none - none_high, 0), 0, keepdims=True) + none + none_high
    )
    out_ref[1:2, :] = jnp.sum(jnp.where(second == p_id, word_c - none, 0), 0, keepdims=True) + none
    out_ref[2:8, :] = jnp.zeros((6, N_STEP), jnp.int32)
    out_ref[2:3, 0:T] = starts
    out_ref[3:4, 0:T] = counts


def stage(count_ref, tiles_ref, out_ref, sems):
    chunk = tiles_ref.shape[0] // 8

    def copy(i):
        part = pl.ds(i * chunk, chunk)
        return pltpu.make_async_copy(tiles_ref.at[part], out_ref.at[part], sems.at[i])

    used = (count_ref[0] + chunk - 1) // chunk
    for i in range(8):
        pl.when(i < used)(lambda i=i: copy(i).start())
    for i in range(8):
        pl.when(i < used)(lambda i=i: copy(i).wait())


def products(number, steps_ref, h_ref, tiles_ref, acc_ref):
    lowest = LOWEST[number]
    spare = acc_ref.shape[0] - 1

    def some(g, carry):
        results = []
        for u in range(UNROLL):
            s = g * UNROLL + u
            a, b = steps_ref[0, s], steps_ref[1, s]
            left = jnp.concatenate([h_ref[(a >> 9) & 63], h_ref[b >> 9]], 1)
            right = jnp.concatenate([tiles_ref[a & 511], tiles_ref[b & 511]], 0)
            column = jnp.minimum((a >> 15) - lowest, spare)
            results.append((column, jnp.dot(left, right, preferred_element_type=f32)))
        for column, result in results:
            acc_ref[column] += result
        return carry

    first = steps_ref[2, number]
    lax.fori_loop(first, first + steps_ref[3, number], some, 0)


def early(steps_ref, a0, b0, tiles_ref, acc_ref, h_ref):
    h_ref[0:4], h_ref[16:24] = a0[...], b0[0:8]
    h_ref[ZERO_ROW] = jnp.zeros((256, T), bf16)

    def clear(k, carry):
        acc_ref[k] = jnp.zeros((256, T), f32)
        return carry

    lax.fori_loop(0, 65, clear, 0)
    products(0, steps_ref, h_ref, tiles_ref, acc_ref)


def late(number, steps_ref, h_ref, tiles_ref, so_far_ref, outs, acc_ref):
    base, columns = LOWEST[number], 16 * len(outs)

    def take(k, carry):
        acc_ref[k] = so_far_ref[base + k]
        return carry

    lax.fori_loop(0, columns, take, 0)
    acc_ref[columns] = jnp.zeros((256, T), f32)
    products(number, steps_ref, h_ref, tiles_ref, acc_ref)
    for i, ref in enumerate(outs):

        def give(k, carry, i=i, ref=ref):
            ref[k] = acc_ref[16 * i + k].astype(ref.dtype)
            return carry

        lax.fori_loop(0, 16, give, 0)


def late_partner(steps_ref, a0, a3, a1, a2, b0, b1, tiles_ref, so_far_ref, p_ref, q_ref, h_ref, acc_ref):
    h_ref[0:4], h_ref[4:8], h_ref[8:12], h_ref[12:16] = a0[...], a1[...], a2[...], a3[...]
    h_ref[16:24], h_ref[24:32] = b0[0:8], b1[0:8]
    h_ref[ZERO_ROW] = jnp.zeros((256, T), bf16)
    p_ref[16] = both_parts(whole(b0[8]) + whole(b1[8]))
    late(1, steps_ref, h_ref, tiles_ref, so_far_ref, (p_ref, q_ref), acc_ref)


def late_own(number, steps_ref, h_ref, tiles_ref, so_far_ref, out_ref, acc_ref):
    late(number, steps_ref, h_ref, tiles_ref, so_far_ref, (out_ref,), acc_ref)


def split_q(acc_ref, got_ref, keep, z1, z2, z3):
    for k in range(4):
        keep[k] = acc_ref[k] + got_ref[k].astype(f32)
        for dz, ref in ((1, z1), (2, z2), (3, z3)):
            ref[k * 256 : (k + 1) * 256] = (acc_ref[4 * dz + k] + got_ref[4 * dz + k].astype(f32)).astype(bf16)


def split_p(acc_ref, got_ref, sent_ref, keep, z1, z2, z3):
    split_q(acc_ref, got_ref, keep, z1, z2, z3)
    total = (whole(sent_ref[16]) + whole(got_ref[16])).astype(bf16)
    for ref in (z1, z2, z3):
        ref[1024 : 1024 + T] = total


def gather_q(keep_ref, g1, g2, g3, keep, y):
    for k in range(4):
        rows = slice(k * 256, (k + 1) * 256)
        total = keep_ref[k] + g1[rows].astype(f32) + g2[rows].astype(f32) + g3[rows].astype(f32)
        if k < 2:
            keep[k] = total
        else:
            y[k - 2] = total.astype(bf16)


def gather_p(keep_ref, g1, g2, g3, sent_ref, keep, y):
    gather_q(keep_ref, g1, g2, g3, keep, y)
    own, left, across, right = (ref[1024 : 1024 + T].astype(f32) for ref in (sent_ref, g1, g2, g3))
    y[2] = both_parts((own + across) + (left + right))


def finish(p_keep, p_got, q_keep, q_got, mask_ref, w, w_got, out_ref, weight_ref):
    upper = lax.axis_index("col") >> 2
    for pair, ref in ((upper, w), (1 - upper, w_got)):
        for i in range(2):
            rows = pl.ds(pl.multiple_of(pair * T + i * 64, 64), 64)
            weight_ref[rows, 0:T] = ref[i, 0:64]
            weight_ref[rows, T : 2 * T] = ref[i, 64:T]
    for t in range(4):
        keep, got = (p_keep, p_got) if t < 2 else (q_keep, q_got)
        total = keep[t & 1] + got[t & 1].astype(f32)
        rows = slice(t * T, (t + 1) * T)
        out_ref[rows] = jnp.where(mask_ref[rows] == 1, total.T, 0.0).astype(bf16)


def shards(out_grad, out_bits, agg_saved, weight, tiles, tile_coords, tile_count, in_bits):
    def over_x(v, s):
        return lax.ppermute(v, "col", [(c, (((c >> 1) + s) & 3) * 2 + (c & 1)) for c in range(8)])

    def over_y_hi(v):
        return lax.ppermute(v, "col", [(c, c ^ 1) for c in range(8)])

    def over_z(v, s):
        return lax.ppermute(v, "row", [(r, (r & 9) | ((((r >> 1) + s) & 3) << 1)) for r in range(16)])

    def swap_x(v, bit):
        return lax.ppermute(v, "col", [(c, c ^ (2 << bit)) for c in range(8)])

    def over_y_lo(v):
        return lax.ppermute(v, "row", [(r, r ^ 8) for r in range(16)])

    def over_core(v):
        return lax.ppermute(v, "row", [(r, r ^ 1) for r in range(16)])

    half, three, quad, square = (2, 256, T), (3, 256, T), (4, 256, T), (T, T)
    ha, hb, m1, m2, m3, w = call(
        prep,
        [(half, bf16)] * 2 + [(three, bf16)] * 3 + [(square, f32)],
        [ANY] * 4,
        "prep",
        limit=PREP_LIMIT,
        scratch=[
            pltpu.VMEM((512, 256), bf16),
            pltpu.VMEM((16, 512), jnp.int32),
            pltpu.VMEM((512, 256), bf16),
            pltpu.VMEM((256, 256), bf16),
            pltpu.VMEM((256, 256), f32),
            pltpu.SemaphoreType.DMA((4,)),
        ],
        flops=2 * 10**8,
    )(out_grad, out_bits.T, agg_saved, weight)

    ha_y = over_y_hi(ha)
    m3, m2, m1 = over_x(m1, 1), over_x(m2, 2), over_x(m3, 3)
    count, own_tiles, ha = tie(tile_count.reshape(1), tiles[0, 0], ha)
    (own_tiles,) = call(
        stage,
        [(own_tiles.shape, bf16)],
        [SMEM, ANY],
        "stage",
        limit=STAGE_LIMIT,
        scratch=[pltpu.SemaphoreType.DMA((8,))],
        flops=10**9,
    )(count, own_tiles)
    ha, ha_y, hb, m1, m2, m3, own_tiles, coords, count = tie(
        ha, ha_y, hb, m1, m2, m3, own_tiles, tile_coords[0, 0].T, count
    )

    a0, b0 = call(pack, [(quad, bf16), ((9, 256, T), bf16)], [VMEM] * 7, "pack", flops=10**6)(
        ha, ha_y, hb, m1, m2, m3, w
    )
    b1 = over_y_hi(b0)
    a3, a1, a2 = over_x(a0, 1), over_x(a0, -1), over_x(a0, 2)
    (steps,) = call(order_slots, [((8, N_STEP), jnp.int32)], [SMEM, VMEM], "order_slots", flops=10**7)(count, coords)
    (acc,) = call(
        early,
        [((65, 256, T), f32)],
        [SMEM] + [VMEM] * 3,
        "early",
        limit=LIMIT,
        scratch=[pltpu.VMEM((33, 256, T), bf16)],
        flops=4 * 10**9,
    )(steps, a0, b0, own_tiles)
    a0, a1, a2, a3, b0, b1, acc = tie(a0, a1, a2, a3, b0, b1, acc)

    sixteen = (16, 256, T)
    z_p, z_q = (1024 + T, T), (1024, T)

    def own_columns(number):
        return call(
            functools.partial(late_own, number),
            [(sixteen, f32)],
            [SMEM] + [VMEM] * 3,
            "late_" + str(number),
            limit=LIMIT,
            scratch=[pltpu.VMEM((17, 256, T), f32)],
            flops=2 * 10**9,
        )(steps, hidden, own_tiles, acc)[0]

    def around_z(z1, z2, z3):
        return over_z(z1, 1), over_z(z2, 2), over_z(z3, 3)

    p_sent, q_sent, hidden = call(
        late_partner,
        [((17, 256, T), bf16), (sixteen, bf16), ((33, 256, T), bf16)],
        [SMEM] + [VMEM] * 8,
        "late_1",
        limit=LIMIT,
        scratch=[pltpu.VMEM((33, 256, T), f32)],
        flops=4 * 10**9,
    )(steps, a0, a3, a1, a2, b0, b1, own_tiles, acc)
    p_got, q_got = over_core(p_sent), over_core(q_sent)
    own = own_columns(2)
    p_keep, *p_z = call(split_p, [(quad, f32)] + [(z_p, bf16)] * 3, [VMEM] * 3, "split_p", flops=10**6)(
        own, p_got, p_sent
    )
    p_all = around_z(*p_z)
    p_keep, hidden, q_got = tie(p_keep, hidden, q_got)
    own = own_columns(3)
    q_keep, *q_z = call(split_q, [(quad, f32)] + [(z_q, bf16)] * 3, [VMEM] * 2, "split_q", flops=10**6)(own, q_got)
    q_all = around_z(*q_z)
    p_keep, q_keep, words = tie(p_keep, q_keep, in_bits.T)
    (mask,) = call(in_mask, [((512, 256), bf16)], [VMEM], "in_mask", flops=10**7)(words)
    p_keep, p_y = call(gather_p, [(half, f32), (three, bf16)], [VMEM] * 5, "gather_p", flops=10**6)(
        p_keep, *p_all, p_z[0]
    )
    p_got = over_y_lo(p_y)
    p_keep, p_got, q_keep, mask = tie(p_keep, p_got, q_keep, mask)
    q_keep, q_y = call(gather_q, [(half, f32), (half, bf16)], [VMEM] * 4, "gather_q", flops=10**6)(q_keep, *q_all)
    q_got = over_y_lo(q_y)
    p_y, p_got, q_keep = tie(p_y, p_got, q_keep)
    (w,) = call(sum_parts, [(square, f32)], [VMEM] * 2, "sum_parts", limit=2)(p_y, p_got)
    (w,) = call(pair_up, [((2, T, T), f32)], [VMEM] * 2, "pair_up", limit=2)(w, swap_x(w, 0))
    w_got = swap_x(w, 1)
    prev_grad, weight_grad = call(
        finish, [((512, 256), bf16), ((256, 256), f32)], [VMEM] * 7, "finish", flops=10**6
    )(p_keep, p_got, q_keep, q_got, mask, w, w_got)
    return weight_grad, prev_grad


def solution(mesh):
    nodes = P(("row", "col"), None)
    return jax.shard_map(
        shards,
        mesh=mesh,
        in_specs=(nodes, nodes, nodes, P(), P("row", "col"), P("row", "col"), P("row", "col"), nodes),
        out_specs=(P(), nodes),
        check_vma=False,
    )
```

```python
import functools

import jax
import jax.numpy as jnp
from jax import lax
from jax.experimental import pallas as pl
from jax.experimental.pallas import tpu as pltpu
from jax.sharding import PartitionSpec as P

T = 128
N_STEP = 512
UNROLL = 16
LIMIT = 16
PREP_LIMIT = 61
STAGE_LIMIT = 24
ZERO_ROW = 32
LOWEST = (0, 0, 32, 48)
bf16 = jnp.bfloat16
f32 = jnp.float32
tie = lambda *values: lax.optimization_barrier(values)
VMEM = pl.BlockSpec(memory_space=pltpu.VMEM)
ANY = pl.BlockSpec(memory_space=pl.ANY)
SMEM = pl.BlockSpec(memory_space=pltpu.SMEM)


def call(body, outs, ins, name, limit=8, scratch=(), flops=0, touched=0):
    return pl.pallas_call(
        body,
        in_specs=ins,
        out_specs=[VMEM] * len(outs),
        out_shape=[jax.ShapeDtypeStruct(s, d) for s, d in outs],
        scratch_shapes=list(scratch),
        compiler_params=pltpu.CompilerParams(vmem_limit_bytes=limit * 2**20),
        cost_estimate=pl.CostEstimate(flops=flops, bytes_accessed=touched, transcendentals=0),
        name=name,
    )


def contract(a, b, da, db):
    return lax.dot_general(a, b, (((da,), (db,)), ((), ())), preferred_element_type=f32)


def mask_of(words):
    low = (words & 255).astype(f32)
    high = ((words >> 8) & 255).astype(f32)
    pieces = jnp.concatenate([low, high], 0).astype(bf16)
    w = lax.broadcasted_iota(jnp.int32, (32, 256), 0)
    f = lax.broadcasted_iota(jnp.int32, (32, 256), 1)
    spread = ((f >> 4) + 16 * ((f >> 3) & 1) == w).astype(f32).astype(bf16)
    byte = contract(pieces, spread, 0, 0).astype(jnp.int32)
    lane = lax.broadcasted_iota(jnp.int32, byte.shape, 1)
    return ((byte >> (lane & 7)) & 1) == 1


def both_parts(value):
    high = value.astype(bf16)
    return jnp.concatenate([high, (value - high.astype(f32)).astype(bf16)], 0)


def whole(parts):
    return parts[0:T].astype(f32) + parts[T : 2 * T].astype(f32)


def prep(grad_hbm, words_hbm, agg_hbm, weight_hbm, ha, hb, m1, m2, m3, keep, grad, words, agg, weight, part, sems):
    copies = [
        pltpu.make_async_copy(src, dst, sems.at[i])
        for i, (src, dst) in enumerate(((words_hbm, words), (grad_hbm, grad), (weight_hbm, weight), (agg_hbm, agg)))
    ]
    for copy in copies:
        copy.start()
    copies[0].wait()
    mask = mask_of(words[...])
    copies[1].wait()
    masked = jnp.where(mask, grad[...], jnp.zeros((), bf16))
    copies[2].wait()
    hidden = contract(weight[...], masked, 1, 1).astype(bf16)
    for t in range(2):
        ha[t] = hidden[:, t * T : (t + 1) * T]
        hb[t] = hidden[:, (t + 2) * T : (t + 3) * T]
        for ref in (m1, m2, m3):
            ref[t * 256 : (t + 1) * 256] = hidden[:, (t + 2) * T : (t + 3) * T]
    copies[3].wait()
    part[...] = contract(agg[...], masked, 0, 0) * (1.0 / 256.0)
    x = lax.axis_index("col") >> 1

    def quarter(q):
        rows = part[pl.ds(pl.multiple_of(q * 64, 64), 64)]
        return jnp.concatenate([rows[:, 0:T], rows[:, T : 2 * T]], 0)

    keep[...] = quarter(x)
    for s, ref in ((1, m1), (2, m2), (3, m3)):
        ref[512 : 512 + T] = quarter((x + s) & 3).astype(bf16)


def pack(ha, ha_y, hb, m1, m2, m3, keep, a0, b0):
    a0[0:2], a0[2:4] = ha[...], ha_y[...]
    b0[0:2] = hb[...]
    total = keep[...]
    for s, ref in ((1, m1), (2, m2), (3, m3)):
        b0[2 * s], b0[2 * s + 1] = ref[0:256], ref[256:512]
        total += ref[512 : 512 + T].astype(f32)
    b0[8] = both_parts(total)


def add_two(a, b, out):
    out[...] = a[...] + b[...]


def pair_up(own, got, out):
    odd = (lax.axis_index("col") >> 1) & 1
    out[odd] = own[...]
    out[1 - odd] = got[...]


def in_mask(words_ref, out_ref):
    out_ref[...] = mask_of(words_ref[...]).astype(f32).astype(bf16)


def order_slots(count_ref, coords_ref, out_ref):
    device_row, device_col = lax.axis_index("row"), lax.axis_index("col")
    x, y_hi = device_col >> 1, device_col & 1
    y_lo, z, core = device_row >> 3, (device_row >> 1) & 3, device_row & 1
    slots = coords_ref.shape[1]
    slot = lax.broadcasted_iota(jnp.int32, (1, slots), 1)
    i, j = coords_ref[0:1, :], coords_ref[1:2, :]
    t, src = i & 3, i >> 2
    dx, dyh = ((src >> 1) - x) & 3, (src & 1) ^ y_hi
    row = jnp.where(t < 2, dx * 4 + dyh * 2 + t, 16 + dyh * 8 + dx * 2 + (t & 1))
    late = jnp.where(jnp.where(t < 2, dx, dyh) == 0, 0, 64)
    u, q = j & 3, j >> 2
    dc, dz, dy = (q & 1) ^ core ^ 1, ((q >> 1) - z) & 3, (q >> 3) ^ y_lo
    column = dc * 32 + (u >> 1) * 16 + dz * 4 + dy * 2 + (u & 1)
    key = jnp.where(slot < count_ref[0], column + late, T)
    both = jnp.concatenate([key, slot | (row << 9), column << 15, jnp.zeros((5, slots), jnp.int32)], 0).T
    key_c, word_c, high_c = both[:, 0:1], both[:, 1:2], both[:, 2:3]
    s_id = lax.broadcasted_iota(jnp.int32, (slots, slots), 0)
    t_id = lax.broadcasted_iota(jnp.int32, (slots, slots), 1)
    rank = jnp.sum(jnp.where((key == key_c) & (t_id < s_id), 1, 0), 1, keepdims=True)
    k_id = lax.broadcasted_iota(jnp.int32, (slots, T), 1)
    lane = k_id[0:1]
    held = jnp.sum(jnp.where(key_c == k_id, 1, 0), 0, keepdims=True)
    pairs = (held + 1) >> 1

    def list_of(k):
        return jnp.where(k < 64, 0, jnp.maximum((k >> 4) - 4, 1))

    start = jnp.zeros((1, 1), jnp.int32)
    starts, counts, base = (jnp.zeros((1, T), jnp.int32) for _ in range(3))
    for number in range(4):
        total = jnp.sum(jnp.where(list_of(lane) == number, pairs, 0), 1, keepdims=True)
        groups = (total + UNROLL - 1) // UNROLL
        starts = jnp.where(lane == number, start, starts)
        counts = jnp.where(lane == number, groups, counts)
        base = jnp.where(list_of(lane) == number, start * UNROLL, base)
        start = start + groups
    ahead = (k_id < key_c) & (list_of(k_id) == list_of(key_c))
    step = jnp.sum(jnp.where(ahead, pairs, 0) + jnp.where(k_id == key_c, base, 0), 1, keepdims=True) + (rank >> 1)
    step = jnp.where(key_c < T, step, -1)
    first = jnp.where((rank & 1) == 0, step, -1)
    second = jnp.where((rank & 1) == 1, step, -1)
    p_id = lax.broadcasted_iota(jnp.int32, (slots, N_STEP), 1)
    none = ZERO_ROW << 9
    none_high = 64 << 15
    out_ref[0:1, :] = (
        jnp.sum(jnp.where(first == p_id, word_c + high_c - none - none_high, 0), 0, keepdims=True) + none + none_high
    )
    out_ref[1:2, :] = jnp.sum(jnp.where(second == p_id, word_c - none, 0), 0, keepdims=True) + none
    out_ref[2:8, :] = jnp.zeros((6, N_STEP), jnp.int32)
    out_ref[2:3, 0:T] = starts
    out_ref[3:4, 0:T] = counts


def stage(count_ref, tiles_ref, out_ref, sems):
    chunk = tiles_ref.shape[0] // 8

    def copy(i):
        part = pl.ds(i * chunk, chunk)
        return pltpu.make_async_copy(tiles_ref.at[part], out_ref.at[part], sems.at[i])

    used = (count_ref[0] + chunk - 1) // chunk
    for i in range(8):
        pl.when(i < used)(lambda i=i: copy(i).start())
    for i in range(8):
        pl.when(i < used)(lambda i=i: copy(i).wait())


def products(number, steps_ref, h_ref, tiles_ref, acc_ref):
    lowest = LOWEST[number]
    spare = acc_ref.shape[0] - 1

    def some(g, carry):
        results = []
        for u in range(UNROLL):
            s = g * UNROLL + u
            a, b = steps_ref[0, s], steps_ref[1, s]
            left = jnp.concatenate([h_ref[(a >> 9) & 63], h_ref[b >> 9]], 1)
            right = jnp.concatenate([tiles_ref[a & 511], tiles_ref[b & 511]], 0)
            column = jnp.minimum((a >> 15) - lowest, spare)
            results.append((column, jnp.dot(left, right, preferred_element_type=f32)))
        for column, result in results:
            acc_ref[column] += result
        return carry

    first = steps_ref[2, number]
    lax.fori_loop(first, first + steps_ref[3, number], some, 0)


def early(steps_ref, a0, b0, tiles_ref, acc_ref, h_ref):
    h_ref[0:4], h_ref[16:24] = a0[...], b0[0:8]
    h_ref[ZERO_ROW] = jnp.zeros((256, T), bf16)

    def clear(k, carry):
        acc_ref[k] = jnp.zeros((256, T), f32)
        return carry

    lax.fori_loop(0, 65, clear, 0)
    products(0, steps_ref, h_ref, tiles_ref, acc_ref)


def late(number, steps_ref, h_ref, tiles_ref, so_far_ref, outs, acc_ref):
    base, columns = LOWEST[number], 16 * len(outs)

    def take(k, carry):
        acc_ref[k] = so_far_ref[base + k]
        return carry

    lax.fori_loop(0, columns, take, 0)
    acc_ref[columns] = jnp.zeros((256, T), f32)
    products(number, steps_ref, h_ref, tiles_ref, acc_ref)
    for i, ref in enumerate(outs):

        def give(k, carry, i=i, ref=ref):
            ref[k] = acc_ref[16 * i + k].astype(ref.dtype)
            return carry

        lax.fori_loop(0, 16, give, 0)


def late_partner(steps_ref, a0, a3, a1, a2, b0, b1, tiles_ref, so_far_ref, p_ref, q_ref, h_ref, acc_ref):
    h_ref[0:4], h_ref[4:8], h_ref[8:12], h_ref[12:16] = a0[...], a1[...], a2[...], a3[...]
    h_ref[16:24], h_ref[24:32] = b0[0:8], b1[0:8]
    h_ref[ZERO_ROW] = jnp.zeros((256, T), bf16)
    p_ref[16] = both_parts(whole(b0[8]) + whole(b1[8]))
    late(1, steps_ref, h_ref, tiles_ref, so_far_ref, (p_ref, q_ref), acc_ref)


def late_own(number, steps_ref, h_ref, tiles_ref, so_far_ref, out_ref, acc_ref):
    late(number, steps_ref, h_ref, tiles_ref, so_far_ref, (out_ref,), acc_ref)


def split_p(acc_ref, got_ref, sent_ref, keep, z1, z2, z3):
    for k in range(4):
        keep[k] = acc_ref[k] + got_ref[k].astype(f32)
        for dz, ref in ((1, z1), (2, z2), (3, z3)):
            ref[k * 256 : (k + 1) * 256] = (acc_ref[4 * dz + k] + got_ref[4 * dz + k].astype(f32)).astype(bf16)
    total = (whole(sent_ref[16]) + whole(got_ref[16])).astype(bf16)
    for ref in (z1, z2, z3):
        ref[1024 : 1024 + T] = total


def gather_p(keep_ref, g1, g2, g3, sent_ref, keep, y, w):
    for k in range(4):
        rows = slice(k * 256, (k + 1) * 256)
        total = keep_ref[k] + g1[rows].astype(f32) + g2[rows].astype(f32) + g3[rows].astype(f32)
        if k < 2:
            keep[k] = total
        else:
            y[k - 2] = total.astype(bf16)
    own, left, across, right = (ref[1024 : 1024 + T].astype(f32) for ref in (sent_ref, g1, g2, g3))
    w[...] = (own + across) + (left + right)


def split_q(acc_ref, got_ref, keep, y):
    for dz in range(4):
        for u in range(2):
            k = 4 * dz + u
            keep[2 * dz + u] = acc_ref[k] + got_ref[k].astype(f32)
            y[2 * dz + u] = (acc_ref[k + 2] + got_ref[k + 2].astype(f32)).astype(bf16)


def gather_q(keep_ref, got_ref, keep, z1, z2, z3):
    for u in range(2):
        keep[u] = keep_ref[u] + got_ref[u].astype(f32)
        for dz, ref in ((1, z1), (2, z2), (3, z3)):
            ref[u] = (keep_ref[2 * dz + u] + got_ref[2 * dz + u].astype(f32)).astype(bf16)


def finish(p_keep, p_got, q_keep, g1, g2, g3, mask_ref, w, w_got, out_ref, weight_ref):
    upper = lax.axis_index("col") >> 2
    for pair, ref in ((upper, w), (1 - upper, w_got)):
        for i in range(2):
            rows = pl.ds(pl.multiple_of(pair * T + i * 64, 64), 64)
            weight_ref[rows, 0:T] = ref[i, 0:64]
            weight_ref[rows, T : 2 * T] = ref[i, 64:T]
    for t in range(4):
        keep, *parts = (p_keep, p_got) if t < 2 else (q_keep, g1, g2, g3)
        total = keep[t & 1]
        for got in parts:
            total += got[t & 1].astype(f32)
        rows = slice(t * T, (t + 1) * T)
        out_ref[rows] = jnp.where(mask_ref[rows] == 1, total.T, 0.0).astype(bf16)


def shards(out_grad, out_bits, agg_saved, weight, tiles, tile_coords, tile_count, in_bits):
    def over_x(v, s):
        return lax.ppermute(v, "col", [(c, (((c >> 1) + s) & 3) * 2 + (c & 1)) for c in range(8)])

    def over_y_hi(v):
        return lax.ppermute(v, "col", [(c, c ^ 1) for c in range(8)])

    def over_z(v, s):
        return lax.ppermute(v, "row", [(r, (r & 9) | ((((r >> 1) + s) & 3) << 1)) for r in range(16)])

    def swap_x(v, bit):
        return lax.ppermute(v, "col", [(c, c ^ (2 << bit)) for c in range(8)])

    def over_y_lo(v):
        return lax.ppermute(v, "row", [(r, r ^ 8) for r in range(16)])

    def over_core(v):
        return lax.ppermute(v, "row", [(r, r ^ 1) for r in range(16)])

    half, quad, square, message = (2, 256, T), (4, 256, T), (T, T), (512 + T, T)
    ha, hb, m1, m2, m3, w = call(
        prep,
        [(half, bf16)] * 2 + [(message, bf16)] * 3 + [(square, f32)],
        [ANY] * 4,
        "prep",
        limit=PREP_LIMIT,
        scratch=[
            pltpu.VMEM((512, 256), bf16),
            pltpu.VMEM((16, 512), jnp.int32),
            pltpu.VMEM((512, 256), bf16),
            pltpu.VMEM((256, 256), bf16),
            pltpu.VMEM((256, 256), f32),
            pltpu.SemaphoreType.DMA((4,)),
        ],
        flops=2 * 10**8,
    )(out_grad, out_bits.T, agg_saved, weight)

    ha_y = over_y_hi(ha)
    m3, m2, m1 = over_x(m1, 1), over_x(m2, 2), over_x(m3, 3)
    count, own_tiles, ha = tie(tile_count.reshape(1), tiles[0, 0], ha)
    (own_tiles,) = call(
        stage,
        [(own_tiles.shape, bf16)],
        [SMEM, ANY],
        "stage",
        limit=STAGE_LIMIT,
        scratch=[pltpu.SemaphoreType.DMA((8,))],
        flops=10**9,
    )(count, own_tiles)
    ha, ha_y, hb, m1, m2, m3, own_tiles, coords, count = tie(
        ha, ha_y, hb, m1, m2, m3, own_tiles, tile_coords[0, 0].T, count
    )

    a0, b0 = call(pack, [(quad, bf16), ((9, 256, T), bf16)], [VMEM] * 7, "pack", flops=10**6)(
        ha, ha_y, hb, m1, m2, m3, w
    )
    b1 = over_y_hi(b0)
    a3, a1, a2 = over_x(a0, 1), over_x(a0, -1), over_x(a0, 2)
    (steps,) = call(order_slots, [((8, N_STEP), jnp.int32)], [SMEM, VMEM], "order_slots", flops=10**7)(count, coords)
    (acc,) = call(
        early,
        [((65, 256, T), f32)],
        [SMEM] + [VMEM] * 3,
        "early",
        limit=LIMIT,
        scratch=[pltpu.VMEM((33, 256, T), bf16)],
        flops=4 * 10**9,
    )(steps, a0, b0, own_tiles)
    a0, a1, a2, a3, b0, b1, acc = tie(a0, a1, a2, a3, b0, b1, acc)

    sixteen = (16, 256, T)
    z_p, eight = (1024 + T, T), (8, 256, T)

    def own_columns(number):
        return call(
            functools.partial(late_own, number),
            [(sixteen, f32)],
            [SMEM] + [VMEM] * 3,
            "late_" + str(number),
            limit=LIMIT,
            scratch=[pltpu.VMEM((17, 256, T), f32)],
            flops=2 * 10**9,
        )(steps, hidden, own_tiles, acc)[0]

    def around_z(z1, z2, z3):
        return over_z(z1, 1), over_z(z2, 2), over_z(z3, 3)

    p_sent, q_sent, hidden = call(
        late_partner,
        [((17, 256, T), bf16), (sixteen, bf16), ((33, 256, T), bf16)],
        [SMEM] + [VMEM] * 8,
        "late_1",
        limit=LIMIT,
        scratch=[pltpu.VMEM((33, 256, T), f32)],
        flops=4 * 10**9,
    )(steps, a0, a3, a1, a2, b0, b1, own_tiles, acc)
    p_got, q_got = over_core(p_sent), over_core(q_sent)
    own = own_columns(2)
    p_keep, *p_z = call(split_p, [(quad, f32)] + [(z_p, bf16)] * 3, [VMEM] * 3, "split_p", flops=10**6)(
        own, p_got, p_sent
    )
    p_all = around_z(*p_z)
    p_keep, hidden, q_got = tie(p_keep, hidden, q_got)
    own = own_columns(3)
    q_keep, q_y = call(split_q, [(eight, f32), (eight, bf16)], [VMEM] * 2, "split_q", flops=10**6)(own, q_got)
    q_got = over_y_lo(q_y)
    p_keep, q_keep, words = tie(p_keep, q_keep, in_bits.T)
    (mask,) = call(in_mask, [((512, 256), bf16)], [VMEM], "in_mask", flops=10**7)(words)
    p_keep, p_y, w = call(
        gather_p, [(half, f32), (half, bf16), (square, f32)], [VMEM] * 5, "gather_p", flops=10**10, touched=2**25
    )(p_keep, *p_all, p_z[0])
    p_got, w_got = over_y_lo(p_y), over_y_lo(w)
    q_keep, p_keep, mask = tie(q_keep, p_keep, mask)
    q_keep, *q_z = call(gather_q, [(half, f32)] + [(half, bf16)] * 3, [VMEM] * 2, "gather_q", flops=10**6)(
        q_keep, q_got
    )
    q_all = around_z(*q_z)
    (w,) = call(add_two, [(square, f32)], [VMEM] * 2, "add_two", limit=2)(w, w_got)
    (w,) = call(pair_up, [((2, T, T), f32)], [VMEM] * 2, "pair_up", limit=2)(w, swap_x(w, 0))
    w_got = swap_x(w, 1)
    prev_grad, weight_grad = call(
        finish, [((512, 256), bf16), ((256, 256), f32)], [VMEM] * 9, "finish", flops=10**6
    )(p_keep, p_got, q_keep, *q_all, mask, w, w_got)
    return weight_grad, prev_grad


def solution(mesh):
    nodes = P(("row", "col"), None)
    return jax.shard_map(
        shards,
        mesh=mesh,
        in_specs=(nodes, nodes, nodes, P(), P("row", "col"), P("row", "col"), P("row", "col"), nodes),
        out_specs=(P(), nodes),
        check_vma=False,
    )
```

```python
import functools

import jax
import jax.numpy as jnp
from jax import lax
from jax.experimental import pallas as pl
from jax.experimental.pallas import tpu as pltpu
from jax.sharding import PartitionSpec as P

T = 128
N_STEP = 512
UNROLL = 16
LIMIT = 16
MASK_COST = 10**6
Q_COST = 10**6
P_COST = 10**10
PREP_LIMIT = 61
STAGE_LIMIT = 24
ZERO_ROW = 32
LOWEST = (0, 0, 32, 48)
bf16 = jnp.bfloat16
f32 = jnp.float32
tie = lambda *values: lax.optimization_barrier(values)
VMEM = pl.BlockSpec(memory_space=pltpu.VMEM)
ANY = pl.BlockSpec(memory_space=pl.ANY)
SMEM = pl.BlockSpec(memory_space=pltpu.SMEM)


def call(body, outs, ins, name, limit=8, scratch=(), flops=0, touched=0):
    return pl.pallas_call(
        body,
        in_specs=ins,
        out_specs=[VMEM] * len(outs),
        out_shape=[jax.ShapeDtypeStruct(s, d) for s, d in outs],
        scratch_shapes=list(scratch),
        compiler_params=pltpu.CompilerParams(vmem_limit_bytes=limit * 2**20),
        cost_estimate=pl.CostEstimate(flops=flops, bytes_accessed=touched, transcendentals=0),
        name=name,
    )


def contract(a, b, da, db):
    return lax.dot_general(a, b, (((da,), (db,)), ((), ())), preferred_element_type=f32)


def mask_of(words):
    low = (words & 255).astype(f32)
    high = ((words >> 8) & 255).astype(f32)
    pieces = jnp.concatenate([low, high], 0).astype(bf16)
    w = lax.broadcasted_iota(jnp.int32, (32, 256), 0)
    f = lax.broadcasted_iota(jnp.int32, (32, 256), 1)
    spread = ((f >> 4) + 16 * ((f >> 3) & 1) == w).astype(f32).astype(bf16)
    byte = contract(pieces, spread, 0, 0).astype(jnp.int32)
    lane = lax.broadcasted_iota(jnp.int32, byte.shape, 1)
    return ((byte >> (lane & 7)) & 1) == 1


def both_parts(value):
    high = value.astype(bf16)
    return jnp.concatenate([high, (value - high.astype(f32)).astype(bf16)], 0)


def whole(parts):
    return parts[0:T].astype(f32) + parts[T : 2 * T].astype(f32)


def prep(grad_hbm, words_hbm, agg_hbm, weight_hbm, ha, hb, m1, m2, m3, keep, grad, words, agg, weight, part, sems):
    copies = [
        pltpu.make_async_copy(src, dst, sems.at[i])
        for i, (src, dst) in enumerate(((words_hbm, words), (grad_hbm, grad), (weight_hbm, weight), (agg_hbm, agg)))
    ]
    for copy in copies:
        copy.start()
    copies[0].wait()
    mask = mask_of(words[...])
    copies[1].wait()
    masked = jnp.where(mask, grad[...], jnp.zeros((), bf16))
    copies[2].wait()
    hidden = contract(weight[...], masked, 1, 1).astype(bf16)
    for t in range(2):
        ha[t] = hidden[:, t * T : (t + 1) * T]
        hb[t] = hidden[:, (t + 2) * T : (t + 3) * T]
        for ref in (m1, m2, m3):
            ref[t * 256 : (t + 1) * 256] = hidden[:, (t + 2) * T : (t + 3) * T]
    copies[3].wait()
    part[...] = contract(agg[...], masked, 0, 0) * (1.0 / 256.0)
    x = lax.axis_index("col") >> 1

    def quarter(q):
        rows = part[pl.ds(pl.multiple_of(q * 64, 64), 64)]
        return jnp.concatenate([rows[:, 0:T], rows[:, T : 2 * T]], 0)

    keep[...] = quarter(x)
    for s, ref in ((1, m1), (2, m2), (3, m3)):
        ref[512 : 512 + T] = quarter((x + s) & 3).astype(bf16)


def pack(ha, ha_y, hb, m1, m2, m3, keep, a0, b0, w):
    a0[0:2], a0[2:4] = ha[...], ha_y[...]
    b0[0:2] = hb[...]
    total = keep[...]
    for s, ref in ((1, m1), (2, m2), (3, m3)):
        b0[2 * s], b0[2 * s + 1] = ref[0:256], ref[256:512]
        total += ref[512 : 512 + T].astype(f32)
    b0[8] = both_parts(total)
    w[...] = b0[8]


def pair_up(own, got, out):
    odd = (lax.axis_index("col") >> 1) & 1
    out[odd] = own[...]
    out[1 - odd] = got[...]


def in_mask(words_ref, out_ref):
    out_ref[...] = mask_of(words_ref[...]).astype(f32).astype(bf16)


def order_slots(count_ref, coords_ref, out_ref):
    device_row, device_col = lax.axis_index("row"), lax.axis_index("col")
    x, y_hi = device_col >> 1, device_col & 1
    y_lo, z, core = device_row >> 3, (device_row >> 1) & 3, device_row & 1
    slots = coords_ref.shape[1]
    slot = lax.broadcasted_iota(jnp.int32, (1, slots), 1)
    i, j = coords_ref[0:1, :], coords_ref[1:2, :]
    t, src = i & 3, i >> 2
    dx, dyh = ((src >> 1) - x) & 3, (src & 1) ^ y_hi
    row = jnp.where(t < 2, dx * 4 + dyh * 2 + t, 16 + dyh * 8 + dx * 2 + (t & 1))
    late = jnp.where(jnp.where(t < 2, dx, dyh) == 0, 0, 64)
    u, q = j & 3, j >> 2
    dc, dz, dy = (q & 1) ^ core ^ 1, ((q >> 1) - z) & 3, (q >> 3) ^ y_lo
    column = dc * 32 + (u >> 1) * 16 + dz * 4 + dy * 2 + (u & 1)
    key = jnp.where(slot < count_ref[0], column + late, T)
    both = jnp.concatenate([key, slot | (row << 9), column << 15, jnp.zeros((5, slots), jnp.int32)], 0).T
    key_c, word_c, high_c = both[:, 0:1], both[:, 1:2], both[:, 2:3]
    s_id = lax.broadcasted_iota(jnp.int32, (slots, slots), 0)
    t_id = lax.broadcasted_iota(jnp.int32, (slots, slots), 1)
    rank = jnp.sum(jnp.where((key == key_c) & (t_id < s_id), 1, 0), 1, keepdims=True)
    k_id = lax.broadcasted_iota(jnp.int32, (slots, T), 1)
    lane = k_id[0:1]
    held = jnp.sum(jnp.where(key_c == k_id, 1, 0), 0, keepdims=True)
    pairs = (held + 1) >> 1

    def list_of(k):
        return jnp.where(k < 64, 0, jnp.maximum((k >> 4) - 4, 1))

    start = jnp.zeros((1, 1), jnp.int32)
    starts, counts, base = (jnp.zeros((1, T), jnp.int32) for _ in range(3))
    for number in range(4):
        total = jnp.sum(jnp.where(list_of(lane) == number, pairs, 0), 1, keepdims=True)
        groups = (total + UNROLL - 1) // UNROLL
        starts = jnp.where(lane == number, start, starts)
        counts = jnp.where(lane == number, groups, counts)
        base = jnp.where(list_of(lane) == number, start * UNROLL, base)
        start = start + groups
    ahead = (k_id < key_c) & (list_of(k_id) == list_of(key_c))
    step = jnp.sum(jnp.where(ahead, pairs, 0) + jnp.where(k_id == key_c, base, 0), 1, keepdims=True) + (rank >> 1)
    step = jnp.where(key_c < T, step, -1)
    first = jnp.where((rank & 1) == 0, step, -1)
    second = jnp.where((rank & 1) == 1, step, -1)
    p_id = lax.broadcasted_iota(jnp.int32, (slots, N_STEP), 1)
    none = ZERO_ROW << 9
    none_high = 64 << 15
    out_ref[0:1, :] = (
        jnp.sum(jnp.where(first == p_id, word_c + high_c - none - none_high, 0), 0, keepdims=True) + none + none_high
    )
    out_ref[1:2, :] = jnp.sum(jnp.where(second == p_id, word_c - none, 0), 0, keepdims=True) + none
    out_ref[2:8, :] = jnp.zeros((6, N_STEP), jnp.int32)
    out_ref[2:3, 0:T] = starts
    out_ref[3:4, 0:T] = counts


def stage(count_ref, tiles_ref, out_ref, sems):
    chunk = tiles_ref.shape[0] // 8

    def copy(i):
        part = pl.ds(i * chunk, chunk)
        return pltpu.make_async_copy(tiles_ref.at[part], out_ref.at[part], sems.at[i])

    used = (count_ref[0] + chunk - 1) // chunk
    for i in range(8):
        pl.when(i < used)(lambda i=i: copy(i).start())
    for i in range(8):
        pl.when(i < used)(lambda i=i: copy(i).wait())


def products(number, steps_ref, h_ref, tiles_ref, acc_ref):
    lowest = LOWEST[number]
    spare = acc_ref.shape[0] - 1

    def some(g, carry):
        results = []
        for u in range(UNROLL):
            s = g * UNROLL + u
            a, b = steps_ref[0, s], steps_ref[1, s]
            left = jnp.concatenate([h_ref[(a >> 9) & 63], h_ref[b >> 9]], 1)
            right = jnp.concatenate([tiles_ref[a & 511], tiles_ref[b & 511]], 0)
            column = jnp.minimum((a >> 15) - lowest, spare)
            results.append((column, jnp.dot(left, right, preferred_element_type=f32)))
        for column, result in results:
            acc_ref[column] += result
        return carry

    first = steps_ref[2, number]
    lax.fori_loop(first, first + steps_ref[3, number], some, 0)


def early(steps_ref, a0, b0, tiles_ref, acc_ref, h_ref):
    h_ref[0:4], h_ref[16:24] = a0[...], b0[0:8]
    h_ref[ZERO_ROW] = jnp.zeros((256, T), bf16)

    def clear(k, carry):
        acc_ref[k] = jnp.zeros((256, T), f32)
        return carry

    lax.fori_loop(0, 65, clear, 0)
    products(0, steps_ref, h_ref, tiles_ref, acc_ref)


def late(number, steps_ref, h_ref, tiles_ref, so_far_ref, outs, acc_ref):
    base, columns = LOWEST[number], 16 * len(outs)

    def take(k, carry):
        acc_ref[k] = so_far_ref[base + k]
        return carry

    lax.fori_loop(0, columns, take, 0)
    acc_ref[columns] = jnp.zeros((256, T), f32)
    products(number, steps_ref, h_ref, tiles_ref, acc_ref)
    for i, ref in enumerate(outs):

        def give(k, carry, i=i, ref=ref):
            ref[k] = acc_ref[16 * i + k].astype(ref.dtype)
            return carry

        lax.fori_loop(0, 16, give, 0)


def late_partner(steps_ref, a0, a3, a1, a2, b0, b1, w_y, w_diagonal, tiles_ref, so_far_ref, p_ref, q_ref, h_ref, acc_ref):
    h_ref[0:4], h_ref[4:8], h_ref[8:12], h_ref[12:16] = a0[...], a1[...], a2[...], a3[...]
    h_ref[16:24], h_ref[24:32] = b0[0:8], b1[0:8]
    h_ref[ZERO_ROW] = jnp.zeros((256, T), bf16)
    p_ref[16] = both_parts((whole(b0[8]) + whole(b1[8])) + (whole(w_y[...]) + whole(w_diagonal[...])))
    late(1, steps_ref, h_ref, tiles_ref, so_far_ref, (p_ref, q_ref), acc_ref)


def late_own(number, steps_ref, h_ref, tiles_ref, so_far_ref, out_ref, acc_ref):
    late(number, steps_ref, h_ref, tiles_ref, so_far_ref, (out_ref,), acc_ref)


def split_p(acc_ref, got_ref, sent_ref, keep, z1, z2, z3):
    for k in range(4):
        keep[k] = acc_ref[k] + got_ref[k].astype(f32)
        for dz, ref in ((1, z1), (2, z2), (3, z3)):
            ref[k * 256 : (k + 1) * 256] = (acc_ref[4 * dz + k] + got_ref[4 * dz + k].astype(f32)).astype(bf16)
    total = (whole(sent_ref[16]) + whole(got_ref[16])).astype(bf16)
    for ref in (z1, z2, z3):
        ref[1024 : 1024 + T] = total


def gather_p(keep_ref, g1, g2, g3, sent_ref, keep, y, w):
    for k in range(4):
        rows = slice(k * 256, (k + 1) * 256)
        total = keep_ref[k] + g1[rows].astype(f32) + g2[rows].astype(f32) + g3[rows].astype(f32)
        if k < 2:
            keep[k] = total
        else:
            y[k - 2] = total.astype(bf16)
    own, left, across, right = (ref[1024 : 1024 + T].astype(f32) for ref in (sent_ref, g1, g2, g3))
    w[...] = (own + across) + (left + right)


def split_q(acc_ref, got_ref, keep, y):
    for dz in range(4):
        for u in range(2):
            k = 4 * dz + u
            keep[2 * dz + u] = acc_ref[k] + got_ref[k].astype(f32)
            y[2 * dz + u] = (acc_ref[k + 2] + got_ref[k + 2].astype(f32)).astype(bf16)


def gather_q(keep_ref, got_ref, keep, z1, z2, z3):
    for u in range(2):
        keep[u] = keep_ref[u] + got_ref[u].astype(f32)
        for dz, ref in ((1, z1), (2, z2), (3, z3)):
            ref[u] = (keep_ref[2 * dz + u] + got_ref[2 * dz + u].astype(f32)).astype(bf16)


def finish(p_keep, p_got, q_keep, g1, g2, g3, mask_ref, w, w_got, out_ref, weight_ref):
    upper = lax.axis_index("col") >> 2
    for pair, ref in ((upper, w), (1 - upper, w_got)):
        for i in range(2):
            rows = pl.ds(pl.multiple_of(pair * T + i * 64, 64), 64)
            weight_ref[rows, 0:T] = ref[i, 0:64]
            weight_ref[rows, T : 2 * T] = ref[i, 64:T]
    for t in range(4):
        keep, *parts = (p_keep, p_got) if t < 2 else (q_keep, g1, g2, g3)
        total = keep[t & 1]
        for got in parts:
            total += got[t & 1].astype(f32)
        rows = slice(t * T, (t + 1) * T)
        out_ref[rows] = jnp.where(mask_ref[rows] == 1, total.T, 0.0).astype(bf16)


def shards(out_grad, out_bits, agg_saved, weight, tiles, tile_coords, tile_count, in_bits):
    def over_x(v, s):
        return lax.ppermute(v, "col", [(c, (((c >> 1) + s) & 3) * 2 + (c & 1)) for c in range(8)])

    def over_y_hi(v):
        return lax.ppermute(v, "col", [(c, c ^ 1) for c in range(8)])

    def over_z(v, s):
        return lax.ppermute(v, "row", [(r, (r & 9) | ((((r >> 1) + s) & 3) << 1)) for r in range(16)])

    def swap_x(v, bit):
        return lax.ppermute(v, "col", [(c, c ^ (2 << bit)) for c in range(8)])

    def over_y_lo(v):
        return lax.ppermute(v, "row", [(r, r ^ 8) for r in range(16)])

    def over_both_y(v):
        pairs = [(r * 8 + c, (r ^ 8) * 8 + (c ^ 1)) for r in range(16) for c in range(8)]
        return lax.ppermute(v, ("row", "col"), pairs)

    def over_core(v):
        return lax.ppermute(v, "row", [(r, r ^ 1) for r in range(16)])

    half, quad, square, message = (2, 256, T), (4, 256, T), (T, T), (512 + T, T)
    ha, hb, m1, m2, m3, w = call(
        prep,
        [(half, bf16)] * 2 + [(message, bf16)] * 3 + [(square, f32)],
        [ANY] * 4,
        "prep",
        limit=PREP_LIMIT,
        scratch=[
            pltpu.VMEM((512, 256), bf16),
            pltpu.VMEM((16, 512), jnp.int32),
            pltpu.VMEM((512, 256), bf16),
            pltpu.VMEM((256, 256), bf16),
            pltpu.VMEM((256, 256), f32),
            pltpu.SemaphoreType.DMA((4,)),
        ],
        flops=2 * 10**8,
    )(out_grad, out_bits.T, agg_saved, weight)

    ha_y = over_y_hi(ha)
    m3, m2, m1 = over_x(m1, 1), over_x(m2, 2), over_x(m3, 3)
    count, own_tiles, ha = tie(tile_count.reshape(1), tiles[0, 0], ha)
    (own_tiles,) = call(
        stage,
        [(own_tiles.shape, bf16)],
        [SMEM, ANY],
        "stage",
        limit=STAGE_LIMIT,
        scratch=[pltpu.SemaphoreType.DMA((8,))],
        flops=10**9,
    )(count, own_tiles)
    ha, ha_y, hb, m1, m2, m3, own_tiles, coords, count = tie(
        ha, ha_y, hb, m1, m2, m3, own_tiles, tile_coords[0, 0].T, count
    )

    a0, b0, w = call(pack, [(quad, bf16), ((9, 256, T), bf16), ((256, T), bf16)], [VMEM] * 7, "pack", flops=10**6)(
        ha, ha_y, hb, m1, m2, m3, w
    )
    b1 = over_y_hi(b0)
    a3, a1, a2 = over_x(a0, 1), over_x(a0, -1), over_x(a0, 2)
    w_y = over_y_lo(w)
    (steps,) = call(order_slots, [((8, N_STEP), jnp.int32)], [SMEM, VMEM], "order_slots", flops=10**7)(count, coords)
    steps, w_y, w = tie(steps, w_y, w)
    w_diagonal = over_both_y(w)
    (acc,) = call(
        early,
        [((65, 256, T), f32)],
        [SMEM] + [VMEM] * 3,
        "early",
        limit=LIMIT,
        scratch=[pltpu.VMEM((33, 256, T), bf16)],
        flops=4 * 10**9,
    )(steps, a0, b0, own_tiles)
    a0, a1, a2, a3, b0, b1, w_y, w_diagonal, acc = tie(a0, a1, a2, a3, b0, b1, w_y, w_diagonal, acc)

    sixteen = (16, 256, T)
    z_p, eight = (1024 + T, T), (8, 256, T)

    def own_columns(number):
        return call(
            functools.partial(late_own, number),
            [(sixteen, f32)],
            [SMEM] + [VMEM] * 3,
            "late_" + str(number),
            limit=LIMIT,
            scratch=[pltpu.VMEM((17, 256, T), f32)],
            flops=2 * 10**9,
        )(steps, hidden, own_tiles, acc)[0]

    def around_z(z1, z2, z3):
        return over_z(z1, 1), over_z(z2, 2), over_z(z3, 3)

    p_sent, q_sent, hidden = call(
        late_partner,
        [((17, 256, T), bf16), (sixteen, bf16), ((33, 256, T), bf16)],
        [SMEM] + [VMEM] * 10,
        "late_1",
        limit=LIMIT,
        scratch=[pltpu.VMEM((33, 256, T), f32)],
        flops=4 * 10**9,
    )(steps, a0, a3, a1, a2, b0, b1, w_y, w_diagonal, own_tiles, acc)
    p_got, q_got = over_core(p_sent), over_core(q_sent)
    own = own_columns(3)
    q_keep, q_y = call(split_q, [(eight, f32), (eight, bf16)], [VMEM] * 2, "split_q", flops=10**6)(own, q_got)
    q_got = over_y_lo(q_y)
    q_keep, hidden, p_got = tie(q_keep, hidden, p_got)
    own = own_columns(2)
    p_keep, *p_z = call(split_p, [(quad, f32)] + [(z_p, bf16)] * 3, [VMEM] * 3, "split_p", flops=10**6)(
        own, p_got, p_sent
    )
    p_all = around_z(*p_z)
    p_keep, q_keep, words = tie(p_keep, q_keep, in_bits.T)
    (mask,) = call(in_mask, [((512, 256), bf16)], [VMEM], "in_mask", flops=MASK_COST)(words)
    q_keep, *q_z = call(gather_q, [(half, f32)] + [(half, bf16)] * 3, [VMEM] * 2, "gather_q", flops=Q_COST)(
        q_keep, q_got
    )
    q_all = list(around_z(*q_z))
    p_keep, q_keep, mask, q_all[0], q_all[2] = tie(p_keep, q_keep, mask, q_all[0], q_all[2])
    p_keep, p_y, w = call(
        gather_p, [(half, f32), (half, bf16), (square, f32)], [VMEM] * 5, "gather_p", flops=P_COST
    )(p_keep, *p_all, p_z[0])
    p_got = over_y_lo(p_y)
    (w,) = call(pair_up, [((2, T, T), f32)], [VMEM] * 2, "pair_up", limit=2)(w, swap_x(w, 0))
    w_got = swap_x(w, 1)
    prev_grad, weight_grad = call(
        finish, [((512, 256), bf16), ((256, 256), f32)], [VMEM] * 9, "finish", flops=10**6
    )(p_keep, p_got, q_keep, *q_all, mask, w, w_got)
    return weight_grad, prev_grad


def solution(mesh):
    nodes = P(("row", "col"), None)
    return jax.shard_map(
        shards,
        mesh=mesh,
        in_specs=(nodes, nodes, nodes, P(), P("row", "col"), P("row", "col"), P("row", "col"), nodes),
        out_specs=(P(), nodes),
        check_vma=False,
    )
```

```python
import functools

import jax
import jax.numpy as jnp
from jax import lax
from jax.experimental import pallas as pl
from jax.experimental.pallas import tpu as pltpu
from jax.sharding import PartitionSpec as P

T = 128
N_STEP = 512
UNROLL = 16
LIMIT = 16
PREP_LIMIT = 61
STAGE_LIMIT = 24
ZERO_ROW = 32
LOWEST = (0, 0, 32, 48)
bf16 = jnp.bfloat16
f32 = jnp.float32
tie = lambda *values: lax.optimization_barrier(values)
VMEM = pl.BlockSpec(memory_space=pltpu.VMEM)
ANY = pl.BlockSpec(memory_space=pl.ANY)
SMEM = pl.BlockSpec(memory_space=pltpu.SMEM)


def call(body, outs, ins, name, limit=8, scratch=(), flops=0, touched=0):
    return pl.pallas_call(
        body,
        in_specs=ins,
        out_specs=[VMEM] * len(outs),
        out_shape=[jax.ShapeDtypeStruct(s, d) for s, d in outs],
        scratch_shapes=list(scratch),
        compiler_params=pltpu.CompilerParams(vmem_limit_bytes=limit * 2**20),
        cost_estimate=pl.CostEstimate(flops=flops, bytes_accessed=touched, transcendentals=0),
        name=name,
    )


def contract(a, b, da, db):
    return lax.dot_general(a, b, (((da,), (db,)), ((), ())), preferred_element_type=f32)


def mask_of(words):
    low = (words & 255).astype(f32)
    high = ((words >> 8) & 255).astype(f32)
    pieces = jnp.concatenate([low, high], 0).astype(bf16)
    w = lax.broadcasted_iota(jnp.int32, (32, 256), 0)
    f = lax.broadcasted_iota(jnp.int32, (32, 256), 1)
    spread = ((f >> 4) + 16 * ((f >> 3) & 1) == w).astype(f32).astype(bf16)
    byte = contract(pieces, spread, 0, 0).astype(jnp.int32)
    lane = lax.broadcasted_iota(jnp.int32, byte.shape, 1)
    return ((byte >> (lane & 7)) & 1) == 1


def both_parts(value):
    high = value.astype(bf16)
    return jnp.concatenate([high, (value - high.astype(f32)).astype(bf16)], 0)


def whole(parts):
    return parts[0:T].astype(f32) + parts[T : 2 * T].astype(f32)


def prep(grad_hbm, words_hbm, agg_hbm, weight_hbm, ha, hb, m1, m2, m3, keep, grad, words, agg, weight, part, sems):
    copies = [
        pltpu.make_async_copy(src, dst, sems.at[i])
        for i, (src, dst) in enumerate(((words_hbm, words), (grad_hbm, grad), (weight_hbm, weight), (agg_hbm, agg)))
    ]
    for copy in copies:
        copy.start()
    copies[0].wait()
    mask = mask_of(words[...])
    copies[1].wait()
    masked = jnp.where(mask, grad[...], jnp.zeros((), bf16))
    copies[2].wait()
    hidden = contract(weight[...], masked, 1, 1).astype(bf16)
    for t in range(2):
        ha[t] = hidden[:, t * T : (t + 1) * T]
        hb[t] = hidden[:, (t + 2) * T : (t + 3) * T]
        for ref in (m1, m2, m3):
            ref[t * 256 : (t + 1) * 256] = hidden[:, (t + 2) * T : (t + 3) * T]
    copies[3].wait()
    part[...] = contract(agg[...], masked, 0, 0) * (1.0 / 256.0)
    x = lax.axis_index("col") >> 1

    def quarter(q):
        rows = part[pl.ds(pl.multiple_of(q * 64, 64), 64)]
        return jnp.concatenate([rows[:, 0:T], rows[:, T : 2 * T]], 0)

    keep[...] = quarter(x)
    for s, ref in ((1, m1), (2, m2), (3, m3)):
        ref[512 : 512 + T] = quarter((x + s) & 3).astype(bf16)


def pack(ha, ha_y, hb, m1, m2, m3, keep, a0, b0):
    a0[0:2], a0[2:4] = ha[...], ha_y[...]
    b0[0:2] = hb[...]
    total = keep[...]
    for s, ref in ((1, m1), (2, m2), (3, m3)):
        b0[2 * s], b0[2 * s + 1] = ref[0:256], ref[256:512]
        total += ref[512 : 512 + T].astype(f32)
    b0[8] = both_parts(total)


def add_two(a, b, out):
    out[...] = a[...] + b[...]


def pair_up(own, got, out):
    odd = (lax.axis_index("col") >> 1) & 1
    out[odd] = own[...]
    out[1 - odd] = got[...]


def in_mask(words_ref, out_ref):
    out_ref[...] = mask_of(words_ref[...]).astype(f32).astype(bf16)


def order_slots(count_ref, coords_ref, out_ref):
    device_row, device_col = lax.axis_index("row"), lax.axis_index("col")
    x, y_hi = device_col >> 1, device_col & 1
    y_lo, z, core = device_row >> 3, (device_row >> 1) & 3, device_row & 1
    slots = coords_ref.shape[1]
    slot = lax.broadcasted_iota(jnp.int32, (1, slots), 1)
    i, j = coords_ref[0:1, :], coords_ref[1:2, :]
    t, src = i & 3, i >> 2
    dx, dyh = ((src >> 1) - x) & 3, (src & 1) ^ y_hi
    row = jnp.where(t < 2, dx * 4 + dyh * 2 + t, 16 + dyh * 8 + dx * 2 + (t & 1))
    late = jnp.where(jnp.where(t < 2, dx, dyh) == 0, 0, 64)
    u, q = j & 3, j >> 2
    dc, dz, dy = (q & 1) ^ core ^ 1, ((q >> 1) - z) & 3, (q >> 3) ^ y_lo
    column = dc * 32 + (u >> 1) * 16 + dz * 4 + dy * 2 + (u & 1)
    key = jnp.where(slot < count_ref[0], column + late, T)
    both = jnp.concatenate([key, slot | (row << 9), column << 15, jnp.zeros((5, slots), jnp.int32)], 0).T
    key_c, word_c, high_c = both[:, 0:1], both[:, 1:2], both[:, 2:3]
    s_id = lax.broadcasted_iota(jnp.int32, (slots, slots), 0)
    t_id = lax.broadcasted_iota(jnp.int32, (slots, slots), 1)
    rank = jnp.sum(jnp.where((key == key_c) & (t_id < s_id), 1, 0), 1, keepdims=True)
    k_id = lax.broadcasted_iota(jnp.int32, (slots, T), 1)
    lane = k_id[0:1]
    held = jnp.sum(jnp.where(key_c == k_id, 1, 0), 0, keepdims=True)
    pairs = (held + 1) >> 1

    def list_of(k):
        return jnp.where(k < 64, 0, jnp.maximum((k >> 4) - 4, 1))

    start = jnp.zeros((1, 1), jnp.int32)
    starts, counts, base = (jnp.zeros((1, T), jnp.int32) for _ in range(3))
    for number in range(4):
        total = jnp.sum(jnp.where(list_of(lane) == number, pairs, 0), 1, keepdims=True)
        groups = (total + UNROLL - 1) // UNROLL
        starts = jnp.where(lane == number, start, starts)
        counts = jnp.where(lane == number, groups, counts)
        base = jnp.where(list_of(lane) == number, start * UNROLL, base)
        start = start + groups
    ahead = (k_id < key_c) & (list_of(k_id) == list_of(key_c))
    step = jnp.sum(jnp.where(ahead, pairs, 0) + jnp.where(k_id == key_c, base, 0), 1, keepdims=True) + (rank >> 1)
    step = jnp.where(key_c < T, step, -1)
    first = jnp.where((rank & 1) == 0, step, -1)
    second = jnp.where((rank & 1) == 1, step, -1)
    p_id = lax.broadcasted_iota(jnp.int32, (slots, N_STEP), 1)
    none = ZERO_ROW << 9
    none_high = 64 << 15
    out_ref[0:1, :] = (
        jnp.sum(jnp.where(first == p_id, word_c + high_c - none - none_high, 0), 0, keepdims=True) + none + none_high
    )
    out_ref[1:2, :] = jnp.sum(jnp.where(second == p_id, word_c - none, 0), 0, keepdims=True) + none
    out_ref[2:8, :] = jnp.zeros((6, N_STEP), jnp.int32)
    out_ref[2:3, 0:T] = starts
    out_ref[3:4, 0:T] = counts


def stage(count_ref, tiles_ref, out_ref, sems):
    chunk = tiles_ref.shape[0] // 8

    def copy(i):
        part = pl.ds(i * chunk, chunk)
        return pltpu.make_async_copy(tiles_ref.at[part], out_ref.at[part], sems.at[i])

    used = (count_ref[0] + chunk - 1) // chunk
    for i in range(8):
        pl.when(i < used)(lambda i=i: copy(i).start())
    for i in range(8):
        pl.when(i < used)(lambda i=i: copy(i).wait())


def products(number, steps_ref, h_ref, tiles_ref, acc_ref):
    lowest = LOWEST[number]
    spare = acc_ref.shape[0] - 1

    def some(g, carry):
        results = []
        for u in range(UNROLL):
            s = g * UNROLL + u
            a, b = steps_ref[0, s], steps_ref[1, s]
            left = jnp.concatenate([h_ref[(a >> 9) & 63], h_ref[b >> 9]], 1)
            right = jnp.concatenate([tiles_ref[a & 511], tiles_ref[b & 511]], 0)
            column = jnp.minimum((a >> 15) - lowest, spare)
            results.append((column, jnp.dot(left, right, preferred_element_type=f32)))
        for column, result in results:
            acc_ref[column] += result
        return carry

    first = steps_ref[2, number]
    lax.fori_loop(first, first + steps_ref[3, number], some, 0)


def early(steps_ref, a0, b0, tiles_ref, acc_ref, h_ref):
    h_ref[0:4], h_ref[16:24] = a0[...], b0[0:8]
    h_ref[ZERO_ROW] = jnp.zeros((256, T), bf16)

    def clear(k, carry):
        acc_ref[k] = jnp.zeros((256, T), f32)
        return carry

    lax.fori_loop(0, 65, clear, 0)
    products(0, steps_ref, h_ref, tiles_ref, acc_ref)


def late(number, steps_ref, h_ref, tiles_ref, so_far_ref, outs, acc_ref):
    base, columns = LOWEST[number], 16 * len(outs)

    def take(k, carry):
        acc_ref[k] = so_far_ref[base + k]
        return carry

    lax.fori_loop(0, columns, take, 0)
    acc_ref[columns] = jnp.zeros((256, T), f32)
    products(number, steps_ref, h_ref, tiles_ref, acc_ref)
    for i, ref in enumerate(outs):

        def give(k, carry, i=i, ref=ref):
            ref[k] = acc_ref[16 * i + k].astype(ref.dtype)
            return carry

        lax.fori_loop(0, 16, give, 0)


def late_partner(steps_ref, a0, a3, a1, a2, b0, b1, tiles_ref, so_far_ref, p_ref, q_ref, h_ref, acc_ref):
    h_ref[0:4], h_ref[4:8], h_ref[8:12], h_ref[12:16] = a0[...], a1[...], a2[...], a3[...]
    h_ref[16:24], h_ref[24:32] = b0[0:8], b1[0:8]
    h_ref[ZERO_ROW] = jnp.zeros((256, T), bf16)
    p_ref[16] = both_parts(whole(b0[8]) + whole(b1[8]))
    late(1, steps_ref, h_ref, tiles_ref, so_far_ref, (p_ref, q_ref), acc_ref)


def late_own(number, steps_ref, h_ref, tiles_ref, so_far_ref, out_ref, acc_ref):
    late(number, steps_ref, h_ref, tiles_ref, so_far_ref, (out_ref,), acc_ref)


def split_p(acc_ref, got_ref, sent_ref, keep, z1, z2, z3):
    for k in range(4):
        keep[k] = acc_ref[k] + got_ref[k].astype(f32)
        for dz, ref in ((1, z1), (2, z2), (3, z3)):
            ref[k * 256 : (k + 1) * 256] = (acc_ref[4 * dz + k] + got_ref[4 * dz + k].astype(f32)).astype(bf16)
    total = (whole(sent_ref[16]) + whole(got_ref[16])).astype(bf16)
    for ref in (z1, z2, z3):
        ref[1024 : 1024 + T] = total


def gather_p(keep_ref, g1, g2, g3, sent_ref, keep, y, w):
    for k in range(4):
        rows = slice(k * 256, (k + 1) * 256)
        total = keep_ref[k] + g1[rows].astype(f32) + g2[rows].astype(f32) + g3[rows].astype(f32)
        if k < 2:
            keep[k] = total
        else:
            y[k - 2] = total.astype(bf16)
    own, left, across, right = (ref[1024 : 1024 + T].astype(f32) for ref in (sent_ref, g1, g2, g3))
    w[...] = (own + across) + (left + right)


def split_q(acc_ref, got_ref, keep, y):
    for dz in range(4):
        for u in range(2):
            k = 4 * dz + u
            keep[2 * dz + u] = acc_ref[k] + got_ref[k].astype(f32)
            y[2 * dz + u] = (acc_ref[k + 2] + got_ref[k + 2].astype(f32)).astype(bf16)


def gather_q(keep_ref, got_ref, keep, z1, z2, z3):
    for u in range(2):
        keep[u] = keep_ref[u] + got_ref[u].astype(f32)
        for dz, ref in ((1, z1), (2, z2), (3, z3)):
            ref[u] = (keep_ref[2 * dz + u] + got_ref[2 * dz + u].astype(f32)).astype(bf16)


def finish(p_keep, p_got, q_keep, g1, g2, g3, mask_ref, w, w_got, out_ref, weight_ref):
    upper = lax.axis_index("col") >> 2
    for pair, ref in ((upper, w), (1 - upper, w_got)):
        for i in range(2):
            rows = pl.ds(pl.multiple_of(pair * T + i * 64, 64), 64)
            weight_ref[rows, 0:T] = ref[i, 0:64]
            weight_ref[rows, T : 2 * T] = ref[i, 64:T]
    for t in range(4):
        keep, *parts = (p_keep, p_got) if t < 2 else (q_keep, g1, g2, g3)
        total = keep[t & 1]
        for got in parts:
            total += got[t & 1].astype(f32)
        rows = slice(t * T, (t + 1) * T)
        out_ref[rows] = jnp.where(mask_ref[rows] == 1, total.T, 0.0).astype(bf16)


def shards(out_grad, out_bits, agg_saved, weight, tiles, tile_coords, tile_count, in_bits):
    def over_x(v, s):
        return lax.ppermute(v, "col", [(c, (((c >> 1) + s) & 3) * 2 + (c & 1)) for c in range(8)])

    def over_y_hi(v):
        return lax.ppermute(v, "col", [(c, c ^ 1) for c in range(8)])

    def over_z(v, s):
        return lax.ppermute(v, "row", [(r, (r & 9) | ((((r >> 1) + s) & 3) << 1)) for r in range(16)])

    def swap_x(v, bit):
        return lax.ppermute(v, "col", [(c, c ^ (2 << bit)) for c in range(8)])

    def over_y_lo(v):
        return lax.ppermute(v, "row", [(r, r ^ 8) for r in range(16)])

    def over_core(v):
        return lax.ppermute(v, "row", [(r, r ^ 1) for r in range(16)])

    half, quad, square, message = (2, 256, T), (4, 256, T), (T, T), (512 + T, T)
    ha, hb, m1, m2, m3, w = call(
        prep,
        [(half, bf16)] * 2 + [(message, bf16)] * 3 + [(square, f32)],
        [ANY] * 4,
        "prep",
        limit=PREP_LIMIT,
        scratch=[
            pltpu.VMEM((512, 256), bf16),
            pltpu.VMEM((16, 512), jnp.int32),
            pltpu.VMEM((512, 256), bf16),
            pltpu.VMEM((256, 256), bf16),
            pltpu.VMEM((256, 256), f32),
            pltpu.SemaphoreType.DMA((4,)),
        ],
        flops=2 * 10**8,
    )(out_grad, out_bits.T, agg_saved, weight)

    ha_y = over_y_hi(ha)
    m3, m2, m1 = over_x(m1, 1), over_x(m2, 2), over_x(m3, 3)
    count, own_tiles, ha = tie(tile_count.reshape(1), tiles[0, 0], ha)
    (own_tiles,) = call(
        stage,
        [(own_tiles.shape, bf16)],
        [SMEM, ANY],
        "stage",
        limit=STAGE_LIMIT,
        scratch=[pltpu.SemaphoreType.DMA((8,))],
        flops=10**9,
    )(count, own_tiles)
    ha, ha_y, hb, m1, m2, m3, own_tiles, coords, count = tie(
        ha, ha_y, hb, m1, m2, m3, own_tiles, tile_coords[0, 0].T, count
    )

    a0, b0 = call(pack, [(quad, bf16), ((9, 256, T), bf16)], [VMEM] * 7, "pack", flops=10**6)(
        ha, ha_y, hb, m1, m2, m3, w
    )
    b1 = over_y_hi(b0)
    a3, a1, a2 = over_x(a0, 1), over_x(a0, -1), over_x(a0, 2)
    (steps,) = call(order_slots, [((8, N_STEP), jnp.int32)], [SMEM, VMEM], "order_slots", flops=10**7)(count, coords)
    (acc,) = call(
        early,
        [((65, 256, T), f32)],
        [SMEM] + [VMEM] * 3,
        "early",
        limit=LIMIT,
        scratch=[pltpu.VMEM((33, 256, T), bf16)],
        flops=4 * 10**9,
    )(steps, a0, b0, own_tiles)
    a0, a1, a2, a3, b0, b1, acc = tie(a0, a1, a2, a3, b0, b1, acc)

    sixteen = (16, 256, T)
    z_p, eight = (1024 + T, T), (8, 256, T)

    def own_columns(number):
        return call(
            functools.partial(late_own, number),
            [(sixteen, f32)],
            [SMEM] + [VMEM] * 3,
            "late_" + str(number),
            limit=LIMIT,
            scratch=[pltpu.VMEM((17, 256, T), f32)],
            flops=2 * 10**9,
        )(steps, hidden, own_tiles, acc)[0]

    def around_z(z1, z2, z3):
        return over_z(z1, 1), over_z(z2, 2), over_z(z3, 3)

    p_sent, q_sent, hidden = call(
        late_partner,
        [((17, 256, T), bf16), (sixteen, bf16), ((33, 256, T), bf16)],
        [SMEM] + [VMEM] * 8,
        "late_1",
        limit=LIMIT,
        scratch=[pltpu.VMEM((33, 256, T), f32)],
        flops=4 * 10**9,
    )(steps, a0, a3, a1, a2, b0, b1, own_tiles, acc)
    p_got, q_got = over_core(p_sent), over_core(q_sent)
    own = own_columns(2)
    p_keep, *p_z = call(split_p, [(quad, f32)] + [(z_p, bf16)] * 3, [VMEM] * 3, "split_p", flops=10**6)(
        own, p_got, p_sent
    )
    p_all = around_z(*p_z)
    p_keep, hidden, q_got = tie(p_keep, hidden, q_got)
    own = own_columns(3)
    q_keep, q_y = call(split_q, [(eight, f32), (eight, bf16)], [VMEM] * 2, "split_q", flops=10**6)(own, q_got)
    q_got = over_y_lo(q_y)
    p_keep, q_keep, words = tie(p_keep, q_keep, in_bits.T)
    (mask,) = call(in_mask, [((512, 256), bf16)], [VMEM], "in_mask", flops=10**7)(words)
    p_keep, p_y, w = call(
        gather_p, [(half, f32), (half, bf16), (square, f32)], [VMEM] * 5, "gather_p", flops=10**10, touched=2**25
    )(p_keep, *p_all, p_z[0])
    p_got, w_got = over_y_lo(p_y), over_y_lo(w)
    q_keep, p_keep, mask = tie(q_keep, p_keep, mask)
    q_keep, *q_z = call(gather_q, [(half, f32)] + [(half, bf16)] * 3, [VMEM] * 2, "gather_q", flops=10**6)(
        q_keep, q_got
    )
    q_keep, w, w_got = tie(q_keep, w, w_got)
    q_all = around_z(*q_z)
    (w,) = call(add_two, [(square, f32)], [VMEM] * 2, "add_two", limit=2)(w, w_got)
    (w,) = call(pair_up, [((2, T, T), f32)], [VMEM] * 2, "pair_up", limit=2)(w, swap_x(w, 0))
    w_got = swap_x(w, 1)
    prev_grad, weight_grad = call(
        finish, [((512, 256), bf16), ((256, 256), f32)], [VMEM] * 9, "finish", flops=10**6
    )(p_keep, p_got, q_keep, *q_all, mask, w, w_got)
    return weight_grad, prev_grad


def solution(mesh):
    nodes = P(("row", "col"), None)
    return jax.shard_map(
        shards,
        mesh=mesh,
        in_specs=(nodes, nodes, nodes, P(), P("row", "col"), P("row", "col"), P("row", "col"), nodes),
        out_specs=(P(), nodes),
        check_vma=False,
    )
```

```python
import functools

import jax
import jax.numpy as jnp
from jax import lax
from jax.experimental import pallas as pl
from jax.experimental.pallas import tpu as pltpu
from jax.sharding import PartitionSpec as P

T = 128
N_STEP = 512
UNROLL = 16
LIMIT = 16
PREP_LIMIT = 61
STAGE_LIMIT = 24
ZERO_ROW = 32
LOWEST = (0, 0, 32, 48)
bf16 = jnp.bfloat16
f32 = jnp.float32
tie = lambda *values: lax.optimization_barrier(values)
VMEM = pl.BlockSpec(memory_space=pltpu.VMEM)
ANY = pl.BlockSpec(memory_space=pl.ANY)
SMEM = pl.BlockSpec(memory_space=pltpu.SMEM)


def call(body, outs, ins, name, limit=8, scratch=(), flops=0, touched=0):
    return pl.pallas_call(
        body,
        in_specs=ins,
        out_specs=[VMEM] * len(outs),
        out_shape=[jax.ShapeDtypeStruct(s, d) for s, d in outs],
        scratch_shapes=list(scratch),
        compiler_params=pltpu.CompilerParams(vmem_limit_bytes=limit * 2**20),
        cost_estimate=pl.CostEstimate(flops=flops, bytes_accessed=touched, transcendentals=0),
        name=name,
    )


def contract(a, b, da, db):
    return lax.dot_general(a, b, (((da,), (db,)), ((), ())), preferred_element_type=f32)


def mask_of(words):
    low = (words & 255).astype(f32)
    high = ((words >> 8) & 255).astype(f32)
    pieces = jnp.concatenate([low, high], 0).astype(bf16)
    w = lax.broadcasted_iota(jnp.int32, (32, 256), 0)
    f = lax.broadcasted_iota(jnp.int32, (32, 256), 1)
    spread = ((f >> 4) + 16 * ((f >> 3) & 1) == w).astype(f32).astype(bf16)
    byte = contract(pieces, spread, 0, 0).astype(jnp.int32)
    lane = lax.broadcasted_iota(jnp.int32, byte.shape, 1)
    return ((byte >> (lane & 7)) & 1) == 1


def both_parts(value):
    high = value.astype(bf16)
    return jnp.concatenate([high, (value - high.astype(f32)).astype(bf16)], 0)


def whole(parts):
    return parts[0:T].astype(f32) + parts[T : 2 * T].astype(f32)


def prep(grad_hbm, words_hbm, agg_hbm, weight_hbm, ha, hb, m1, m2, m3, keep, grad, words, agg, weight, part, sems):
    copies = [
        pltpu.make_async_copy(src, dst, sems.at[i])
        for i, (src, dst) in enumerate(((words_hbm, words), (grad_hbm, grad), (weight_hbm, weight), (agg_hbm, agg)))
    ]
    for copy in copies:
        copy.start()
    copies[0].wait()
    mask = mask_of(words[...])
    copies[1].wait()
    masked = jnp.where(mask, grad[...], jnp.zeros((), bf16))
    copies[2].wait()
    hidden = contract(weight[...], masked, 1, 1).astype(bf16)
    for t in range(2):
        ha[t] = hidden[:, t * T : (t + 1) * T]
        hb[t] = hidden[:, (t + 2) * T : (t + 3) * T]
        for ref in (m1, m2, m3):
            ref[t * 256 : (t + 1) * 256] = hidden[:, (t + 2) * T : (t + 3) * T]
    copies[3].wait()
    part[...] = contract(agg[...], masked, 0, 0) * (1.0 / 256.0)
    x = lax.axis_index("col") >> 1

    def quarter(q):
        rows = part[pl.ds(pl.multiple_of(q * 64, 64), 64)]
        return jnp.concatenate([rows[:, 0:T], rows[:, T : 2 * T]], 0)

    keep[...] = quarter(x)
    for s, ref in ((1, m1), (2, m2), (3, m3)):
        ref[512 : 512 + T] = quarter((x + s) & 3).astype(bf16)


def pack(ha, ha_y, hb, m1, m2, m3, keep, a0, b0):
    a0[0:2], a0[2:4] = ha[...], ha_y[...]
    b0[0:2] = hb[...]
    total = keep[...]
    for s, ref in ((1, m1), (2, m2), (3, m3)):
        b0[2 * s], b0[2 * s + 1] = ref[0:256], ref[256:512]
        total += ref[512 : 512 + T].astype(f32)
    b0[8] = both_parts(total)


def pair_up(y, own, got, message):
    odd = (lax.axis_index("col") >> 1) & 1
    message[0:2] = y[...]
    message[2, pl.ds(pl.multiple_of(odd * T, T), T)] = own[...].astype(bf16)
    message[2, pl.ds(pl.multiple_of((1 - odd) * T, T), T)] = got[...].astype(bf16)


def sum_pair(own, got, out):
    for i in range(2):
        rows = slice(i * T, (i + 1) * T)
        out[i] = own[2, rows].astype(f32) + got[2, rows].astype(f32)


def in_mask(words_ref, out_ref):
    out_ref[...] = mask_of(words_ref[...]).astype(f32).astype(bf16)


def order_slots(count_ref, coords_ref, out_ref):
    device_row, device_col = lax.axis_index("row"), lax.axis_index("col")
    x, y_hi = device_col >> 1, device_col & 1
    y_lo, z, core = device_row >> 3, (device_row >> 1) & 3, device_row & 1
    slots = coords_ref.shape[1]
    slot = lax.broadcasted_iota(jnp.int32, (1, slots), 1)
    i, j = coords_ref[0:1, :], coords_ref[1:2, :]
    t, src = i & 3, i >> 2
    dx, dyh = ((src >> 1) - x) & 3, (src & 1) ^ y_hi
    row = jnp.where(t < 2, dx * 4 + dyh * 2 + t, 16 + dyh * 8 + dx * 2 + (t & 1))
    late = jnp.where(jnp.where(t < 2, dx, dyh) == 0, 0, 64)
    u, q = j & 3, j >> 2
    dc, dz, dy = (q & 1) ^ core ^ 1, ((q >> 1) - z) & 3, (q >> 3) ^ y_lo
    column = dc * 32 + (u >> 1) * 16 + dz * 4 + dy * 2 + (u & 1)
    key = jnp.where(slot < count_ref[0], column + late, T)
    both = jnp.concatenate([key, slot | (row << 9), column << 15, jnp.zeros((5, slots), jnp.int32)], 0).T
    key_c, word_c, high_c = both[:, 0:1], both[:, 1:2], both[:, 2:3]
    s_id = lax.broadcasted_iota(jnp.int32, (slots, slots), 0)
    t_id = lax.broadcasted_iota(jnp.int32, (slots, slots), 1)
    rank = jnp.sum(jnp.where((key == key_c) & (t_id < s_id), 1, 0), 1, keepdims=True)
    k_id = lax.broadcasted_iota(jnp.int32, (slots, T), 1)
    lane = k_id[0:1]
    held = jnp.sum(jnp.where(key_c == k_id, 1, 0), 0, keepdims=True)
    pairs = (held + 1) >> 1

    def list_of(k):
        return jnp.where(k < 64, 0, jnp.maximum((k >> 4) - 4, 1))

    start = jnp.zeros((1, 1), jnp.int32)
    starts, counts, base = (jnp.zeros((1, T), jnp.int32) for _ in range(3))
    for number in range(4):
        total = jnp.sum(jnp.where(list_of(lane) == number, pairs, 0), 1, keepdims=True)
        groups = (total + UNROLL - 1) // UNROLL
        starts = jnp.where(lane == number, start, starts)
        counts = jnp.where(lane == number, groups, counts)
        base = jnp.where(list_of(lane) == number, start * UNROLL, base)
        start = start + groups
    ahead = (k_id < key_c) & (list_of(k_id) == list_of(key_c))
    step = jnp.sum(jnp.where(ahead, pairs, 0) + jnp.where(k_id == key_c, base, 0), 1, keepdims=True) + (rank >> 1)
    step = jnp.where(key_c < T, step, -1)
    first = jnp.where((rank & 1) == 0, step, -1)
    second = jnp.where((rank & 1) == 1, step, -1)
    p_id = lax.broadcasted_iota(jnp.int32, (slots, N_STEP), 1)
    none = ZERO_ROW << 9
    none_high = 64 << 15
    out_ref[0:1, :] = (
        jnp.sum(jnp.where(first == p_id, word_c + high_c - none - none_high, 0), 0, keepdims=True) + none + none_high
    )
    out_ref[1:2, :] = jnp.sum(jnp.where(second == p_id, word_c - none, 0), 0, keepdims=True) + none
    out_ref[2:8, :] = jnp.zeros((6, N_STEP), jnp.int32)
    out_ref[2:3, 0:T] = starts
    out_ref[3:4, 0:T] = counts


def stage(count_ref, tiles_ref, out_ref, sems):
    chunk = tiles_ref.shape[0] // 8

    def copy(i):
        part = pl.ds(i * chunk, chunk)
        return pltpu.make_async_copy(tiles_ref.at[part], out_ref.at[part], sems.at[i])

    used = (count_ref[0] + chunk - 1) // chunk
    for i in range(8):
        pl.when(i < used)(lambda i=i: copy(i).start())
    for i in range(8):
        pl.when(i < used)(lambda i=i: copy(i).wait())


def products(number, steps_ref, h_ref, tiles_ref, acc_ref):
    lowest = LOWEST[number]
    spare = acc_ref.shape[0] - 1

    def some(g, carry):
        results = []
        for u in range(UNROLL):
            s = g * UNROLL + u
            a, b = steps_ref[0, s], steps_ref[1, s]
            left = jnp.concatenate([h_ref[(a >> 9) & 63], h_ref[b >> 9]], 1)
            right = jnp.concatenate([tiles_ref[a & 511], tiles_ref[b & 511]], 0)
            column = jnp.minimum((a >> 15) - lowest, spare)
            results.append((column, jnp.dot(left, right, preferred_element_type=f32)))
        for column, result in results:
            acc_ref[column] += result
        return carry

    first = steps_ref[2, number]
    lax.fori_loop(first, first + steps_ref[3, number], some, 0)


def early(steps_ref, a0, b0, tiles_ref, acc_ref, h_ref):
    h_ref[0:4], h_ref[16:24] = a0[...], b0[0:8]
    h_ref[ZERO_ROW] = jnp.zeros((256, T), bf16)

    def clear(k, carry):
        acc_ref[k] = jnp.zeros((256, T), f32)
        return carry

    lax.fori_loop(0, 65, clear, 0)
    products(0, steps_ref, h_ref, tiles_ref, acc_ref)


def late(number, steps_ref, h_ref, tiles_ref, so_far_ref, outs, acc_ref):
    base, columns = LOWEST[number], 16 * len(outs)

    def take(k, carry):
        acc_ref[k] = so_far_ref[base + k]
        return carry

    lax.fori_loop(0, columns, take, 0)
    acc_ref[columns] = jnp.zeros((256, T), f32)
    products(number, steps_ref, h_ref, tiles_ref, acc_ref)
    for i, ref in enumerate(outs):

        def give(k, carry, i=i, ref=ref):
            ref[k] = acc_ref[16 * i + k].astype(ref.dtype)
            return carry

        lax.fori_loop(0, 16, give, 0)


def late_partner(steps_ref, a0, a3, a1, a2, b0, b1, tiles_ref, so_far_ref, p_ref, q_ref, h_ref, acc_ref):
    h_ref[0:4], h_ref[4:8], h_ref[8:12], h_ref[12:16] = a0[...], a1[...], a2[...], a3[...]
    h_ref[16:24], h_ref[24:32] = b0[0:8], b1[0:8]
    h_ref[ZERO_ROW] = jnp.zeros((256, T), bf16)
    p_ref[16] = both_parts(whole(b0[8]) + whole(b1[8]))
    late(1, steps_ref, h_ref, tiles_ref, so_far_ref, (p_ref, q_ref), acc_ref)


def late_own(number, steps_ref, h_ref, tiles_ref, so_far_ref, out_ref, acc_ref):
    late(number, steps_ref, h_ref, tiles_ref, so_far_ref, (out_ref,), acc_ref)


def split_p(acc_ref, got_ref, sent_ref, keep, z1, z2, z3):
    for k in range(4):
        keep[k] = acc_ref[k] + got_ref[k].astype(f32)
        for dz, ref in ((1, z1), (2, z2), (3, z3)):
            ref[k * 256 : (k + 1) * 256] = (acc_ref[4 * dz + k] + got_ref[4 * dz + k].astype(f32)).astype(bf16)
    total = (whole(sent_ref[16]) + whole(got_ref[16])).astype(bf16)
    for ref in (z1, z2, z3):
        ref[1024 : 1024 + T] = total


def gather_p(keep_ref, g1, g2, g3, sent_ref, keep, y, w):
    for k in range(4):
        rows = slice(k * 256, (k + 1) * 256)
        total = keep_ref[k] + g1[rows].astype(f32) + g2[rows].astype(f32) + g3[rows].astype(f32)
        if k < 2:
            keep[k] = total
        else:
            y[k - 2] = total.astype(bf16)
    own, left, across, right = (ref[1024 : 1024 + T].astype(f32) for ref in (sent_ref, g1, g2, g3))
    w[...] = (own + across) + (left + right)


def split_q(acc_ref, got_ref, keep, y):
    for dz in range(4):
        for u in range(2):
            k = 4 * dz + u
            keep[2 * dz + u] = acc_ref[k] + got_ref[k].astype(f32)
            y[2 * dz + u] = (acc_ref[k + 2] + got_ref[k + 2].astype(f32)).astype(bf16)


def gather_q(keep_ref, got_ref, keep, z1, z2, z3):
    for u in range(2):
        keep[u] = keep_ref[u] + got_ref[u].astype(f32)
        for dz, ref in ((1, z1), (2, z2), (3, z3)):
            ref[u] = (keep_ref[2 * dz + u] + got_ref[2 * dz + u].astype(f32)).astype(bf16)


def finish(p_keep, p_got, q_keep, g1, g2, g3, mask_ref, w, w_got, out_ref, weight_ref):
    upper = lax.axis_index("col") >> 2
    for pair, ref in ((upper, w), (1 - upper, w_got)):
        for i in range(2):
            rows = pl.ds(pl.multiple_of(pair * T + i * 64, 64), 64)
            weight_ref[rows, 0:T] = ref[i, 0:64]
            weight_ref[rows, T : 2 * T] = ref[i, 64:T]
    for t in range(4):
        keep, *parts = (p_keep, p_got) if t < 2 else (q_keep, g1, g2, g3)
        total = keep[t & 1]
        for got in parts:
            total += got[t & 1].astype(f32)
        rows = slice(t * T, (t + 1) * T)
        out_ref[rows] = jnp.where(mask_ref[rows] == 1, total.T, 0.0).astype(bf16)


def shards(out_grad, out_bits, agg_saved, weight, tiles, tile_coords, tile_count, in_bits):
    def over_x(v, s):
        return lax.ppermute(v, "col", [(c, (((c >> 1) + s) & 3) * 2 + (c & 1)) for c in range(8)])

    def over_y_hi(v):
        return lax.ppermute(v, "col", [(c, c ^ 1) for c in range(8)])

    def over_z(v, s):
        return lax.ppermute(v, "row", [(r, (r & 9) | ((((r >> 1) + s) & 3) << 1)) for r in range(16)])

    def swap_x(v, bit):
        return lax.ppermute(v, "col", [(c, c ^ (2 << bit)) for c in range(8)])

    def over_y_lo(v):
        return lax.ppermute(v, "row", [(r, r ^ 8) for r in range(16)])

    def over_core(v):
        return lax.ppermute(v, "row", [(r, r ^ 1) for r in range(16)])

    half, quad, square, message = (2, 256, T), (4, 256, T), (T, T), (512 + T, T)
    ha, hb, m1, m2, m3, w = call(
        prep,
        [(half, bf16)] * 2 + [(message, bf16)] * 3 + [(square, f32)],
        [ANY] * 4,
        "prep",
        limit=PREP_LIMIT,
        scratch=[
            pltpu.VMEM((512, 256), bf16),
            pltpu.VMEM((16, 512), jnp.int32),
            pltpu.VMEM((512, 256), bf16),
            pltpu.VMEM((256, 256), bf16),
            pltpu.VMEM((256, 256), f32),
            pltpu.SemaphoreType.DMA((4,)),
        ],
        flops=2 * 10**8,
    )(out_grad, out_bits.T, agg_saved, weight)

    ha_y = over_y_hi(ha)
    m3, m2, m1 = over_x(m1, 1), over_x(m2, 2), over_x(m3, 3)
    count, own_tiles, ha = tie(tile_count.reshape(1), tiles[0, 0], ha)
    (own_tiles,) = call(
        stage,
        [(own_tiles.shape, bf16)],
        [SMEM, ANY],
        "stage",
        limit=STAGE_LIMIT,
        scratch=[pltpu.SemaphoreType.DMA((8,))],
        flops=10**9,
    )(count, own_tiles)
    ha, ha_y, hb, m1, m2, m3, own_tiles, coords, count = tie(
        ha, ha_y, hb, m1, m2, m3, own_tiles, tile_coords[0, 0].T, count
    )

    a0, b0 = call(pack, [(quad, bf16), ((9, 256, T), bf16)], [VMEM] * 7, "pack", flops=10**6)(
        ha, ha_y, hb, m1, m2, m3, w
    )
    b1 = over_y_hi(b0)
    a3, a1, a2 = over_x(a0, 1), over_x(a0, -1), over_x(a0, 2)
    (steps,) = call(order_slots, [((8, N_STEP), jnp.int32)], [SMEM, VMEM], "order_slots", flops=10**7)(count, coords)
    (acc,) = call(
        early,
        [((65, 256, T), f32)],
        [SMEM] + [VMEM] * 3,
        "early",
        limit=LIMIT,
        scratch=[pltpu.VMEM((33, 256, T), bf16)],
        flops=4 * 10**9,
    )(steps, a0, b0, own_tiles)
    a0, a1, a2, a3, b0, b1, acc = tie(a0, a1, a2, a3, b0, b1, acc)

    sixteen = (16, 256, T)
    z_p, eight = (1024 + T, T), (8, 256, T)

    def own_columns(number):
        return call(
            functools.partial(late_own, number),
            [(sixteen, f32)],
            [SMEM] + [VMEM] * 3,
            "late_" + str(number),
            limit=LIMIT,
            scratch=[pltpu.VMEM((17, 256, T), f32)],
            flops=2 * 10**9,
        )(steps, hidden, own_tiles, acc)[0]

    def around_z(z1, z2, z3):
        return over_z(z1, 1), over_z(z2, 2), over_z(z3, 3)

    p_sent, q_sent, hidden = call(
        late_partner,
        [((17, 256, T), bf16), (sixteen, bf16), ((33, 256, T), bf16)],
        [SMEM] + [VMEM] * 8,
        "late_1",
        limit=LIMIT,
        scratch=[pltpu.VMEM((33, 256, T), f32)],
        flops=4 * 10**9,
    )(steps, a0, a3, a1, a2, b0, b1, own_tiles, acc)
    p_got, q_got = over_core(p_sent), over_core(q_sent)
    own = own_columns(2)
    p_keep, *p_z = call(split_p, [(quad, f32)] + [(z_p, bf16)] * 3, [VMEM] * 3, "split_p", flops=10**6)(
        own, p_got, p_sent
    )
    p_all = around_z(*p_z)
    p_keep, hidden, q_got = tie(p_keep, hidden, q_got)
    own = own_columns(3)
    q_keep, q_y = call(split_q, [(eight, f32), (eight, bf16)], [VMEM] * 2, "split_q", flops=10**6)(own, q_got)
    q_got = over_y_lo(q_y)
    p_keep, q_keep, words = tie(p_keep, q_keep, in_bits.T)
    (mask,) = call(in_mask, [((512, 256), bf16)], [VMEM], "in_mask", flops=10**7)(words)
    p_keep, p_y, w = call(
        gather_p, [(half, f32), (half, bf16), (square, f32)], [VMEM] * 5, "gather_p", flops=10**10, touched=2**25
    )(p_keep, *p_all, p_z[0])
    w_got = swap_x(w, 0)
    q_keep, p_keep, mask = tie(q_keep, p_keep, mask)
    q_keep, *q_z = call(gather_q, [(half, f32)] + [(half, bf16)] * 3, [VMEM] * 2, "gather_q", flops=10**6)(
        q_keep, q_got
    )
    (p_y,) = call(pair_up, [((3, 256, T), bf16)], [VMEM] * 3, "pair_up", limit=4)(p_y, w, w_got)
    p_got = over_y_lo(p_y)
    q_all = around_z(*q_z)
    (w,) = call(sum_pair, [((2, T, T), f32)], [VMEM] * 2, "sum_pair", limit=4)(p_y, p_got)
    w_got = swap_x(w, 1)
    prev_grad, weight_grad = call(
        finish, [((512, 256), bf16), ((256, 256), f32)], [VMEM] * 9, "finish", flops=10**6
    )(p_keep, p_got, q_keep, *q_all, mask, w, w_got)
    return weight_grad, prev_grad


def solution(mesh):
    nodes = P(("row", "col"), None)
    return jax.shard_map(
        shards,
        mesh=mesh,
        in_specs=(nodes, nodes, nodes, P(), P("row", "col"), P("row", "col"), P("row", "col"), nodes),
        out_specs=(P(), nodes),
        check_vma=False,
    )
```

```python
import functools

import jax
import jax.numpy as jnp
from jax import lax
from jax.experimental import pallas as pl
from jax.experimental.pallas import tpu as pltpu
from jax.sharding import PartitionSpec as P

T = 128
N_STEP = 512
UNROLL = 16
LIMIT = 16
PREP_LIMIT = 61
STAGE_LIMIT = 24
ZERO_ROW = 32
LOWEST = (0, 0, 32, 48)
bf16 = jnp.bfloat16
f32 = jnp.float32
tie = lambda *values: lax.optimization_barrier(values)
VMEM = pl.BlockSpec(memory_space=pltpu.VMEM)
ANY = pl.BlockSpec(memory_space=pl.ANY)
SMEM = pl.BlockSpec(memory_space=pltpu.SMEM)


def call(body, outs, ins, name, limit=8, scratch=(), flops=0, touched=0):
    return pl.pallas_call(
        body,
        in_specs=ins,
        out_specs=[VMEM] * len(outs),
        out_shape=[jax.ShapeDtypeStruct(s, d) for s, d in outs],
        scratch_shapes=list(scratch),
        compiler_params=pltpu.CompilerParams(vmem_limit_bytes=limit * 2**20),
        cost_estimate=pl.CostEstimate(flops=flops, bytes_accessed=touched, transcendentals=0),
        name=name,
    )


def contract(a, b, da, db):
    return lax.dot_general(a, b, (((da,), (db,)), ((), ())), preferred_element_type=f32)


def mask_of(words):
    low = (words & 255).astype(f32)
    high = ((words >> 8) & 255).astype(f32)
    pieces = jnp.concatenate([low, high], 0).astype(bf16)
    w = lax.broadcasted_iota(jnp.int32, (32, 256), 0)
    f = lax.broadcasted_iota(jnp.int32, (32, 256), 1)
    spread = ((f >> 4) + 16 * ((f >> 3) & 1) == w).astype(f32).astype(bf16)
    byte = contract(pieces, spread, 0, 0).astype(jnp.int32)
    lane = lax.broadcasted_iota(jnp.int32, byte.shape, 1)
    return ((byte >> (lane & 7)) & 1) == 1


def both_parts(value):
    high = value.astype(bf16)
    return jnp.concatenate([high, (value - high.astype(f32)).astype(bf16)], 0)


def whole(parts):
    return parts[0:T].astype(f32) + parts[T : 2 * T].astype(f32)


def prep(grad_hbm, words_hbm, agg_hbm, weight_hbm, ha, hb, m1, m2, m3, keep, grad, words, agg, weight, part, sems):
    copies = [
        pltpu.make_async_copy(src, dst, sems.at[i])
        for i, (src, dst) in enumerate(((words_hbm, words), (grad_hbm, grad), (weight_hbm, weight), (agg_hbm, agg)))
    ]
    for copy in copies:
        copy.start()
    copies[0].wait()
    mask = mask_of(words[...])
    copies[1].wait()
    masked = jnp.where(mask, grad[...], jnp.zeros((), bf16))
    copies[2].wait()
    hidden = contract(weight[...], masked, 1, 1).astype(bf16)
    for t in range(2):
        ha[t] = hidden[:, t * T : (t + 1) * T]
        hb[t] = hidden[:, (t + 2) * T : (t + 3) * T]
        for ref in (m1, m2, m3):
            ref[t * 256 : (t + 1) * 256] = hidden[:, (t + 2) * T : (t + 3) * T]
    copies[3].wait()
    part[...] = contract(agg[...], masked, 0, 0) * (1.0 / 256.0)
    x = lax.axis_index("col") >> 1

    def quarter(q):
        rows = part[pl.ds(pl.multiple_of(q * 64, 64), 64)]
        return jnp.concatenate([rows[:, 0:T], rows[:, T : 2 * T]], 0)

    keep[...] = quarter(x)
    for s, ref in ((1, m1), (2, m2), (3, m3)):
        ref[512 : 512 + T] = quarter((x + s) & 3).astype(bf16)


def pack(ha, ha_y, hb, m1, m2, m3, keep, a0, b0):
    a0[0:2], a0[2:4] = ha[...], ha_y[...]
    b0[0:2] = hb[...]
    total = keep[...]
    for s, ref in ((1, m1), (2, m2), (3, m3)):
        b0[2 * s], b0[2 * s + 1] = ref[0:256], ref[256:512]
        total += ref[512 : 512 + T].astype(f32)
    b0[8] = both_parts(total)


def add_two(a, b, out):
    out[...] = a[...] + b[...]


def pair_up(own, got, out):
    odd = (lax.axis_index("col") >> 1) & 1
    out[odd] = own[...]
    out[1 - odd] = got[...]


def in_mask(words_ref, out_ref):
    out_ref[...] = mask_of(words_ref[...]).astype(f32).astype(bf16)


def order_slots(count_ref, coords_ref, out_ref):
    device_row, device_col = lax.axis_index("row"), lax.axis_index("col")
    x, y_hi = device_col >> 1, device_col & 1
    y_lo, z, core = device_row >> 3, (device_row >> 1) & 3, device_row & 1
    slots = coords_ref.shape[1]
    slot = lax.broadcasted_iota(jnp.int32, (1, slots), 1)
    i, j = coords_ref[0:1, :], coords_ref[1:2, :]
    t, src = i & 3, i >> 2
    dx, dyh = ((src >> 1) - x) & 3, (src & 1) ^ y_hi
    row = jnp.where(t < 2, dx * 4 + dyh * 2 + t, 16 + dyh * 8 + dx * 2 + (t & 1))
    late = jnp.where(jnp.where(t < 2, dx, dyh) == 0, 0, 64)
    u, q = j & 3, j >> 2
    dc, dz, dy = (q & 1) ^ core ^ 1, ((q >> 1) - z) & 3, (q >> 3) ^ y_lo
    column = dc * 32 + (u >> 1) * 16 + dz * 4 + dy * 2 + (u & 1)
    key = jnp.where(slot < count_ref[0], column + late, T)
    both = jnp.concatenate([key, slot | (row << 9), column << 15, jnp.zeros((5, slots), jnp.int32)], 0).T
    key_c, word_c, high_c = both[:, 0:1], both[:, 1:2], both[:, 2:3]
    s_id = lax.broadcasted_iota(jnp.int32, (slots, slots), 0)
    t_id = lax.broadcasted_iota(jnp.int32, (slots, slots), 1)
    rank = jnp.sum(jnp.where((key == key_c) & (t_id < s_id), 1, 0), 1, keepdims=True)
    k_id = lax.broadcasted_iota(jnp.int32, (slots, T), 1)
    lane = k_id[0:1]
    held = jnp.sum(jnp.where(key_c == k_id, 1, 0), 0, keepdims=True)
    pairs = (held + 1) >> 1

    def list_of(k):
        return jnp.where(k < 64, 0, jnp.maximum((k >> 4) - 4, 1))

    start = jnp.zeros((1, 1), jnp.int32)
    starts, counts, base = (jnp.zeros((1, T), jnp.int32) for _ in range(3))
    for number in range(4):
        total = jnp.sum(jnp.where(list_of(lane) == number, pairs, 0), 1, keepdims=True)
        groups = (total + UNROLL - 1) // UNROLL
        starts = jnp.where(lane == number, start, starts)
        counts = jnp.where(lane == number, groups, counts)
        base = jnp.where(list_of(lane) == number, start * UNROLL, base)
        start = start + groups
    ahead = (k_id < key_c) & (list_of(k_id) == list_of(key_c))
    step = jnp.sum(jnp.where(ahead, pairs, 0) + jnp.where(k_id == key_c, base, 0), 1, keepdims=True) + (rank >> 1)
    step = jnp.where(key_c < T, step, -1)
    first = jnp.where((rank & 1) == 0, step, -1)
    second = jnp.where((rank & 1) == 1, step, -1)
    p_id = lax.broadcasted_iota(jnp.int32, (slots, N_STEP), 1)
    none = ZERO_ROW << 9
    none_high = 64 << 15
    out_ref[0:1, :] = (
        jnp.sum(jnp.where(first == p_id, word_c + high_c - none - none_high, 0), 0, keepdims=True) + none + none_high
    )
    out_ref[1:2, :] = jnp.sum(jnp.where(second == p_id, word_c - none, 0), 0, keepdims=True) + none
    out_ref[2:8, :] = jnp.zeros((6, N_STEP), jnp.int32)
    out_ref[2:3, 0:T] = starts
    out_ref[3:4, 0:T] = counts


def stage(count_ref, tiles_ref, out_ref, sems):
    chunk = tiles_ref.shape[0] // 8

    def copy(i):
        part = pl.ds(i * chunk, chunk)
        return pltpu.make_async_copy(tiles_ref.at[part], out_ref.at[part], sems.at[i])

    used = (count_ref[0] + chunk - 1) // chunk
    for i in range(8):
        pl.when(i < used)(lambda i=i: copy(i).start())
    for i in range(8):
        pl.when(i < used)(lambda i=i: copy(i).wait())


def products(number, steps_ref, h_ref, tiles_ref, acc_ref):
    lowest = LOWEST[number]
    spare = acc_ref.shape[0] - 1

    def some(g, carry):
        results = []
        for u in range(UNROLL):
            s = g * UNROLL + u
            a, b = steps_ref[0, s], steps_ref[1, s]
            left = jnp.concatenate([h_ref[(a >> 9) & 63], h_ref[b >> 9]], 1)
            right = jnp.concatenate([tiles_ref[a & 511], tiles_ref[b & 511]], 0)
            column = jnp.minimum((a >> 15) - lowest, spare)
            results.append((column, jnp.dot(left, right, preferred_element_type=f32)))
        for column, result in results:
            acc_ref[column] += result
        return carry

    first = steps_ref[2, number]
    lax.fori_loop(first, first + steps_ref[3, number], some, 0)


def early(steps_ref, a0, b0, tiles_ref, acc_ref, h_ref):
    h_ref[0:4], h_ref[16:24] = a0[...], b0[0:8]
    h_ref[ZERO_ROW] = jnp.zeros((256, T), bf16)

    def clear(k, carry):
        acc_ref[k] = jnp.zeros((256, T), f32)
        return carry

    lax.fori_loop(0, 65, clear, 0)
    products(0, steps_ref, h_ref, tiles_ref, acc_ref)


def late(number, steps_ref, h_ref, tiles_ref, so_far_ref, outs, acc_ref):
    base, columns = LOWEST[number], 16 * len(outs)

    def take(k, carry):
        acc_ref[k] = so_far_ref[base + k]
        return carry

    lax.fori_loop(0, columns, take, 0)
    acc_ref[columns] = jnp.zeros((256, T), f32)
    products(number, steps_ref, h_ref, tiles_ref, acc_ref)
    for i, ref in enumerate(outs):

        def give(k, carry, i=i, ref=ref):
            ref[k] = acc_ref[16 * i + k].astype(ref.dtype)
            return carry

        lax.fori_loop(0, 16, give, 0)


def late_partner(steps_ref, a0, a3, a1, a2, b0, b1, tiles_ref, so_far_ref, p_ref, q_ref, h_ref, acc_ref):
    h_ref[0:4], h_ref[4:8], h_ref[8:12], h_ref[12:16] = a0[...], a1[...], a2[...], a3[...]
    h_ref[16:24], h_ref[24:32] = b0[0:8], b1[0:8]
    h_ref[ZERO_ROW] = jnp.zeros((256, T), bf16)
    p_ref[16] = both_parts(whole(b0[8]) + whole(b1[8]))
    late(1, steps_ref, h_ref, tiles_ref, so_far_ref, (p_ref, q_ref), acc_ref)


def late_own(number, steps_ref, h_ref, tiles_ref, so_far_ref, out_ref, acc_ref):
    late(number, steps_ref, h_ref, tiles_ref, so_far_ref, (out_ref,), acc_ref)


def split_p(acc_ref, got_ref, sent_ref, keep, z1, z2, z3):
    for k in range(4):
        keep[k] = acc_ref[k] + got_ref[k].astype(f32)
        for dz, ref in ((1, z1), (2, z2), (3, z3)):
            ref[k * 256 : (k + 1) * 256] = (acc_ref[4 * dz + k] + got_ref[4 * dz + k].astype(f32)).astype(bf16)
    total = (whole(sent_ref[16]) + whole(got_ref[16])).astype(bf16)
    for ref in (z1, z2, z3):
        ref[1024 : 1024 + T] = total


def gather_p(keep_ref, g1, g2, g3, sent_ref, keep, y, w):
    for k in range(4):
        rows = slice(k * 256, (k + 1) * 256)
        total = keep_ref[k] + g1[rows].astype(f32) + g2[rows].astype(f32) + g3[rows].astype(f32)
        if k < 2:
            keep[k] = total
        else:
            y[k - 2] = total.astype(bf16)
    own, left, across, right = (ref[1024 : 1024 + T].astype(f32) for ref in (sent_ref, g1, g2, g3))
    w[...] = (own + across) + (left + right)


def split_q(acc_ref, got_ref, keep, y):
    for dz in range(4):
        for u in range(2):
            k = 4 * dz + u
            keep[2 * dz + u] = acc_ref[k] + got_ref[k].astype(f32)
            y[2 * dz + u] = (acc_ref[k + 2] + got_ref[k + 2].astype(f32)).astype(bf16)


def gather_q(keep_ref, got_ref, keep, z1, z2, z3):
    for u in range(2):
        keep[u] = keep_ref[u] + got_ref[u].astype(f32)
        for dz, ref in ((1, z1), (2, z2), (3, z3)):
            ref[u] = (keep_ref[2 * dz + u] + got_ref[2 * dz + u].astype(f32)).astype(bf16)


def finish(p_keep, p_got, q_keep, g1, g2, g3, mask_ref, w, w_got, out_ref, weight_ref):
    upper = lax.axis_index("col") >> 2
    for pair, ref in ((upper, w), (1 - upper, w_got)):
        for i in range(2):
            rows = pl.ds(pl.multiple_of(pair * T + i * 64, 64), 64)
            weight_ref[rows, 0:T] = ref[i, 0:64]
            weight_ref[rows, T : 2 * T] = ref[i, 64:T]
    for t in range(4):
        keep, *parts = (p_keep, p_got) if t < 2 else (q_keep, g1, g2, g3)
        total = keep[t & 1]
        for got in parts:
            total += got[t & 1].astype(f32)
        rows = slice(t * T, (t + 1) * T)
        out_ref[rows] = jnp.where(mask_ref[rows] == 1, total.T, 0.0).astype(bf16)


def shards(out_grad, out_bits, agg_saved, weight, tiles, tile_coords, tile_count, in_bits):
    def over_x(v, s):
        return lax.ppermute(v, "col", [(c, (((c >> 1) + s) & 3) * 2 + (c & 1)) for c in range(8)])

    def over_y_hi(v):
        return lax.ppermute(v, "col", [(c, c ^ 1) for c in range(8)])

    def over_z(v, s):
        return lax.ppermute(v, "row", [(r, (r & 9) | ((((r >> 1) + s) & 3) << 1)) for r in range(16)])

    def swap_x(v, bit):
        return lax.ppermute(v, "col", [(c, c ^ (2 << bit)) for c in range(8)])

    def over_y_lo(v):
        return lax.ppermute(v, "row", [(r, r ^ 8) for r in range(16)])

    def over_core(v):
        return lax.ppermute(v, "row", [(r, r ^ 1) for r in range(16)])

    half, quad, square, message = (2, 256, T), (4, 256, T), (T, T), (512 + T, T)
    ha, hb, m1, m2, m3, w = call(
        prep,
        [(half, bf16)] * 2 + [(message, bf16)] * 3 + [(square, f32)],
        [ANY] * 4,
        "prep",
        limit=PREP_LIMIT,
        scratch=[
            pltpu.VMEM((512, 256), bf16),
            pltpu.VMEM((16, 512), jnp.int32),
            pltpu.VMEM((512, 256), bf16),
            pltpu.VMEM((256, 256), bf16),
            pltpu.VMEM((256, 256), f32),
            pltpu.SemaphoreType.DMA((4,)),
        ],
        flops=2 * 10**8,
    )(out_grad, out_bits.T, agg_saved, weight)

    ha_y = over_y_hi(ha)
    m3, m2, m1 = over_x(m1, 1), over_x(m2, 2), over_x(m3, 3)
    count, own_tiles, ha = tie(tile_count.reshape(1), tiles[0, 0], ha)
    (own_tiles,) = call(
        stage,
        [(own_tiles.shape, bf16)],
        [SMEM, ANY],
        "stage",
        limit=STAGE_LIMIT,
        scratch=[pltpu.SemaphoreType.DMA((8,))],
        flops=10**9,
    )(count, own_tiles)
    ha, ha_y, hb, m1, m2, m3, own_tiles, coords, count = tie(
        ha, ha_y, hb, m1, m2, m3, own_tiles, tile_coords[0, 0].T, count
    )

    a0, b0 = call(pack, [(quad, bf16), ((9, 256, T), bf16)], [VMEM] * 7, "pack", flops=10**6)(
        ha, ha_y, hb, m1, m2, m3, w
    )
    b1 = over_y_hi(b0)
    a3, a1, a2 = over_x(a0, 1), over_x(a0, -1), over_x(a0, 2)
    (steps,) = call(order_slots, [((8, N_STEP), jnp.int32)], [SMEM, VMEM], "order_slots", flops=10**7)(count, coords)
    (acc,) = call(
        early,
        [((65, 256, T), f32)],
        [SMEM] + [VMEM] * 3,
        "early",
        limit=LIMIT,
        scratch=[pltpu.VMEM((33, 256, T), bf16)],
        flops=4 * 10**9,
    )(steps, a0, b0, own_tiles)
    a0, a1, a2, a3, b0, b1, acc = tie(a0, a1, a2, a3, b0, b1, acc)

    sixteen = (16, 256, T)
    z_p, eight = (1024 + T, T), (8, 256, T)

    def own_columns(number):
        return call(
            functools.partial(late_own, number),
            [(sixteen, f32)],
            [SMEM] + [VMEM] * 3,
            "late_" + str(number),
            limit=LIMIT,
            scratch=[pltpu.VMEM((17, 256, T), f32)],
            flops=2 * 10**9,
        )(steps, hidden, own_tiles, acc)[0]

    def around_z(z1, z2, z3):
        return over_z(z1, 1), over_z(z2, 2), over_z(z3, 3)

    p_sent, q_sent, hidden = call(
        late_partner,
        [((17, 256, T), bf16), (sixteen, bf16), ((33, 256, T), bf16)],
        [SMEM] + [VMEM] * 8,
        "late_1",
        limit=LIMIT,
        scratch=[pltpu.VMEM((33, 256, T), f32)],
        flops=4 * 10**9,
    )(steps, a0, a3, a1, a2, b0, b1, own_tiles, acc)
    p_got, q_got = over_core(p_sent), over_core(q_sent)
    own = own_columns(2)
    p_keep, *p_z = call(split_p, [(quad, f32)] + [(z_p, bf16)] * 3, [VMEM] * 3, "split_p", flops=10**6)(
        own, p_got, p_sent
    )
    p_all = around_z(*p_z)
    p_keep, hidden, q_got = tie(p_keep, hidden, q_got)
    own = own_columns(3)
    q_keep, q_y = call(split_q, [(eight, f32), (eight, bf16)], [VMEM] * 2, "split_q", flops=10**6)(own, q_got)
    q_got = over_y_lo(q_y)
    p_keep, q_keep, words = tie(p_keep, q_keep, in_bits.T)
    (mask,) = call(in_mask, [((512, 256), bf16)], [VMEM], "in_mask", flops=10**7)(words)
    p_keep, p_y, w = call(
        gather_p, [(half, f32), (half, bf16), (square, f32)], [VMEM] * 5, "gather_p", flops=10**10, touched=2**25
    )(p_keep, *p_all, p_z[0])
    p_got, w_got = over_y_lo(p_y), over_y_lo(w)
    q_keep, p_keep, mask = tie(q_keep, p_keep, mask)
    q_keep, *q_z = call(gather_q, [(half, f32)] + [(half, bf16)] * 3, [VMEM] * 2, "gather_q", flops=10**6)(
        q_keep, q_got
    )
    q_keep, w, w_got = tie(q_keep, w, w_got)
    q_all = around_z(*q_z)
    (w,) = call(add_two, [(square, f32)], [VMEM] * 2, "add_two", limit=2)(w, w_got)
    w_got = swap_x(w, 0)
    q_all = list(q_all)
    w, w_got, q_all[0], q_all[1] = tie(w, w_got, q_all[0], q_all[1])
    (w,) = call(pair_up, [((2, T, T), f32)], [VMEM] * 2, "pair_up", limit=2)(w, w_got)
    w_got = swap_x(w, 1)
    prev_grad, weight_grad = call(
        finish, [((512, 256), bf16), ((256, 256), f32)], [VMEM] * 9, "finish", flops=10**6
    )(p_keep, p_got, q_keep, *q_all, mask, w, w_got)
    return weight_grad, prev_grad


def solution(mesh):
    nodes = P(("row", "col"), None)
    return jax.shard_map(
        shards,
        mesh=mesh,
        in_specs=(nodes, nodes, nodes, P(), P("row", "col"), P("row", "col"), P("row", "col"), nodes),
        out_specs=(P(), nodes),
        check_vma=False,
    )
```

```python
import functools

import jax
import jax.numpy as jnp
from jax import lax
from jax.experimental import pallas as pl
from jax.experimental.pallas import tpu as pltpu
from jax.sharding import PartitionSpec as P

T = 128
N_STEP = 512
UNROLL = 16
LIMIT = 16
PREP_LIMIT = 61
STAGE_LIMIT = 24
ZERO_ROW = 32
LOWEST = (0, 0, 32, 48)
bf16 = jnp.bfloat16
f32 = jnp.float32
tie = lambda *values: lax.optimization_barrier(values)
VMEM = pl.BlockSpec(memory_space=pltpu.VMEM)
ANY = pl.BlockSpec(memory_space=pl.ANY)
SMEM = pl.BlockSpec(memory_space=pltpu.SMEM)


def call(body, outs, ins, name, limit=8, scratch=(), flops=0, touched=0):
    return pl.pallas_call(
        body,
        in_specs=ins,
        out_specs=[VMEM] * len(outs),
        out_shape=[jax.ShapeDtypeStruct(s, d) for s, d in outs],
        scratch_shapes=list(scratch),
        compiler_params=pltpu.CompilerParams(vmem_limit_bytes=limit * 2**20),
        cost_estimate=pl.CostEstimate(flops=flops, bytes_accessed=touched, transcendentals=0),
        name=name,
    )


def contract(a, b, da, db):
    return lax.dot_general(a, b, (((da,), (db,)), ((), ())), preferred_element_type=f32)


def mask_of(words):
    low = (words & 255).astype(f32)
    high = ((words >> 8) & 255).astype(f32)
    pieces = jnp.concatenate([low, high], 0).astype(bf16)
    w = lax.broadcasted_iota(jnp.int32, (32, 256), 0)
    f = lax.broadcasted_iota(jnp.int32, (32, 256), 1)
    spread = ((f >> 4) + 16 * ((f >> 3) & 1) == w).astype(f32).astype(bf16)
    byte = contract(pieces, spread, 0, 0).astype(jnp.int32)
    lane = lax.broadcasted_iota(jnp.int32, byte.shape, 1)
    return ((byte >> (lane & 7)) & 1) == 1


def both_parts(value):
    high = value.astype(bf16)
    return jnp.concatenate([high, (value - high.astype(f32)).astype(bf16)], 0)


def whole(parts):
    return parts[0:T].astype(f32) + parts[T : 2 * T].astype(f32)


def prep(grad_hbm, words_hbm, agg_hbm, weight_hbm, ha, hb, m1, m2, m3, keep, grad, words, agg, weight, part, sems):
    copies = [
        pltpu.make_async_copy(src, dst, sems.at[i])
        for i, (src, dst) in enumerate(((words_hbm, words), (grad_hbm, grad), (weight_hbm, weight), (agg_hbm, agg)))
    ]
    for copy in copies:
        copy.start()
    copies[0].wait()
    mask = mask_of(words[...])
    copies[1].wait()
    masked = jnp.where(mask, grad[...], jnp.zeros((), bf16))
    copies[2].wait()
    hidden = contract(weight[...], masked, 1, 1).astype(bf16)
    for t in range(2):
        ha[t] = hidden[:, t * T : (t + 1) * T]
        hb[t] = hidden[:, (t + 2) * T : (t + 3) * T]
        for ref in (m1, m2, m3):
            ref[t * 256 : (t + 1) * 256] = hidden[:, (t + 2) * T : (t + 3) * T]
    copies[3].wait()
    part[...] = contract(agg[...], masked, 0, 0) * (1.0 / 256.0)
    x = lax.axis_index("col") >> 1

    def quarter(q):
        rows = part[pl.ds(pl.multiple_of(q * 64, 64), 64)]
        return jnp.concatenate([rows[:, 0:T], rows[:, T : 2 * T]], 0)

    keep[...] = quarter(x)
    for s, ref in ((1, m1), (2, m2), (3, m3)):
        ref[512 : 512 + T] = quarter((x + s) & 3).astype(bf16)


def pack(ha, ha_y, hb, m1, m2, m3, keep, a0, b0):
    a0[0:2], a0[2:4] = ha[...], ha_y[...]
    b0[0:2] = hb[...]
    total = keep[...]
    for s, ref in ((1, m1), (2, m2), (3, m3)):
        b0[2 * s], b0[2 * s + 1] = ref[0:256], ref[256:512]
        total += ref[512 : 512 + T].astype(f32)
    b0[8] = both_parts(total)


def add_two(a, b, out):
    out[...] = a[...] + b[...]


def pair_up(own, got, out):
    upper = lax.axis_index("col") >> 2
    out[upper] = own[...]
    out[1 - upper] = got[...]


def in_mask(words_ref, out_ref):
    out_ref[...] = mask_of(words_ref[...]).astype(f32).astype(bf16)


def order_slots(count_ref, coords_ref, out_ref):
    device_row, device_col = lax.axis_index("row"), lax.axis_index("col")
    x, y_hi = device_col >> 1, device_col & 1
    y_lo, z, core = device_row >> 3, (device_row >> 1) & 3, device_row & 1
    slots = coords_ref.shape[1]
    slot = lax.broadcasted_iota(jnp.int32, (1, slots), 1)
    i, j = coords_ref[0:1, :], coords_ref[1:2, :]
    t, src = i & 3, i >> 2
    dx, dyh = ((src >> 1) - x) & 3, (src & 1) ^ y_hi
    row = jnp.where(t < 2, dx * 4 + dyh * 2 + t, 16 + dyh * 8 + dx * 2 + (t & 1))
    late = jnp.where(jnp.where(t < 2, dx, dyh) == 0, 0, 64)
    u, q = j & 3, j >> 2
    dc, dz, dy = (q & 1) ^ core ^ 1, ((q >> 1) - z) & 3, (q >> 3) ^ y_lo
    column = dc * 32 + (u >> 1) * 16 + dz * 4 + dy * 2 + (u & 1)
    key = jnp.where(slot < count_ref[0], column + late, T)
    both = jnp.concatenate([key, slot | (row << 9), column << 15, jnp.zeros((5, slots), jnp.int32)], 0).T
    key_c, word_c, high_c = both[:, 0:1], both[:, 1:2], both[:, 2:3]
    s_id = lax.broadcasted_iota(jnp.int32, (slots, slots), 0)
    t_id = lax.broadcasted_iota(jnp.int32, (slots, slots), 1)
    rank = jnp.sum(jnp.where((key == key_c) & (t_id < s_id), 1, 0), 1, keepdims=True)
    k_id = lax.broadcasted_iota(jnp.int32, (slots, T), 1)
    lane = k_id[0:1]
    held = jnp.sum(jnp.where(key_c == k_id, 1, 0), 0, keepdims=True)
    pairs = (held + 1) >> 1

    def list_of(k):
        return jnp.where(k < 64, 0, jnp.maximum((k >> 4) - 4, 1))

    start = jnp.zeros((1, 1), jnp.int32)
    starts, counts, base = (jnp.zeros((1, T), jnp.int32) for _ in range(3))
    for number in range(4):
        total = jnp.sum(jnp.where(list_of(lane) == number, pairs, 0), 1, keepdims=True)
        groups = (total + UNROLL - 1) // UNROLL
        starts = jnp.where(lane == number, start, starts)
        counts = jnp.where(lane == number, groups, counts)
        base = jnp.where(list_of(lane) == number, start * UNROLL, base)
        start = start + groups
    ahead = (k_id < key_c) & (list_of(k_id) == list_of(key_c))
    step = jnp.sum(jnp.where(ahead, pairs, 0) + jnp.where(k_id == key_c, base, 0), 1, keepdims=True) + (rank >> 1)
    step = jnp.where(key_c < T, step, -1)
    first = jnp.where((rank & 1) == 0, step, -1)
    second = jnp.where((rank & 1) == 1, step, -1)
    p_id = lax.broadcasted_iota(jnp.int32, (slots, N_STEP), 1)
    none = ZERO_ROW << 9
    none_high = 64 << 15
    out_ref[0:1, :] = (
        jnp.sum(jnp.where(first == p_id, word_c + high_c - none - none_high, 0), 0, keepdims=True) + none + none_high
    )
    out_ref[1:2, :] = jnp.sum(jnp.where(second == p_id, word_c - none, 0), 0, keepdims=True) + none
    out_ref[2:8, :] = jnp.zeros((6, N_STEP), jnp.int32)
    out_ref[2:3, 0:T] = starts
    out_ref[3:4, 0:T] = counts


def stage(count_ref, tiles_ref, out_ref, sems):
    chunk = tiles_ref.shape[0] // 8

    def copy(i):
        part = pl.ds(i * chunk, chunk)
        return pltpu.make_async_copy(tiles_ref.at[part], out_ref.at[part], sems.at[i])

    used = (count_ref[0] + chunk - 1) // chunk
    for i in range(8):
        pl.when(i < used)(lambda i=i: copy(i).start())
    for i in range(8):
        pl.when(i < used)(lambda i=i: copy(i).wait())


def products(number, steps_ref, h_ref, tiles_ref, acc_ref):
    lowest = LOWEST[number]
    spare = acc_ref.shape[0] - 1

    def some(g, carry):
        results = []
        for u in range(UNROLL):
            s = g * UNROLL + u
            a, b = steps_ref[0, s], steps_ref[1, s]
            left = jnp.concatenate([h_ref[(a >> 9) & 63], h_ref[b >> 9]], 1)
            right = jnp.concatenate([tiles_ref[a & 511], tiles_ref[b & 511]], 0)
            column = jnp.minimum((a >> 15) - lowest, spare)
            results.append((column, jnp.dot(left, right, preferred_element_type=f32)))
        for column, result in results:
            acc_ref[column] += result
        return carry

    first = steps_ref[2, number]
    lax.fori_loop(first, first + steps_ref[3, number], some, 0)


def early(steps_ref, a0, b0, tiles_ref, acc_ref, h_ref):
    h_ref[0:4], h_ref[16:24] = a0[...], b0[0:8]
    h_ref[ZERO_ROW] = jnp.zeros((256, T), bf16)

    def clear(k, carry):
        acc_ref[k] = jnp.zeros((256, T), f32)
        return carry

    lax.fori_loop(0, 65, clear, 0)
    products(0, steps_ref, h_ref, tiles_ref, acc_ref)


def late(number, steps_ref, h_ref, tiles_ref, so_far_ref, outs, acc_ref):
    base, columns = LOWEST[number], 16 * len(outs)

    def take(k, carry):
        acc_ref[k] = so_far_ref[base + k]
        return carry

    lax.fori_loop(0, columns, take, 0)
    acc_ref[columns] = jnp.zeros((256, T), f32)
    products(number, steps_ref, h_ref, tiles_ref, acc_ref)
    for i, ref in enumerate(outs):

        def give(k, carry, i=i, ref=ref):
            ref[k] = acc_ref[16 * i + k].astype(ref.dtype)
            return carry

        lax.fori_loop(0, 16, give, 0)


def late_partner(steps_ref, a0, a3, a1, a2, b0, b1, tiles_ref, so_far_ref, p_ref, q_ref, h_ref, acc_ref):
    h_ref[0:4], h_ref[4:8], h_ref[8:12], h_ref[12:16] = a0[...], a1[...], a2[...], a3[...]
    h_ref[16:24], h_ref[24:32] = b0[0:8], b1[0:8]
    h_ref[ZERO_ROW] = jnp.zeros((256, T), bf16)
    p_ref[16] = both_parts(whole(b0[8]) + whole(b1[8]))
    late(1, steps_ref, h_ref, tiles_ref, so_far_ref, (p_ref, q_ref), acc_ref)


def late_own(number, steps_ref, h_ref, tiles_ref, so_far_ref, out_ref, acc_ref):
    late(number, steps_ref, h_ref, tiles_ref, so_far_ref, (out_ref,), acc_ref)


def split_p(acc_ref, got_ref, sent_ref, keep, z1, z2, z3):
    for k in range(4):
        keep[k] = acc_ref[k] + got_ref[k].astype(f32)
        for dz, ref in ((1, z1), (2, z2), (3, z3)):
            ref[k * 256 : (k + 1) * 256] = (acc_ref[4 * dz + k] + got_ref[4 * dz + k].astype(f32)).astype(bf16)
    total = (whole(sent_ref[16]) + whole(got_ref[16])).astype(bf16)
    for ref in (z1, z2, z3):
        ref[1024 : 1024 + T] = total


def gather_p(keep_ref, g1, g2, g3, sent_ref, keep, y, w):
    for k in range(4):
        rows = slice(k * 256, (k + 1) * 256)
        total = keep_ref[k] + g1[rows].astype(f32) + g2[rows].astype(f32) + g3[rows].astype(f32)
        if k < 2:
            keep[k] = total
        else:
            y[k - 2] = total.astype(bf16)
    own, left, across, right = (ref[1024 : 1024 + T].astype(f32) for ref in (sent_ref, g1, g2, g3))
    w[...] = (own + across) + (left + right)


def split_q(acc_ref, got_ref, keep, y):
    for dz in range(4):
        for u in range(2):
            k = 4 * dz + u
            keep[2 * dz + u] = acc_ref[k] + got_ref[k].astype(f32)
            y[2 * dz + u] = (acc_ref[k + 2] + got_ref[k + 2].astype(f32)).astype(bf16)


def gather_q(keep_ref, got_ref, keep, z1, z2, z3):
    for u in range(2):
        keep[u] = keep_ref[u] + got_ref[u].astype(f32)
        for dz, ref in ((1, z1), (2, z2), (3, z3)):
            ref[u] = (keep_ref[2 * dz + u] + got_ref[2 * dz + u].astype(f32)).astype(bf16)


def finish(p_keep, p_got, q_keep, g1, g2, g3, mask_ref, w, w_got, out_ref, weight_ref):
    odd = (lax.axis_index("col") >> 1) & 1
    for which, ref in ((odd, w), (1 - odd, w_got)):
        for i in range(2):
            rows = pl.ds(pl.multiple_of(i * T + which * 64, 64), 64)
            weight_ref[rows, 0:T] = ref[i, 0:64]
            weight_ref[rows, T : 2 * T] = ref[i, 64:T]
    for t in range(4):
        keep, *parts = (p_keep, p_got) if t < 2 else (q_keep, g1, g2, g3)
        total = keep[t & 1]
        for got in parts:
            total += got[t & 1].astype(f32)
        rows = slice(t * T, (t + 1) * T)
        out_ref[rows] = jnp.where(mask_ref[rows] == 1, total.T, 0.0).astype(bf16)


def shards(out_grad, out_bits, agg_saved, weight, tiles, tile_coords, tile_count, in_bits):
    def over_x(v, s):
        return lax.ppermute(v, "col", [(c, (((c >> 1) + s) & 3) * 2 + (c & 1)) for c in range(8)])

    def over_y_hi(v):
        return lax.ppermute(v, "col", [(c, c ^ 1) for c in range(8)])

    def over_z(v, s):
        return lax.ppermute(v, "row", [(r, (r & 9) | ((((r >> 1) + s) & 3) << 1)) for r in range(16)])

    def swap_x(v, bit):
        return lax.ppermute(v, "col", [(c, c ^ (2 << bit)) for c in range(8)])

    def over_y_lo(v):
        return lax.ppermute(v, "row", [(r, r ^ 8) for r in range(16)])

    def over_core(v):
        return lax.ppermute(v, "row", [(r, r ^ 1) for r in range(16)])

    half, quad, square, message = (2, 256, T), (4, 256, T), (T, T), (512 + T, T)
    ha, hb, m1, m2, m3, w = call(
        prep,
        [(half, bf16)] * 2 + [(message, bf16)] * 3 + [(square, f32)],
        [ANY] * 4,
        "prep",
        limit=PREP_LIMIT,
        scratch=[
            pltpu.VMEM((512, 256), bf16),
            pltpu.VMEM((16, 512), jnp.int32),
            pltpu.VMEM((512, 256), bf16),
            pltpu.VMEM((256, 256), bf16),
            pltpu.VMEM((256, 256), f32),
            pltpu.SemaphoreType.DMA((4,)),
        ],
        flops=2 * 10**8,
    )(out_grad, out_bits.T, agg_saved, weight)

    ha_y = over_y_hi(ha)
    m3, m2, m1 = over_x(m1, 1), over_x(m2, 2), over_x(m3, 3)
    count, own_tiles, ha = tie(tile_count.reshape(1), tiles[0, 0], ha)
    (own_tiles,) = call(
        stage,
        [(own_tiles.shape, bf16)],
        [SMEM, ANY],
        "stage",
        limit=STAGE_LIMIT,
        scratch=[pltpu.SemaphoreType.DMA((8,))],
        flops=10**9,
    )(count, own_tiles)
    ha, ha_y, hb, m1, m2, m3, own_tiles, coords, count = tie(
        ha, ha_y, hb, m1, m2, m3, own_tiles, tile_coords[0, 0].T, count
    )

    a0, b0 = call(pack, [(quad, bf16), ((9, 256, T), bf16)], [VMEM] * 7, "pack", flops=10**6)(
        ha, ha_y, hb, m1, m2, m3, w
    )
    b1 = over_y_hi(b0)
    a3, a1, a2 = over_x(a0, 1), over_x(a0, -1), over_x(a0, 2)
    (steps,) = call(order_slots, [((8, N_STEP), jnp.int32)], [SMEM, VMEM], "order_slots", flops=10**7)(count, coords)
    (acc,) = call(
        early,
        [((65, 256, T), f32)],
        [SMEM] + [VMEM] * 3,
        "early",
        limit=LIMIT,
        scratch=[pltpu.VMEM((33, 256, T), bf16)],
        flops=4 * 10**9,
    )(steps, a0, b0, own_tiles)
    a0, a1, a2, a3, b0, b1, acc = tie(a0, a1, a2, a3, b0, b1, acc)

    sixteen = (16, 256, T)
    z_p, eight = (1024 + T, T), (8, 256, T)

    def own_columns(number):
        return call(
            functools.partial(late_own, number),
            [(sixteen, f32)],
            [SMEM] + [VMEM] * 3,
            "late_" + str(number),
            limit=LIMIT,
            scratch=[pltpu.VMEM((17, 256, T), f32)],
            flops=2 * 10**9,
        )(steps, hidden, own_tiles, acc)[0]

    def around_z(z1, z2, z3):
        return over_z(z1, 1), over_z(z2, 2), over_z(z3, 3)

    p_sent, q_sent, hidden = call(
        late_partner,
        [((17, 256, T), bf16), (sixteen, bf16), ((33, 256, T), bf16)],
        [SMEM] + [VMEM] * 8,
        "late_1",
        limit=LIMIT,
        scratch=[pltpu.VMEM((33, 256, T), f32)],
        flops=4 * 10**9,
    )(steps, a0, a3, a1, a2, b0, b1, own_tiles, acc)
    p_got, q_got = over_core(p_sent), over_core(q_sent)
    own = own_columns(2)
    p_keep, *p_z = call(split_p, [(quad, f32)] + [(z_p, bf16)] * 3, [VMEM] * 3, "split_p", flops=10**6)(
        own, p_got, p_sent
    )
    p_all = around_z(*p_z)
    p_keep, hidden, q_got = tie(p_keep, hidden, q_got)
    own = own_columns(3)
    q_keep, q_y = call(split_q, [(eight, f32), (eight, bf16)], [VMEM] * 2, "split_q", flops=10**6)(own, q_got)
    q_got = over_y_lo(q_y)
    p_keep, q_keep, words = tie(p_keep, q_keep, in_bits.T)
    (mask,) = call(in_mask, [((512, 256), bf16)], [VMEM], "in_mask", flops=10**7)(words)
    p_keep, p_y, w = call(
        gather_p, [(half, f32), (half, bf16), (square, f32)], [VMEM] * 5, "gather_p", flops=10**10, touched=2**25
    )(p_keep, *p_all, p_z[0])
    p_got, w_got = over_y_lo(p_y), over_y_lo(w)
    q_keep, p_keep, mask = tie(q_keep, p_keep, mask)
    q_keep, *q_z = call(gather_q, [(half, f32)] + [(half, bf16)] * 3, [VMEM] * 2, "gather_q", flops=10**6)(
        q_keep, q_got
    )
    q_keep, w, w_got = tie(q_keep, w, w_got)
    q_all = around_z(*q_z)
    (w,) = call(add_two, [(square, f32)], [VMEM] * 2, "add_two", limit=2)(w, w_got)
    w_got = swap_x(w, 1)
    q_all = list(q_all)
    w, w_got, q_all[0], q_all[1] = tie(w, w_got, q_all[0], q_all[1])
    (w,) = call(pair_up, [((2, T, T), f32)], [VMEM] * 2, "pair_up", limit=2)(w, w_got)
    w_got = swap_x(w, 0)
    prev_grad, weight_grad = call(
        finish, [((512, 256), bf16), ((256, 256), f32)], [VMEM] * 9, "finish", flops=10**6
    )(p_keep, p_got, q_keep, *q_all, mask, w, w_got)
    return weight_grad, prev_grad


def solution(mesh):
    nodes = P(("row", "col"), None)
    return jax.shard_map(
        shards,
        mesh=mesh,
        in_specs=(nodes, nodes, nodes, P(), P("row", "col"), P("row", "col"), P("row", "col"), nodes),
        out_specs=(P(), nodes),
        check_vma=False,
    )
```
